256 devices in a mesh: mesh: 256 (over x, y, z, core).
Axes of the slice: x: 4, y: 4, z: 8, core: 2. Of those that a mesh axis runs over, the one named last changes fastest.
Arguments:
- state: float32 [256, 65536], P(None, 'mesh'), may hold values from -6 to 6
- target: float32 [256, 65536], P(None, 'mesh'), may hold values from -15 to 15
- weight_in: float32 [256, 256], replicated, may hold values from -0.375 to 0.375
- bias_in: float32 [256], replicated, may hold values from -3 to 3
- weight_out: float32 [256, 256], replicated, may hold values from -0.375 to 0.375
- bias_out: float32 [256], replicated, may hold values from -4 to 4
- nbr_face: int32 [6, 65536], P(None, 'mesh'), may hold values from 0 to 2047, as said below
- send_faces: int32 [2, 65536], P(None, 'mesh'), may hold values from 0 to 511, as said below
Outputs:
- final_state: float32 [256, 65536], P(None, 'mesh')
- loss: float32 [], replicated
- step_weight_in: float32 [256, 256], replicated
- step_bias_in: float32 [256], replicated
- step_weight_out: float32 [256, 256], replicated
- step_bias_out: float32 [256], replicated
The draws below stay inside these ranges and needn't reach their ends.
Inputs may be any that keep to these rules, and one draw needn't show every extreme that they name: `nbr_face`: A face of the device's own elements refers to a column of the opposite face (f xor 1) of a neighbouring element, with the same order of nodes; faces on the first dimension at a device's lower or upper end refer to the received columns. Every received column is referred to by exactly one face. `send_faces`: entries of row 0 are face-0 columns of the device's own elements (below 256), entries of row 1 face-1 columns (256 to 511), none twice in a block; entry t of row 1 (row 0) is the face seen across by the face that refers to received slot t on the device above (below).
All inputs are finite; a program needn't handle non-finite values.
Results may differ from the reference program's by a relative error of at most 0.0001.
Values sent between devices are 32-bit elements; how exact they have to be, the bound alone decides.
No kernel may reach another device: no remote copies, remote signals or barrier semaphores. Data moves between devices by JAX's collectives and lax.ppermute only.
A program may use at most 64 MiB of HBM per device.

```python
import jax
import jax.numpy as jnp
import numpy as np
from jax import lax

STATE = 256
HID = 256
SX = 1
GY = 16
GZ = 16
TSTEPS = 2
E_DEV = 256
HALO = 256
ELEMS = 65536
N_MESH = 256


def device_order(subkey):
    owned = E_DEV
    cross = GY * GZ
    key_perm, key_low, key_shift = jax.random.split(subkey, 3)
    order = jax.random.permutation(key_perm, owned).astype(jnp.int32)
    low_cell = jax.random.randint(key_low, (), 0, cross).astype(jnp.int32)
    high_cell = ((low_cell + 1 + jax.random.randint(key_shift, (), 0, max(cross - 1, 1))) % cross).astype(jnp.int32)
    high_elem = ((SX - 1) * cross + high_cell).astype(jnp.int32)
    low_elem = low_cell
    positions = jnp.arange(owned, dtype=jnp.int32)
    high_pos = jnp.sum(jnp.where(order == high_elem, positions, 0)).astype(jnp.int32)
    last_value = order[owned - 1]
    order = order.at[high_pos].set(last_value).at[owned - 1].set(high_elem)
    low_pos = jnp.sum(jnp.where(order == low_elem, positions, 0)).astype(jnp.int32)
    first_value = order[0]
    order = order.at[low_pos].set(first_value).at[0].set(low_elem)
    return order


def build_mesh(key):
    devices = N_MESH
    owned = E_DEV
    slots = HALO
    cross = GY * GZ
    key_order, key_upward, key_downward = jax.random.split(key, 3)
    order = jax.vmap(device_order)(jax.random.split(key_order, devices)).astype(jnp.int32)
    place = jnp.argsort(order, axis=1).astype(jnp.int32)
    upward = jax.vmap(lambda subkey: jax.random.permutation(subkey, slots))(jax.random.split(key_upward, devices)).astype(jnp.int32)
    downward = jax.vmap(lambda subkey: jax.random.permutation(subkey, slots))(jax.random.split(key_downward, devices)).astype(jnp.int32)
    upward_slot = jnp.argsort(upward, axis=1).astype(jnp.int32)
    downward_slot_next = jnp.roll(jnp.argsort(downward, axis=1).astype(jnp.int32), -1, axis=0)
    upward_next = jnp.roll(upward, -1, axis=0)
    geometric = jnp.arange(owned, dtype=jnp.int32)
    layer = geometric // cross
    cell = geometric % cross
    row_y = cell // GZ
    row_z = cell % GZ
    neighbours = [jnp.clip(geometric - cross, 0, owned - 1), jnp.clip(geometric + cross, 0, owned - 1), layer * cross + (row_y + GY - 1) % GY * GZ + row_z, layer * cross + (row_y + 1) % GY * GZ + row_z, layer * cross + row_y * GZ + (row_z + GZ - 1) % GZ, layer * cross + row_y * GZ + (row_z + 1) % GZ]
    faces = []
    for face in range(6):
        local_ids = (face ^ 1) * owned + jnp.take_along_axis(place, jnp.broadcast_to(neighbours[face][None, :], (devices, owned)), axis=1)
        if face == 0:
            remote_ids = 6 * owned + jnp.take_along_axis(upward_slot, jnp.broadcast_to(cell[None, :], (devices, owned)), axis=1)
            local_ids = jnp.where((layer == 0)[None, :], remote_ids, local_ids)
        if face == 1:
            remote_ids = 6 * owned + slots + jnp.take_along_axis(downward_slot_next, jnp.broadcast_to(cell[None, :], (devices, owned)), axis=1)
            local_ids = jnp.where((layer == SX - 1)[None, :], remote_ids, local_ids)
        faces.append(local_ids)
    geometric_table = jnp.stack(faces, axis=1)
    stored = jnp.take_along_axis(geometric_table, jnp.broadcast_to(order[:, None, :], (devices, 6, owned)), axis=2)
    nbr_table = stored.transpose(1, 0, 2).reshape(6, devices * owned).astype(jnp.int32)
    to_lower = jnp.take_along_axis(place, downward, axis=1)
    to_upper = owned + jnp.take_along_axis(place, (SX - 1) * cross + upward_next, axis=1)
    send_table = jnp.stack([to_lower, to_upper], axis=1).transpose(1, 0, 2).reshape(2, devices * slots).astype(jnp.int32)
    return (nbr_table, send_table)


def draw_nbr_face(key, part):
    return build_mesh(key)[0]


def draw_send_faces(key, part):
    return build_mesh(key)[1]


def draw_target(key, part):
    key = jax.random.fold_in(key, 11)
    column_scale = 1.0 + 2.0 * jnp.arange(ELEMS, dtype=jnp.float32) / ELEMS
    values = jnp.clip(jax.random.normal(key, (STATE, ELEMS), jnp.float32), -5.0, 5.0)
    return (values * column_scale[None, :]).astype(jnp.float32)


def levels(stream_key, extent, pieces, smallest, high):
    gain = 1.0
    for dim, parts in pieces:
        heights = jax.random.uniform(jax.random.fold_in(jax.random.fold_in(stream_key, 6), dim), (parts,), jnp.float32, smallest / len(pieces), high / len(pieces))
        gain = gain * jnp.repeat(jnp.exp(heights), extent[dim] // parts).reshape((-1,) + (1,) * (len(extent) - 1 - dim))
    return gain


def scatter_about(stream_key, shape, width, limit, shards=(), kind=jnp.bfloat16):
    level = levels(stream_key, shape, shards, -0.22, 0.18) if shards else 1.0
    entries = jax.random.normal(stream_key, shape, jnp.float32) * width * level
    return jnp.minimum(jnp.maximum(entries, -limit), limit).astype(kind)


def setup_inputs(seed: int = 0) -> dict:
    key_of = jax.random.split(jax.random.key(seed), 9)
    return {
        "state": scatter_about(key_of[0], (STATE, ELEMS), 1.0, 6.0, ((1, 256),), jnp.float32),
        "target": draw_target(jax.random.fold_in(key_of[8], 71), 0),
        "weight_in": scatter_about(key_of[2], (HID, STATE), STATE ** -0.5, 0.375, (), jnp.float32),
        "bias_in": scatter_about(key_of[3], (HID,), 0.5, 3.0, (), jnp.float32),
        "weight_out": scatter_about(key_of[4], (STATE, HID), HID ** -0.5, 0.375, (), jnp.float32),
        "bias_out": scatter_about(key_of[5], (STATE,), 1.0, 4.0, (), jnp.float32),
        "nbr_face": draw_nbr_face(jax.random.fold_in(key_of[8], 71), 0),
        "send_faces": draw_send_faces(jax.random.fold_in(key_of[8], 71), 0),
    }


HIGH = lax.Precision.HIGHEST
TIME_STEP = 0.05
LIFT_FACTOR = 6.0
TINY = 1e-20

def derivative_tables():
    gll_points = np.array([-1.0, -1.0 / np.sqrt(5.0), 1.0 / np.sqrt(5.0), 1.0])
    bary_weights = np.array([1.0 / np.prod([gll_points[first] - gll_points[second] for second in range(4) if second != first]) for first in range(4)])
    derivative = np.zeros((4, 4))
    for first in range(4):
        for second in range(4):
            if first != second:
                derivative[first, second] = bary_weights[second] / bary_weights[first] / (gll_points[first] - gll_points[second])
        derivative[first, first] = -np.sum(derivative[first])
    identity_four = np.eye(4)
    along_first = np.kron(np.kron(derivative, identity_four), identity_four)
    along_second = np.kron(np.kron(identity_four, derivative), identity_four)
    along_third = np.kron(identity_four, np.kron(identity_four, derivative))
    return jnp.asarray(np.stack([along_first, along_second, along_third]), dtype=jnp.float32)

def matmul(left, right):
    return jnp.dot(left, right, precision=HIGH, preferred_element_type=jnp.float32)

def face_part(block, face):
    layer = 0 if face % 2 == 0 else 3
    direction = face // 2
    if direction == 0:
        piece = block[layer]
    elif direction == 1:
        piece = block[:, layer]
    else:
        piece = block[:, :, layer]
    return piece.reshape(16, block.shape[-1])

def face_index(field, face):
    layer = 0 if face % 2 == 0 else 3
    direction = face // 2
    if direction == 0:
        return (field, layer)
    if direction == 1:
        return (field, slice(None), layer)
    return (field, slice(None), slice(None), layer)

def traces(state_now):
    cells = state_now.shape[1]
    blocks = state_now.reshape(4, 4, 4, 4, cells)
    columns = []
    for face in range(6):
        pressure = face_part(blocks[0], face)
        normal_speed = face_part(blocks[1 + face // 2], face)
        columns.append(jnp.concatenate([pressure, normal_speed], axis=0))
    return jnp.concatenate(columns, axis=1)

def local_rhs(state_now, outside, weight_in, bias_in, weight_out, bias_out):
    cells = state_now.shape[1]
    tables = derivative_tables()
    inner = traces(state_now)
    pressure = state_now[0:64]
    volume_p = -(matmul(tables[0], state_now[64:128]) + matmul(tables[1], state_now[128:192]) + matmul(tables[2], state_now[192:256]))
    volume_v = [-matmul(tables[axis_num], pressure) for axis_num in range(3)]
    result = jnp.concatenate([volume_p] + volume_v, axis=0).reshape(4, 4, 4, 4, cells)
    for face in range(6):
        sign = -1.0 if face % 2 == 0 else 1.0
        inner_face = inner[:, face * cells:(face + 1) * cells]
        outer_face = outside[:, face * cells:(face + 1) * cells]
        jump_p = inner_face[:16] - outer_face[:16]
        jump_v = sign * (inner_face[16:] - outer_face[16:])
        flux = 0.5 * jump_v - 0.5 * jump_p
        result = result.at[face_index(0, face)].add((LIFT_FACTOR * flux).reshape(4, 4, cells))
        result = result.at[face_index(1 + face // 2, face)].add((-LIFT_FACTOR * sign * flux).reshape(4, 4, cells))
    hidden = jnp.tanh(matmul(weight_in, state_now) + bias_in[:, None])
    closure = matmul(weight_out, hidden) + bias_out[:, None]
    return result.reshape(state_now.shape[0], cells) + closure

def exterior_global(inner, nbr_face, send_faces):
    devices = N_MESH
    owned = E_DEV
    slots = HALO
    rows = inner.shape[0]
    per_device = inner.reshape(rows, 6, devices, owned).transpose(2, 0, 1, 3).reshape(devices, rows, 6 * owned)
    sends = send_faces.reshape(2, devices, slots).transpose(1, 0, 2).reshape(devices, 2 * slots)
    outgoing = jnp.take_along_axis(per_device, sends[:, None, :], axis=2)
    from_below = jnp.roll(outgoing[:, :, slots:], 1, axis=0)
    from_above = jnp.roll(outgoing[:, :, :slots], -1, axis=0)
    table = jnp.concatenate([per_device, from_below, from_above], axis=2)
    lookup = nbr_face.reshape(6, devices, owned).transpose(1, 0, 2).reshape(devices, 6 * owned)
    picked = jnp.take_along_axis(table, lookup[:, None, :], axis=2)
    return picked.reshape(devices, rows, 6, owned).transpose(1, 2, 0, 3).reshape(rows, 6 * devices * owned)

def reference(state, target, weight_in, bias_in, weight_out, bias_out, nbr_face, send_faces):

    def rhs_full(state_now, params):
        outside = exterior_global(traces(state_now), nbr_face, send_faces)
        return local_rhs(state_now, outside, *params)
    rhs_saved = jax.checkpoint(rhs_full)

    def evolve(params):
        current = state
        for step_index in range(TSTEPS):
            first_section = current + TIME_STEP * rhs_saved(current, params)
            current = 0.5 * current + 0.5 * (first_section + TIME_STEP * rhs_saved(first_section, params))
        return current
    params = (weight_in, bias_in, weight_out, bias_out)
    final_state, pullback = jax.vjp(evolve, params)
    count = float(final_state.shape[0] * final_state.shape[1])
    mismatch = final_state - target
    loss = 0.5 * jnp.sum(mismatch * mismatch) / count
    gradients = pullback(mismatch / count)[0]
    param_count = float(sum((grad_item.size for grad_item in gradients)))
    total_sq = sum((jnp.sum(grad_item * grad_item) for grad_item in gradients))
    scale = lax.rsqrt(total_sq / param_count + TINY)
    return (final_state, loss, gradients[0] * scale, gradients[1] * scale, gradients[2] * scale, gradients[3] * scale)
```

```python
import functools

import jax
import jax.numpy as jnp
import ml_dtypes
import numpy as np
from jax import lax
from jax.experimental import pallas as pl
from jax.experimental.pallas import tpu as pltpu
from jax.sharding import Mesh, PartitionSpec as P

AXES = ("x", "y", "z", "core")
PLANE = ("x", "y")
SIZES = (4, 4, 8, 2)
DEVICES = 256
WIDTH = 256
COUNT = 16777216.0
PARAMS = 131584.0
TIME_STEP = 0.05
HALF_STEP = 0.025
TINY = 1e-20
F32 = jnp.float32
BF16 = jnp.bfloat16


def face_rows(face):
    layer = 0 if face % 2 == 0 else 3
    grid = np.arange(64).reshape(4, 4, 4)
    return np.take(grid, layer, axis=face // 2).reshape(16)


def operators():
    points = np.array([-1.0, -1.0 / np.sqrt(5.0), 1.0 / np.sqrt(5.0), 1.0])
    bary = np.array(
        [1.0 / np.prod([points[m] - points[n] for n in range(4) if n != m]) for m in range(4)]
    )
    deriv = np.zeros((4, 4))
    for m in range(4):
        for n in range(4):
            if m != n:
                deriv[m, n] = bary[n] / bary[m] / (points[m] - points[n])
        deriv[m, m] = -np.sum(deriv[m])
    eye = np.eye(4)
    tables = [
        np.kron(np.kron(deriv, eye), eye),
        np.kron(np.kron(eye, deriv), eye),
        np.kron(eye, np.kron(eye, deriv)),
    ]
    inner = np.zeros((256, 256))
    for a in range(3):
        inner[0:64, 64 * (a + 1) : 64 * (a + 2)] -= tables[a]
        inner[64 * (a + 1) : 64 * (a + 2), 0:64] -= tables[a]
    for face in range(6):
        sign = 2.0 * (face % 2) - 1.0
        for row in face_rows(face):
            speed = 64 * (face // 2 + 1) + row
            inner[row, row] -= 3.0
            inner[row, speed] += 3.0 * sign
            inner[speed, speed] -= 3.0
            inner[speed, row] += 3.0 * sign
    leave = np.zeros((64, 256))
    lift = np.zeros((256, 64))
    for face in range(2, 6):
        sign = 2.0 * (face % 2) - 1.0
        base = 16 * (face - 2)
        for n, row in enumerate(face_rows(face ^ 1)):
            leave[base + n, row] = 3.0
            leave[base + n, 64 * (face // 2 + 1) + row] = -3.0 * sign
        for n, row in enumerate(face_rows(face)):
            lift[row, base + n] = 1.0
            lift[64 * (face // 2 + 1) + row, base + n] = -sign
    return inner, leave, lift


def halves(values):
    high = values.astype(ml_dtypes.bfloat16)
    low = (values - high.astype(np.float64)).astype(ml_dtypes.bfloat16)
    return np.stack([high, low])


def split(values):
    high = values.astype(BF16)
    return high, (values - high.astype(F32)).astype(BF16)


def mm(left, right):
    return jnp.dot(left, right, preferred_element_type=F32)


def mm_nt(left, right):
    return lax.dot_general(left, right, (((1,), (1,)), ((), ())), preferred_element_type=F32)


def mm3(left, right, dot=mm):
    return dot(left[0], right[0]) + (dot(left[0], right[1]) + dot(left[1], right[0]))


def pair(ref):
    return ref[0], ref[1]


def call(body, outs, *args, flops=2e8, name):
    specs = [
        pl.BlockSpec(memory_space=pltpu.SMEM)
        if a.shape == (1,)
        else pl.BlockSpec(memory_space=pltpu.VMEM)
        for a in args
    ]
    return list(pl.pallas_call(
        body,
        out_shape=[jax.ShapeDtypeStruct(s, t) for s, t in outs],
        in_specs=specs,
        out_specs=[pl.BlockSpec(memory_space=pltpu.VMEM)] * len(outs),
        cost_estimate=pl.CostEstimate(flops=int(flops), bytes_accessed=2000000, transcendentals=0),
        compiler_params=pltpu.CompilerParams(vmem_limit_bytes=24 * 1024 * 1024),
        name=name,
    )(*args))


SQUARE = ((256, 256), F32)
PAIR = ((2, 256, 256), BF16)
EDGE = ((16, 256), F32)
EXTRA = ((8, 256), F32)


def edges(values):
    return values[0:16], values[48:64], values[64:80], values[112:128]


def leaving(values):
    p_low, p_high, u_low, u_high = edges(values)
    return 3.0 * (p_high + u_high), 3.0 * (p_low - u_low)


def put(parity, upward, downward, in_chip_ref, cross_ref):
    even = parity == 0
    in_chip_ref[0:16] = jnp.where(even, upward, downward)
    cross_ref[0:16] = jnp.where(even, downward, upward)


def take(parity, in_chip, cross):
    even = parity == 0
    return jnp.where(even, cross, in_chip), jnp.where(even, in_chip, cross)


def pick(values, table, dot=mm):
    both = dot(jnp.concatenate(split(values), axis=0), table)
    return both[0:16] + both[16:32]


def add_edges(values_ref, first, second, third, fourth):
    values_ref[0:16] += first
    values_ref[48:64] += second
    values_ref[64:80] += third
    values_ref[112:128] += fourth


def first_kernel(parity_ref, state_ref, send_ref, in_chip_ref, cross_ref):
    upward, downward = leaving(state_ref)
    parity = parity_ref[0]
    put(parity, upward, downward, in_chip_ref, cross_ref)
    down_index = send_ref[0:1].astype(F32)
    up_index = (send_ref[1:2] - 256).astype(F32)
    even = parity == 0
    in_chip_ref[16:24] = jnp.broadcast_to(jnp.where(even, up_index, down_index), (8, 256))
    cross_ref[16:24] = jnp.broadcast_to(jnp.where(even, down_index, up_index), (8, 256))


def setup_kernel(w_in_ref, w_out_ref, nbr_ref, in_ref, out_ref, in_t_ref, out_t_ref, near_ref, far_ref):
    for source, ref, ref_t in ((w_in_ref, in_ref, in_t_ref), (w_out_ref, out_ref, out_t_ref)):
        values = source[...]
        ref[0], ref[1] = split(values)
        ref_t[0], ref_t[1] = split(values.T)
    rows = lax.broadcasted_iota(jnp.int32, (256, 256), 0)
    for face in range(6):
        column = nbr_ref[face : face + 1]
        if face < 2:
            far_ref[face] = (rows + (1536 + 256 * face) == column).astype(F32).astype(BF16)
        else:
            near_ref[face - 2] = (rows + 256 * (face ^ 1) == column).astype(F32).astype(BF16)


def local_rates(values, w_in, b_in, w_out, b_out, inner, leave, lift, near, hidden_ref):
    parts = split(values)
    hidden = jnp.tanh(mm3(w_in, parts) + b_in)
    hidden_ref[...] = hidden
    rates = mm3(inner, parts) + b_out
    out = mm(leave, parts[0]) + mm(leave, parts[1])
    high, low = split(out)
    arrived = []
    for n in range(4):
        both = jnp.concatenate([high[16 * n : 16 * n + 16], low[16 * n : 16 * n + 16]], axis=0)
        arrived.append(mm(both, near[n]).astype(BF16))
    for part in range(2):
        rates += mm(lift, jnp.concatenate([a[16 * part : 16 * part + 16] for a in arrived], axis=0))
    return rates + mm3(w_out, split(hidden))


def forward_kernel(stage, *refs):
    refs = list(refs)
    parity = refs.pop(0)[0]
    base_ref = refs.pop(0)
    if stage % 2 == 1:
        before_ref = refs.pop(0)
    if stage > 0:
        in_chip, cross = refs.pop(0), refs.pop(0)
        far_ref = refs.pop(0)
    w_in, b_in, w_out, b_out, inner, leave, lift, near = refs[:8]
    refs = refs[8:]
    if stage > 0:
        now_ref = refs.pop(0)
    if stage == 1:
        link_ref = refs.pop(0)
    next_ref, hidden_ref = refs[:2]
    refs = refs[2:]
    if stage == 0:
        values = base_ref[...]
    else:
        below, above = take(parity, in_chip[...], cross[...])
        if stage == 1:
            rows = lax.broadcasted_iota(jnp.int32, (256, 256), 0).astype(F32)
            for side, received in enumerate((below, above)):
                chosen = (rows == received[16:17]).astype(F32).astype(BF16)
                link_ref[side] = mm(chosen, far_ref[side]).astype(BF16)
            far_ref = link_ref
        weight = TIME_STEP if stage % 2 == 1 else HALF_STEP
        low = weight * pick(below[0:16], far_ref[0])
        high = weight * pick(above[0:16], far_ref[1])
        now_ref[...] = base_ref[...]
        add_edges(now_ref, low, high, low, -high)
        values = now_ref[...]
    rates = local_rates(
        values, pair(w_in), b_in[...], pair(w_out), b_out[...], pair(inner), leave[...], lift[...], near, hidden_ref
    )
    if stage % 2 == 0:
        next_ref[...] = values + TIME_STEP * rates
    else:
        next_ref[...] = 0.5 * (before_ref[...] + values) + HALF_STEP * rates
    if stage < 3:
        upward, downward = leaving(next_ref)
        put(parity, upward, downward, *refs)


def sensitivities(values, link):
    p_low, p_high, u_low, u_high = edges(values)
    return pick(p_high - u_high, link[1], mm_nt), pick(p_low + u_low, link[0], mm_nt)


def turn_kernel(parity_ref, base_ref, in_chip, cross, link, target_ref, final_ref, adjoint_ref, loss_ref, in_chip_out, cross_out):
    parity = parity_ref[0]
    below, above = take(parity, in_chip[...], cross[...])
    low = HALF_STEP * pick(below, link[0])
    high = HALF_STEP * pick(above, link[1])
    final_ref[...] = base_ref[...]
    add_edges(final_ref, low, high, low, -high)
    mismatch = final_ref[...] - target_ref[...]
    adjoint_ref[...] = (HALF_STEP / COUNT) * mismatch
    loss_ref[...] = jnp.broadcast_to(jnp.sum(mismatch * mismatch, axis=0, keepdims=True), (8, 256))
    upward, downward = sensitivities(adjoint_ref, link)
    put(parity, upward, downward, in_chip_out, cross_out)


def backward_kernel(stage, *refs):
    refs = list(refs)
    parity = refs.pop(0)[0]
    base_ref = refs.pop(0)
    if stage < 3:
        in_chip, cross = refs.pop(0), refs.pop(0)
    if stage == 2:
        after_ref = refs.pop(0)
    state_ref, hidden_ref = refs[:2]
    refs = refs[2:]
    if stage > 0:
        w_in_t, w_out_t, inner_t, leave_t, lift_t, near, link = refs[:7]
        refs = refs[7:]
    else:
        w_out_t = refs.pop(0)
    if stage < 3:
        old_in, old_out, old_extra = refs[:3]
        refs = refs[3:]
    if stage == 0:
        loss_ref, keep_ref, send_ref, now_ref = refs
    else:
        grad_in, grad_out, extra = refs[:3]
        refs = refs[3:]
        next_ref = refs.pop(0)
        if stage < 3:
            now_ref = refs.pop(0)
    if stage < 3:
        weight = 3.0 * (HALF_STEP if stage == 1 else TIME_STEP)
        below, above = take(parity, in_chip[...], cross[...])
        low, high = weight * below, weight * above
        now_ref[...] = base_ref[...]
        add_edges(now_ref, low, high, -low, high)
        values = now_ref[...]
    else:
        values = base_ref[...]
    parts = split(values)
    hidden = hidden_ref[...]
    delta = (1.0 - hidden * hidden) * mm3(pair(w_out_t), parts)
    delta_parts = split(delta)
    if stage > 0:
        rates = mm3(pair(inner_t), parts) + mm3(pair(w_in_t), delta_parts)
        high, low = split(mm(lift_t[...], parts[0]) + mm(lift_t[...], parts[1]))
        arrived = []
        for n in range(4):
            both = jnp.concatenate([high[16 * n : 16 * n + 16], low[16 * n : 16 * n + 16]], axis=0)
            arrived.append(mm_nt(both, near[n]))
        high, low = split(jnp.concatenate([a[0:16] + a[16:32] for a in arrived], axis=0))
        rates += mm(leave_t[...], high) + mm(leave_t[...], low)
        if stage == 2:
            next_ref[...] = 0.5 * (after_ref[...] + values) + HALF_STEP * rates
        else:
            next_ref[...] = values + TIME_STEP * rates
        if stage > 1:
            upward, downward = sensitivities(next_ref, link)
            put(parity, upward, downward, *refs)
    ones = jnp.ones((8, 256), BF16)
    first_bias = mm_nt(ones, delta_parts[0]) + mm_nt(ones, delta_parts[1])
    second_bias = mm_nt(ones, parts[0]) + mm_nt(ones, parts[1])
    rows = lax.broadcasted_iota(jnp.int32, (8, 256), 0)
    bias = jnp.where(rows == 0, first_bias, second_bias)
    first = mm3(delta_parts, split(state_ref[...]), mm_nt)
    second = mm3(parts, split(hidden), mm_nt)
    if stage < 3:
        first += old_in[...]
        second += old_out[...]
        bias += old_extra[...]
    if stage > 0:
        grad_in[...] = first
        grad_out[...] = second
        extra[...] = bias
    else:
        even = parity == 0
        keep_ref[0:256] = jnp.where(even, first, second)
        send_ref[0:256] = jnp.where(even, second, first)
        bias = jnp.where(rows == 2, loss_ref[...], bias)
        keep_ref[256:264] = bias
        send_ref[256:264] = bias


def chip_kernel(keep_ref, got_ref, out_ref):
    for n in range(16):
        out_ref[n, 0:16] = keep_ref[16 * n : 16 * n + 16] + got_ref[16 * n : 16 * n + 16]
        out_ref[n, 16:24] = keep_ref[256:264] + got_ref[256:264]


def plane_kernel(parts_ref, out_ref):
    total = jnp.sum(parts_ref[...], axis=0)
    for n in range(8):
        out_ref[n] = total


def line_kernel(parts_ref, out_ref, extra_ref):
    total = jnp.sum(parts_ref[...], axis=0)
    extra_ref[...] = total[16:24]
    for n in range(16):
        out_ref[n] = total[0:16]


def last_kernel(parity_ref, own_ref, other_ref, extra_ref, in_ref, b_in_ref, out_ref, b_out_ref, loss_ref):
    even = parity_ref[0] == 0
    own, other = own_ref[...], other_ref[...]
    first = jnp.where(even, own, other)
    second = jnp.where(even, other, own)
    bias = extra_ref[0:2]
    total = jnp.sum(first * first + second * second, keepdims=True) + jnp.sum(bias * bias, keepdims=True)
    scale = lax.rsqrt(total / PARAMS + TINY)
    in_ref[...] = first * scale
    out_ref[...] = second * scale
    b_in_ref[...] = extra_ref[0:1] * scale
    b_out_ref[...] = extra_ref[1:2] * scale
    loss_ref[...] = jnp.sum(extra_ref[2:3], keepdims=True) * (0.5 / COUNT)


IN_CHIP = [(n, n ^ 1) for n in range(DEVICES)]
CROSS = [(n, (n - 1) % DEVICES if n % 2 == 0 else (n + 1) % DEVICES) for n in range(DEVICES)]


def exchange(in_chip, cross):
    return lax.ppermute(in_chip, AXES, IN_CHIP), lax.ppermute(cross, AXES, CROSS)


def local(state, target, w_in, b_in, w_out, b_out, nbr, send):
    parity = lax.axis_index("core").reshape(1)
    inner, leave, lift = operators()
    one = lambda values: jnp.asarray(values.astype(ml_dtypes.bfloat16))
    two = lambda values: jnp.asarray(halves(values))
    b_in, b_out = b_in.reshape(256, 1), b_out.reshape(256, 1)

    first = call(first_kernel, [((24, 256), F32)] * 2, parity, state, send, name="traces")
    got = [exchange(*first)]
    w_in2, w_out2, w_in_t, w_out_t, near, far = call(
        setup_kernel, [PAIR] * 4 + [((4, 256, 256), BF16), PAIR], w_in, w_out, nbr, name="tables"
    )
    network = (w_in2, b_in, w_out2, b_out, two(inner), one(leave), one(lift), near)
    states, hiddens = [state], []
    base = state
    for stage in range(4):
        args = [parity, base]
        outs = [SQUARE, SQUARE] + ([EDGE, EDGE] if stage < 3 else [])
        if stage % 2 == 1:
            args.append(states[-1])
        if stage > 0:
            args += [*got[stage - 1], far if stage == 1 else link]
            outs = [SQUARE] + ([PAIR] if stage == 1 else []) + outs
        res = call(functools.partial(forward_kernel, stage), outs, *args, *network, name=f"forward{stage}")
        if stage > 0:
            states.append(res.pop(0))
        if stage == 1:
            link = res.pop(0)
        base = res.pop(0)
        hiddens.append(res.pop(0))
        if stage < 3:
            got.append(exchange(*res))
    final, adjoint, loss, *edge = call(
        turn_kernel, [SQUARE, SQUARE, EXTRA, EDGE, EDGE], parity, base, *got[3], link, target, name="turn"
    )
    got = {2: exchange(*edge)}
    back = (w_in_t, w_out_t, two(inner.T), one(leave.T), one(lift.T), near, link)
    grads = []
    base = adjoint
    for stage in (3, 2, 1):
        args = [parity, base]
        outs = [SQUARE, SQUARE, EXTRA, SQUARE]
        if stage < 3:
            args += got[stage]
            outs.append(SQUARE)
        if stage == 2:
            args.append(adjoint)
        if stage > 1:
            outs += [EDGE, EDGE]
        res = call(
            functools.partial(backward_kernel, stage),
            outs, *args, states[stage], hiddens[stage], *back, *grads, name=f"backward{stage}",
        )
        grads = res[:3]
        base = res[3]
        if stage > 1:
            got[stage - 2] = exchange(*res[-2:])
    keep, give, _ = call(
        functools.partial(backward_kernel, 0),
        [((264, 256), F32)] * 2 + [SQUARE],
        parity, base, *got[0], states[0], hiddens[0], w_out_t, *grads, loss, name="backward0",
    )
    swap = [(0, 1), (1, 0)]
    (parts,) = call(chip_kernel, [((16, 24, 256), F32)], keep, lax.ppermute(give, "core", swap), name="chip_sum")
    parts = lax.all_to_all(parts, PLANE, 0, 0, tiled=True)
    (parts,) = call(plane_kernel, [((8, 24, 256), F32)], parts, name="plane_sum")
    parts = lax.all_to_all(parts, "z", 0, 0, tiled=True)
    parts, extra = call(line_kernel, [((16, 16, 256), F32), EXTRA], parts, name="line_sum")
    own = lax.all_to_all(parts, PLANE, 0, 0, tiled=True).reshape(256, 256)
    other = lax.ppermute(own, "core", swap)
    row = ((1, 256), F32)
    step_in, step_b_in, step_out, step_b_out, loss = call(
        last_kernel, [SQUARE, row, SQUARE, row, ((1, 1), F32)], parity, own, other, extra, name="scale"
    )
    return final, loss.reshape(()), step_in, step_b_in.reshape(256), step_out, step_b_out.reshape(256)


def solution(mesh):
    split_mesh = Mesh(mesh.devices.reshape(SIZES), AXES)
    whole = P(None, AXES)
    return jax.shard_map(
        local,
        mesh=split_mesh,
        in_specs=(whole, whole, P(), P(), P(), P(), whole, whole),
        out_specs=(whole, P(), P(), P(), P(), P()),
        check_vma=False,
    )
```

```python
import jax
import jax.numpy as jnp
import ml_dtypes
import numpy as np
from jax import lax
from jax.experimental import pallas as pl
from jax.experimental.pallas import tpu as pltpu
from jax.sharding import Mesh, PartitionSpec as P

AXES = ("x", "y", "z", "core")
PLANE = ("x", "y")
SIZES = (4, 4, 8, 2)
DEVICES = 256
WIDTH = 256
COUNT = 16777216.0
PARAMS = 131584.0
TIME_STEP = 0.05
HALF_STEP = 0.025
TINY = 1e-20
F32 = jnp.float32
BF16 = jnp.bfloat16


def face_rows(face):
    layer = 0 if face % 2 == 0 else 3
    grid = np.arange(64).reshape(4, 4, 4)
    return np.take(grid, layer, axis=face // 2).reshape(16)


def operators():
    points = np.array([-1.0, -1.0 / np.sqrt(5.0), 1.0 / np.sqrt(5.0), 1.0])
    bary = np.array(
        [1.0 / np.prod([points[m] - points[n] for n in range(4) if n != m]) for m in range(4)]
    )
    deriv = np.zeros((4, 4))
    for m in range(4):
        for n in range(4):
            if m != n:
                deriv[m, n] = bary[n] / bary[m] / (points[m] - points[n])
        deriv[m, m] = -np.sum(deriv[m])
    eye = np.eye(4)
    tables = [
        np.kron(np.kron(deriv, eye), eye),
        np.kron(np.kron(eye, deriv), eye),
        np.kron(eye, np.kron(eye, deriv)),
    ]
    inner = np.zeros((256, 256))
    for a in range(3):
        inner[0:64, 64 * (a + 1) : 64 * (a + 2)] -= tables[a]
        inner[64 * (a + 1) : 64 * (a + 2), 0:64] -= tables[a]
    for face in range(6):
        sign = 2.0 * (face % 2) - 1.0
        for row in face_rows(face):
            speed = 64 * (face // 2 + 1) + row
            inner[row, row] -= 3.0
            inner[row, speed] += 3.0 * sign
            inner[speed, speed] -= 3.0
            inner[speed, row] += 3.0 * sign
    leave = np.zeros((64, 256))
    lift = np.zeros((256, 64))
    for face in range(2, 6):
        sign = 2.0 * (face % 2) - 1.0
        base = 16 * (face - 2)
        for n, row in enumerate(face_rows(face ^ 1)):
            leave[base + n, row] = 3.0
            leave[base + n, 64 * (face // 2 + 1) + row] = -3.0 * sign
        for n, row in enumerate(face_rows(face)):
            lift[row, base + n] = 1.0
            lift[64 * (face // 2 + 1) + row, base + n] = -sign
    return inner, leave, lift


def halves(values):
    high = values.astype(ml_dtypes.bfloat16)
    low = (values - high.astype(np.float64)).astype(ml_dtypes.bfloat16)
    return high, low


def split(values):
    high = values.astype(BF16)
    return high, (values - high.astype(F32)).astype(BF16)


def mm(left, right):
    return jnp.dot(left, right, preferred_element_type=F32)


def mm_nt(left, right):
    return lax.dot_general(left, right, (((1,), (1,)), ((), ())), preferred_element_type=F32)


def mm3(left, right, dot=mm):
    return dot(left[0], right[0]) + (dot(left[0], right[1]) + dot(left[1], right[0]))


def pair(ref):
    if len(ref.shape) == 2:
        return ref[0:256], ref[256:512]
    return ref[0], ref[1]


def call(body, outs, *args, name, micros, far=(), scratch=(), limit=24, reads=1000000):
    def space(n, value):
        if value.shape == (1,):
            return pltpu.SMEM
        return pltpu.HBM if n in far else pltpu.VMEM

    return list(pl.pallas_call(
        body,
        out_shape=[jax.ShapeDtypeStruct(s, t) for s, t in outs],
        in_specs=[pl.BlockSpec(memory_space=space(n, a)) for n, a in enumerate(args)],
        out_specs=[pl.BlockSpec(memory_space=pltpu.VMEM)] * len(outs),
        scratch_shapes=scratch,
        cost_estimate=pl.CostEstimate(flops=int(micros * 1.15e9), bytes_accessed=reads, transcendentals=0),
        compiler_params=pltpu.CompilerParams(vmem_limit_bytes=limit * 1024 * 1024),
        name=name,
    )(*args))


SQUARE = ((256, 256), F32)
PAIR = ((2, 256, 256), BF16)
EXTRA = ((8, 128), F32)
PACKED = ((16, 40, 128), F32)
COLUMN = ((256, 128), F32)


def edges(values):
    return values[0:16], values[48:64], values[64:80], values[112:128]


def leaving(values):
    p_low, p_high, u_low, u_high = edges(values)
    return 3.0 * (p_high + u_high), 3.0 * (p_low - u_low)


def put(parity, upward, downward, in_chip_ref, cross_ref, rows=0):
    even = parity == 0
    in_chip_ref[rows : rows + 16] = jnp.where(even, upward, downward)
    cross_ref[rows : rows + 16] = jnp.where(even, downward, upward)


def take(parity, in_chip, cross):
    even = parity == 0
    return jnp.where(even, cross, in_chip), jnp.where(even, in_chip, cross)


def pick(values, table, dot=mm):
    both = dot(jnp.concatenate(split(values), axis=0), table)
    return both[0:16] + both[16:32]


def add_edges(values_ref, first, second, third, fourth):
    values_ref[0:16] += first
    values_ref[48:64] += second
    values_ref[64:80] += third
    values_ref[112:128] += fourth


def one_hot(rows, column):
    return (rows == column).astype(F32).astype(BF16)


def first_kernel(
    parity_ref, state_far, w_in_far, nbr_far, fixed_far, b_in_far, w_out_far, b_out_far, send_far,
    next_ref, hidden_ref, in_chip_ref, cross_ref, w_in, b_in, w_out, b_out, near, state_ref, nbr_ref,
    inner, leave, lift, lift_t, w_in_ref, b_in_ref, w_out_ref, b_out_ref, send_ref, sems,
):
    pairs = (
        (state_far, state_ref), (w_in_far, w_in_ref), (b_in_far, b_in_ref), (fixed_far.at[512:576], leave),
        (nbr_far, nbr_ref), (fixed_far.at[0:512], inner), (fixed_far.at[576:640], lift_t), (w_out_far, w_out_ref),
        (b_out_far, b_out_ref), (send_far, send_ref),
    )
    copies = [pltpu.make_async_copy(s, t, sems.at[n]) for n, (s, t) in enumerate(pairs)]
    for copy in copies:
        copy.start()
    copies[0].wait()
    values = state_ref[...]
    parity = parity_ref[0]
    put(parity, *leaving(state_ref), in_chip_ref, cross_ref)
    copies[1].wait()
    w_in[0], w_in[1] = split(w_in_ref[...])
    for copy in copies[2:5]:
        copy.wait()
    rows = lax.broadcasted_iota(jnp.int32, (256, 256), 0)
    for face in range(2, 6):
        near[face - 2] = one_hot(rows + 256 * (face ^ 1), nbr_ref[face : face + 1])
    for copy in copies[5:]:
        copy.wait()
    lift[...] = flip(lift_t[...])
    w_out[0], w_out[1] = split(w_out_ref[...])
    for row_ref, ref in ((b_in_ref, b_in), (b_out_ref, b_out)):
        ref[...] = jnp.broadcast_to(row_ref[...], (128, 256)).T
    rates = local_rates(values, (w_in, b_in, w_out, b_out, inner, leave, lift, near), hidden_ref)
    next_ref[...] = values + TIME_STEP * rates
    put(parity, *leaving(next_ref), in_chip_ref, cross_ref, 16)
    down_index = send_ref[0:1].astype(F32)
    up_index = (send_ref[1:2] - 256).astype(F32)
    even = parity == 0
    in_chip_ref[32:40] = jnp.broadcast_to(jnp.where(even, up_index, down_index), (8, 256))
    cross_ref[32:40] = jnp.broadcast_to(jnp.where(even, down_index, up_index), (8, 256))


def flip(values):
    return values.astype(F32).T.astype(BF16)


def tables_kernel(
    w_in, w_out, inner, leave, nbr_ref, state_ref, after_ref, in_t_ref, out_t_ref, inner_t, leave_t, far_ref, copy_ref
):
    copy_ref[...] = state_ref[...]
    for part in range(2):
        in_t_ref[part] = flip(w_in[part])
        out_t_ref[part] = flip(w_out[part])
        inner_t[256 * part : 256 * part + 256] = flip(inner[256 * part : 256 * part + 256])
    leave_t[...] = flip(leave[...])
    rows = lax.broadcasted_iota(jnp.int32, (256, 256), 0)
    for face in range(2):
        far_ref[face] = one_hot(rows + (1536 + 256 * face), nbr_ref[face : face + 1])


def wide(column):
    return jnp.concatenate([column[...], column[...]], axis=1)


def local_rates(values, network, hidden_ref):
    w_in, b_in, w_out, b_out, inner, leave, lift, near = network
    parts = split(values)
    hidden = jnp.tanh(mm3(pair(w_in), parts) + wide(b_in))
    hidden_ref[...] = hidden
    rates = mm3(pair(inner), parts) + wide(b_out)
    high, low = split(mm(leave[...], parts[0]) + mm(leave[...], parts[1]))
    arrived = []
    for n in range(4):
        both = jnp.concatenate([high[16 * n : 16 * n + 16], low[16 * n : 16 * n + 16]], axis=0)
        arrived.append(mm(both, near[n]).astype(BF16))
    for part in range(2):
        rates += mm(lift[...], jnp.concatenate([a[16 * part : 16 * part + 16] for a in arrived], axis=0))
    return rates + mm3(pair(w_out), split(hidden))


def add_arrived(weight, base_ref, below, above, link, now_ref):
    low = weight * pick(below, link[0])
    high = weight * pick(above, link[1])
    now_ref[...] = base_ref[...]
    add_edges(now_ref, low, high, low, -high)
    return now_ref[...]


def middle_kernel(
    parity_ref, base_ref, state_ref, in_chip, cross, far_ref,
    w_in, b_in, w_out, b_out, inner, leave, lift, near,
    second_ref, third_ref, hidden_second, hidden_third, next_ref, link, in_chip_out, cross_out, between,
):
    network = (w_in, b_in, w_out, b_out, inner, leave, lift, near)
    parity = parity_ref[0]
    below, above = take(parity, in_chip[...], cross[...])
    rows = lax.broadcasted_iota(jnp.int32, (256, 256), 0).astype(F32)
    for side, received in enumerate((below, above)):
        link[side] = mm(one_hot(rows, received[32:33]), far_ref[side]).astype(BF16)
    values = add_arrived(TIME_STEP, base_ref, below[0:16], above[0:16], link, second_ref)
    between[...] = 0.5 * (state_ref[...] + values) + HALF_STEP * local_rates(values, network, hidden_second)
    put(parity, *leaving(between), in_chip_out, cross_out)
    values = add_arrived(HALF_STEP, between, below[16:32], above[16:32], link, third_ref)
    next_ref[...] = values + TIME_STEP * local_rates(values, network, hidden_third)
    put(parity, *leaving(next_ref), in_chip_out, cross_out, 16)


def sensitivities(values, link):
    p_low, p_high, u_low, u_high = edges(values)
    return pick(p_high - u_high, link[1], mm_nt), pick(p_low + u_low, link[0], mm_nt)


def through_closure(parts, hidden, w_out_t):
    return (1.0 - hidden * hidden) * mm3(w_out_t, parts)


def back_rates(parts, delta_parts, network):
    w_in_t, inner_t, leave_t, lift_t, near = network
    rates = mm3(pair(inner_t), parts) + mm3(pair(w_in_t), delta_parts)
    high, low = split(mm(lift_t[...], parts[0]) + mm(lift_t[...], parts[1]))
    arrived = []
    for n in range(4):
        both = jnp.concatenate([high[16 * n : 16 * n + 16], low[16 * n : 16 * n + 16]], axis=0)
        arrived.append(mm_nt(both, near[n]))
    high, low = split(jnp.concatenate([a[0:16] + a[16:32] for a in arrived], axis=0))
    return rates + (mm(leave_t[...], high) + mm(leave_t[...], low))


def turn_kernel(
    parity_ref, base_ref, third_ref, in_chip, cross, link, target_ref,
    w_in, b_in, w_out, b_out, inner, leave, lift, near, w_in_t, w_out_t, inner_t, leave_t, lift_t,
    final_ref, loss_ref, fourth_ref, hidden_ref, adjoint_ref, delta_ref, next_ref, in_chip_out, cross_out, between,
):
    network = (w_in, b_in, w_out, b_out, inner, leave, lift, near)
    parity = parity_ref[0]
    below, above = take(parity, in_chip[...], cross[...])
    values = add_arrived(TIME_STEP, base_ref, below[0:16], above[0:16], link, fourth_ref)
    between[...] = 0.5 * (third_ref[...] + values) + HALF_STEP * local_rates(values, network, hidden_ref)
    final = add_arrived(HALF_STEP, between, below[16:32], above[16:32], link, final_ref)
    mismatch = final - target_ref[...]
    adjoint = (HALF_STEP / COUNT) * mismatch
    adjoint_ref[...] = adjoint
    squares = jnp.sum(mismatch * mismatch, axis=0, keepdims=True)
    loss_ref[...] = jnp.broadcast_to(squares[:, 0:128] + squares[:, 128:256], (8, 128))
    put(parity, *sensitivities(adjoint_ref, link), in_chip_out, cross_out)
    parts = split(adjoint)
    delta = through_closure(parts, hidden_ref[...], pair(w_out_t))
    delta_ref[...] = delta
    next_ref[...] = adjoint + TIME_STEP * back_rates(parts, split(delta), (w_in_t, inner_t, leave_t, lift_t, near))
    put(parity, *sensitivities(next_ref, link), in_chip_out, cross_out, 16)


def gradients(parts, delta_parts, state, hidden):
    ones = jnp.ones((8, 256), BF16)
    rows = lax.broadcasted_iota(jnp.int32, (8, 128), 0)
    first = mm_nt(ones, delta_parts[0]) + mm_nt(ones, delta_parts[1])
    second = mm_nt(ones, parts[0]) + mm_nt(ones, parts[1])
    bias = jnp.where(rows == 0, first[:, 0:128], jnp.where(rows == 1, first[:, 128:256], 0.0))
    bias = jnp.where(rows == 2, second[:, 0:128], bias)
    if second.shape[1] == 256:
        bias = jnp.where(rows == 3, second[:, 128:256], bias)
    return mm3(delta_parts, split(state), mm_nt), mm3(parts, split(hidden), mm_nt), bias


def beside_kernel(
    adjoint_ref, delta_ref, state_ref, hidden_ref, in_chip, cross, w_in, b_in,
    grad_in, grad_out, extra, in_chip_hidden, cross_hidden,
):
    grad_in[...], grad_out[...], extra[...] = gradients(
        split(adjoint_ref[...]), split(delta_ref[...]), state_ref[...], hidden_ref[...]
    )
    for source, ref in ((in_chip, in_chip_hidden), (cross, cross_hidden)):
        ref[...] = jnp.tanh(mm3(pair(w_in), split(source[...])) + wide(b_in))


def back_kernel(
    parity_ref, base_ref, adjoint_ref, in_chip, cross, link,
    third_ref, hidden_third, second_ref, hidden_second, state_ref, hidden_first,
    in_chip_state, cross_state, in_chip_hidden, cross_hidden,
    near, w_in_t, w_out_t, inner_t, leave_t, lift_t, old_in, old_out, old_extra, loss_ref,
    keep_ref, send_ref, now_ref, between, sum_ref,
):
    network = (w_in_t, inner_t, leave_t, lift_t, near)
    parity = parity_ref[0]
    even = parity == 0
    below, above = take(parity, in_chip[...], cross[...])
    totals = [old_in[...], old_out[...], old_extra[...]]

    def arrive(source_ref, weight, low, high):
        now_ref[...] = source_ref[...]
        low, high = weight * low, weight * high
        add_edges(now_ref, low, high, -low, high)
        return now_ref[...]

    def gather(*args):
        for n, term in enumerate(gradients(*args)):
            totals[n] = totals[n] + term

    values = arrive(base_ref, 3.0 * TIME_STEP, below[0:16], above[0:16])
    parts = split(values)
    delta = split(through_closure(parts, hidden_third[...], pair(w_out_t)))
    between[...] = 0.5 * (adjoint_ref[...] + values) + HALF_STEP * back_rates(parts, delta, network)
    gather(parts, delta, third_ref[...], hidden_third[...])
    upward, downward = sensitivities(between, link)

    values = arrive(between, 3.0 * HALF_STEP, below[16:32], above[16:32])
    parts = split(values)
    delta = split(through_closure(parts, hidden_second[...], pair(w_out_t)))
    values = values + TIME_STEP * back_rates(parts, delta, network)
    gather(parts, delta, second_ref[...], hidden_second[...])

    parts = split(values)
    delta = split(through_closure(parts, hidden_first[...], pair(w_out_t)))
    gather(parts, delta, state_ref[...], hidden_first[...])

    states = take(parity, in_chip_state[...], cross_state[...])
    hiddens = take(parity, in_chip_hidden[...], cross_hidden[...])
    w_edge = w_out_t[0, :, 0:128], w_out_t[1, :, 0:128]
    weight = 3.0 * TIME_STEP
    none = jnp.zeros((48, 256), F32)
    low, high = weight * upward, weight * downward
    for values, state, hidden in (
        (jnp.concatenate([none, high, none, high], axis=0), states[0], hiddens[0]),
        (jnp.concatenate([low, none, -low, none], axis=0), states[1], hiddens[1]),
    ):
        parts = split(values)
        delta = split(through_closure(parts, hidden, w_edge))
        first, second, bias = gradients(parts, delta, state, hidden)
        totals[0] = totals[0] + first
        totals[2] = totals[2] + bias
        sum_ref[...] = totals[1]
        sum_ref[0:128] += second
        totals[1] = sum_ref[...]
    first, second, bias = totals
    rows = lax.broadcasted_iota(jnp.int32, (8, 128), 0)
    bias = jnp.where(rows == 4, loss_ref[...], bias)
    for ref, values in ((keep_ref, jnp.where(even, first, second)), (send_ref, jnp.where(even, second, first))):
        for n in range(16):
            ref[n, 0:16] = values[16 * n : 16 * n + 16, 0:128]
            ref[n, 16:32] = values[16 * n : 16 * n + 16, 128:256]
            ref[n, 32:40] = bias


def chip_kernel(keep_ref, got_ref, out_ref):
    out_ref[...] = keep_ref[...] + got_ref[...]


def plane_kernel(parts_ref, out_ref):
    total = jnp.sum(parts_ref[...], axis=0)
    for n in range(8):
        out_ref[n] = total


def line_kernel(parts_ref, out_ref, extra_ref):
    total = jnp.sum(parts_ref[...], axis=0)
    extra_ref[...] = total[32:40]
    for n in range(16):
        out_ref[n] = total[0:32]


def last_kernel(parity_ref, own_ref, other_ref, extra_ref, in_ref, b_in_ref, out_ref, b_out_ref, loss_ref):
    even = parity_ref[0] == 0
    own, other = own_ref[...], other_ref[...]
    first = jnp.where(even, own, other)
    second = jnp.where(even, other, own)
    bias = extra_ref[0:4]
    squares = jnp.sum(first * first + second * second, axis=0)
    total = jnp.sum(squares, keepdims=True) + jnp.sum(bias * bias, keepdims=True)
    scale = lax.rsqrt(total / PARAMS + TINY)
    for ref, values in ((in_ref, first * scale), (out_ref, second * scale)):
        for n in range(16):
            ref[16 * n : 16 * n + 16, 0:128] = values[n, 0:16]
            ref[16 * n : 16 * n + 16, 128:256] = values[n, 16:32]
    bias = bias * scale
    for row, ref in ((0, b_in_ref), (2, b_out_ref)):
        ref[:, 0:128] = bias[row : row + 1]
        ref[:, 128:256] = bias[row + 1 : row + 2]
    loss_ref[...] = jnp.sum(extra_ref[4:5], keepdims=True) * (0.5 / COUNT)


IN_CHIP = [(n, n ^ 1) for n in range(DEVICES)]
CROSS = [(n, (n - 1) % DEVICES if n % 2 == 0 else (n + 1) % DEVICES) for n in range(DEVICES)]


def exchange(in_chip, cross):
    return lax.ppermute(in_chip, AXES, IN_CHIP), lax.ppermute(cross, AXES, CROSS)


def local(state, target, w_in, b_in, w_out, b_out, nbr, send):
    parity = lax.axis_index("core").reshape(1)
    inner, leave, lift = operators()
    weights = [PAIR, COLUMN, PAIR, COLUMN]
    fixed = np.concatenate([*halves(inner), leave, lift.T], axis=0).astype(ml_dtypes.bfloat16)
    line = lambda values: values.reshape(1, 256)
    tall, flat, thin = ((512, 256), BF16), ((64, 256), BF16), ((256, 64), BF16)
    base, hidden_first, *edge, w_in2, b_in2, w_out2, b_out2, near, state, nbr, inner2, leave1, lift1, lift_t = call(
        first_kernel,
        [SQUARE, SQUARE, ((40, 256), F32), ((40, 256), F32)]
        + weights
        + [((4, 256, 256), BF16), SQUARE, ((6, 256), jnp.int32), tall, flat, thin, flat],
        parity, state, w_in, nbr, jnp.asarray(fixed), line(b_in), w_out, line(b_out), send,
        name="first", micros=1.5,
        far=range(1, 9),
        limit=52,
        scratch=[
            pltpu.VMEM((256, 256), F32), pltpu.VMEM((1, 256), F32), pltpu.VMEM((256, 256), F32),
            pltpu.VMEM((1, 256), F32), pltpu.VMEM((2, 256), jnp.int32), pltpu.SemaphoreType.DMA((10,)),
        ],
    )
    got = exchange(*edge)
    w_in_t, w_out_t, inner_t, leave_t, far, copy = call(
        tables_kernel,
        [PAIR, PAIR, tall, thin, PAIR, SQUARE],
        w_in2, w_out2, inner2, leave1, nbr, state, got[0],
        name="tables", micros=0.4,
    )
    beside = exchange(copy, copy)
    network = (w_in2, b_in2, w_out2, b_out2, inner2, leave1, lift1, near)
    back = (w_in_t, w_out_t, inner_t, leave_t, lift_t)
    edge_shapes = [((32, 256), F32)] * 2
    second, third, hidden_second, hidden_third, base, link, *edge, _ = call(
        middle_kernel,
        [SQUARE] * 5 + [PAIR] + edge_shapes + [SQUARE],
        parity, base, state, *got, far, *network, name="middle", micros=2.8,
    )
    got = exchange(*edge)
    final, loss, fourth, hidden_fourth, adjoint, delta, base, *edge, _ = call(
        turn_kernel,
        [SQUARE, EXTRA] + [SQUARE] * 5 + edge_shapes + [SQUARE],
        parity, base, third, *got, link, target, *network, *back, name="turn", micros=3,
    )
    got = exchange(*edge)
    *grads, in_chip_hidden, cross_hidden = call(
        beside_kernel,
        [SQUARE, SQUARE, EXTRA, SQUARE, SQUARE],
        adjoint, delta, fourth, hidden_fourth, *beside, w_in2, b_in2, name="beside", micros=0.8,
    )
    keep, give, *_ = call(
        back_kernel,
        [PACKED] * 2 + [SQUARE] * 3,
        parity, base, adjoint, *got, link, third, hidden_third, second, hidden_second, state, hidden_first,
        *beside, in_chip_hidden, cross_hidden, near, *back, *grads, loss, name="back", micros=4.5,
    )
    swap = [(0, 1), (1, 0)]
    (parts,) = call(chip_kernel, [PACKED], keep, lax.ppermute(give, "core", swap), name="chip_sum", micros=0.3)
    parts = lax.all_to_all(parts, PLANE, 0, 0, tiled=True)
    (parts,) = call(plane_kernel, [((8, 40, 128), F32)], parts, name="plane_sum", micros=0.3)
    parts = lax.all_to_all(parts, "z", 0, 0, tiled=True)
    parts, extra = call(line_kernel, [((16, 32, 128), F32), EXTRA], parts, name="line_sum", micros=0.3)
    own = lax.all_to_all(parts, PLANE, 0, 0, tiled=True)
    other = lax.ppermute(own, "core", swap)
    row = ((1, 256), F32)
    step_in, step_b_in, step_out, step_b_out, loss = call(
        last_kernel, [SQUARE, row, SQUARE, row, ((1, 1), F32)], parity, own, other, extra, name="scale", micros=1
    )
    return final, loss.reshape(()), step_in, step_b_in.reshape(256), step_out, step_b_out.reshape(256)


def solution(mesh):
    split_mesh = Mesh(mesh.devices.reshape(SIZES), AXES)
    whole = P(None, AXES)
    return jax.shard_map(
        local,
        mesh=split_mesh,
        in_specs=(whole, whole, P(), P(), P(), P(), whole, whole),
        out_specs=(whole, P(), P(), P(), P(), P()),
        check_vma=False,
    )
```

```python
import jax
import jax.numpy as jnp
import ml_dtypes
import numpy as np
from jax import lax
from jax.experimental import pallas as pl
from jax.experimental.pallas import tpu as pltpu
from jax.sharding import Mesh, PartitionSpec as P

AXES = ("x", "y", "z", "core")
PLANE = ("x", "y")
SIZES = (4, 4, 8, 2)
DEVICES = 256
WIDTH = 256
COUNT = 16777216.0
PARAMS = 131584.0
TIME_STEP = 0.05
HALF_STEP = 0.025
TINY = 1e-20
F32 = jnp.float32
BF16 = jnp.bfloat16


def face_rows(face):
    layer = 0 if face % 2 == 0 else 3
    grid = np.arange(64).reshape(4, 4, 4)
    return np.take(grid, layer, axis=face // 2).reshape(16)


def operators():
    points = np.array([-1.0, -1.0 / np.sqrt(5.0), 1.0 / np.sqrt(5.0), 1.0])
    bary = np.array(
        [1.0 / np.prod([points[m] - points[n] for n in range(4) if n != m]) for m in range(4)]
    )
    deriv = np.zeros((4, 4))
    for m in range(4):
        for n in range(4):
            if m != n:
                deriv[m, n] = bary[n] / bary[m] / (points[m] - points[n])
        deriv[m, m] = -np.sum(deriv[m])
    eye = np.eye(4)
    tables = [
        np.kron(np.kron(deriv, eye), eye),
        np.kron(np.kron(eye, deriv), eye),
        np.kron(eye, np.kron(eye, deriv)),
    ]
    inner = np.zeros((256, 256))
    for a in range(3):
        inner[0:64, 64 * (a + 1) : 64 * (a + 2)] -= tables[a]
        inner[64 * (a + 1) : 64 * (a + 2), 0:64] -= tables[a]
    for face in range(6):
        sign = 2.0 * (face % 2) - 1.0
        for row in face_rows(face):
            speed = 64 * (face // 2 + 1) + row
            inner[row, row] -= 3.0
            inner[row, speed] += 3.0 * sign
            inner[speed, speed] -= 3.0
            inner[speed, row] += 3.0 * sign
    leave = np.zeros((64, 256))
    lift = np.zeros((256, 64))
    for face in range(2, 6):
        sign = 2.0 * (face % 2) - 1.0
        base = 16 * (face - 2)
        for n, row in enumerate(face_rows(face ^ 1)):
            leave[base + n, row] = 3.0
            leave[base + n, 64 * (face // 2 + 1) + row] = -3.0 * sign
        for n, row in enumerate(face_rows(face)):
            lift[row, base + n] = 1.0
            lift[64 * (face // 2 + 1) + row, base + n] = -sign
    return inner, leave, lift


def halves(values):
    high = values.astype(ml_dtypes.bfloat16)
    low = (values - high.astype(np.float64)).astype(ml_dtypes.bfloat16)
    return high, low


def split(values):
    high = values.astype(BF16)
    return high, (values - high.astype(F32)).astype(BF16)


def mm(left, right):
    return jnp.dot(left, right, preferred_element_type=F32)


def mm_nt(left, right):
    return lax.dot_general(left, right, (((1,), (1,)), ((), ())), preferred_element_type=F32)


def mm3(left, right, dot=mm):
    return dot(left[0], right[0]) + (dot(left[0], right[1]) + dot(left[1], right[0]))


def pair(ref):
    if len(ref.shape) == 2:
        return ref[0:256], ref[256:512]
    return ref[0], ref[1]


def call(body, outs, *args, name, micros, far=(), scratch=(), limit=24, reads=1000000):
    def space(n, value):
        if value.shape == (1,):
            return pltpu.SMEM
        return pltpu.HBM if n in far else pltpu.VMEM

    return list(pl.pallas_call(
        body,
        out_shape=[jax.ShapeDtypeStruct(s, t) for s, t in outs],
        in_specs=[pl.BlockSpec(memory_space=space(n, a)) for n, a in enumerate(args)],
        out_specs=[pl.BlockSpec(memory_space=pltpu.VMEM)] * len(outs),
        scratch_shapes=scratch,
        cost_estimate=pl.CostEstimate(flops=int(micros * 1.15e9), bytes_accessed=reads, transcendentals=0),
        compiler_params=pltpu.CompilerParams(vmem_limit_bytes=int(limit * 1048576)),
        name=name,
    )(*args))


SQUARE = ((256, 256), F32)
PAIR = ((2, 256, 256), BF16)
EXTRA = ((8, 128), F32)
PACKED = ((16, 40, 128), F32)


def edges(values):
    return values[0:16], values[48:64], values[64:80], values[112:128]


def edge_rows(values):
    return jnp.concatenate(edges(values), axis=0)


def leaving(edge):
    return 3.0 * (edge[16:32] + edge[48:64]), 3.0 * (edge[0:16] - edge[32:48])


def put(parity, upward, downward, in_chip_ref, cross_ref, rows=0):
    even = parity == 0
    in_chip_ref[rows : rows + 16] = jnp.where(even, upward, downward)
    cross_ref[rows : rows + 16] = jnp.where(even, downward, upward)


def take(parity, in_chip, cross):
    even = parity == 0
    return jnp.where(even, cross, in_chip), jnp.where(even, in_chip, cross)


def pick(values, table, dot=mm):
    both = dot(jnp.concatenate(split(values), axis=0), table)
    return both[0:16] + both[16:32]


def add_edges(values_ref, first, second, third, fourth):
    values_ref[0:16] += first
    values_ref[48:64] += second
    values_ref[64:80] += third
    values_ref[112:128] += fourth


def one_hot(rows, column):
    return (rows == column).astype(F32).astype(BF16)


def make_near(nbr_ref, near):
    rows = lax.broadcasted_iota(jnp.int32, (256, 256), 0)
    for face in range(2, 6):
        near[face - 2] = one_hot(rows + 256 * (face ^ 1), nbr_ref[face : face + 1])


def first_kernel(
    parity_ref, state_far, w_in_far, nbr_far, fixed_far, b_in_far, w_out_far, b_out_far, send_far,
    arrived_ref, hidden_ref, in_chip_ref, cross_ref, w_in, w_out, state_ref, nbr_ref, inner, leave, lift, lift_t,
    w_in_ref, b_in_ref, w_out_ref, b_out_ref, send_ref, near, sems,
):
    pairs = (
        (state_far, state_ref), (w_in_far, w_in_ref), (b_in_far, b_in_ref), (fixed_far.at[512:576], leave),
        (nbr_far, nbr_ref), (fixed_far.at[0:512], inner), (fixed_far.at[576:640], lift_t), (w_out_far, w_out_ref),
        (b_out_far, b_out_ref), (send_far, send_ref),
    )
    copies = [pltpu.make_async_copy(s, t, sems.at[n]) for n, (s, t) in enumerate(pairs)]
    for copy in copies:
        copy.start()
    copies[0].wait()
    values = state_ref[...]
    edge = edge_rows(values)
    parts = split(values)
    parity = parity_ref[0]
    put(parity, *leaving(edge), in_chip_ref, cross_ref)
    copies[1].wait()
    w_in[0], w_in[1] = split(w_in_ref[...])
    for copy in copies[2:5]:
        copy.wait()
    make_near(nbr_ref, near)
    arrive_near(parts, leave, near, arrived_ref)
    hidden = jnp.tanh(mm3(pair(w_in), parts) + wide(b_in_ref))
    hidden_ref[...] = hidden
    for copy in copies[5:]:
        copy.wait()
    lift[...] = flip(lift_t[...])
    w_out[0], w_out[1] = split(w_out_ref[...])
    rates = edge_rates(parts, split(hidden), (w_in, b_in_ref, w_out, b_out_ref, inner, leave, lift, near), arrived_ref)
    put(parity, *leaving(edge + TIME_STEP * rates), in_chip_ref, cross_ref, 16)
    down_index = send_ref[0:1].astype(F32)
    up_index = (send_ref[1:2] - 256).astype(F32)
    even = parity == 0
    in_chip_ref[32:40] = jnp.broadcast_to(jnp.where(even, up_index, down_index), (8, 256))
    cross_ref[32:40] = jnp.broadcast_to(jnp.where(even, down_index, up_index), (8, 256))


def flip(values):
    return values.astype(F32).T.astype(BF16)


def tables_kernel(
    w_in, b_in, w_out, b_out, inner, leave, lift, nbr_ref, state_ref, arrived_ref, hidden_ref, after_ref,
    next_ref, in_t_ref, out_t_ref, inner_t, leave_t, near, far_ref, eff_ref, copy_ref, column_in, column_out,
):
    column_in[...] = column(b_in)
    column_out[...] = column(b_out)
    values = state_ref[...]
    copy_ref[...] = values
    network = (w_in, b_in, w_out, b_out, inner, leave, lift, near)
    next_ref[...] = values + TIME_STEP * full_rates(split(values), split(hidden_ref[...]), network, arrived_ref)
    make_near(nbr_ref, near)
    rows = lax.broadcasted_iota(jnp.int32, (256, 256), 0)
    for face in range(2):
        far_ref[face] = one_hot(rows + (1536 + 256 * face), nbr_ref[face : face + 1])
    for part in range(2):
        in_t_ref[part] = flip(w_in[part])
        out_t_ref[part] = flip(w_out[part])
        inner_t[256 * part : 256 * part + 256] = flip(inner[256 * part : 256 * part + 256])
    leave_t[...] = flip(leave[...])
    whole = w_out[0].astype(F32) + w_out[1].astype(F32)
    for side, seen in enumerate((whole[48:64] + whole[112:128], whole[0:16] - whole[64:80])):
        high, low = split(seen.T)
        eff_ref[side] = jnp.concatenate([high, high, low], axis=1)


def column(row):
    return jnp.broadcast_to(row[...], (128, 256)).T


def wide(bias):
    values = column(bias) if bias.shape[0] == 1 else bias[...]
    return jnp.concatenate([values, values], axis=1)


def gather(high, low, near, dot):
    for n in range(4):
        both = jnp.concatenate([high[16 * n : 16 * n + 16], low[16 * n : 16 * n + 16]], axis=0)
        yield dot(both, near[n])


def arrive_near(parts, leave, near, arrived_ref):
    high, low = split(mm(leave[...], parts[0]) + mm(leave[...], parts[1]))
    for n, both in enumerate(gather(high, low, near, mm)):
        both = both.astype(BF16)
        arrived_ref[0, 16 * n : 16 * n + 16] = both[0:16]
        arrived_ref[1, 16 * n : 16 * n + 16] = both[16:32]


def edge_rates(parts, hidden_parts, network, arrived_ref):
    w_in, b_in, w_out, b_out, inner, leave, lift, near = network
    rates = mm3([edge_rows(x) for x in pair(inner)], parts) + edge_rows(wide(b_out))
    rates += mm(edge_rows(lift), arrived_ref[0]) + mm(edge_rows(lift), arrived_ref[1])
    return rates + mm3([edge_rows(x) for x in pair(w_out)], hidden_parts)


def full_rates(parts, hidden_parts, network, arrived_ref):
    w_in, b_in, w_out, b_out, inner, leave, lift, near = network
    rates = mm3(pair(inner), parts) + wide(b_out)
    rates += mm(lift[...], arrived_ref[0]) + mm(lift[...], arrived_ref[1])
    return rates + mm3(pair(w_out), hidden_parts)


def activate(parts, network, hidden_ref, arrived_ref):
    w_in, b_in, w_out, b_out, inner, leave, lift, near = network
    hidden = jnp.tanh(mm3(pair(w_in), parts) + wide(b_in))
    hidden_ref[...] = hidden
    arrive_near(parts, leave, near, arrived_ref)
    return split(hidden)


def add_arrived(weight, base_ref, below, above, link, now_ref):
    low = weight * pick(below, link[0])
    high = weight * pick(above, link[1])
    now_ref[...] = base_ref[...]
    add_edges(now_ref, low, high, low, -high)
    return now_ref[...]


def middle_kernel(
    parity_ref, base_ref, state_ref, in_chip, cross, far_ref,
    w_in, b_in, w_out, b_out, inner, leave, lift, near,
    second_ref, third_ref, hidden_second, hidden_third, arrived_ref, link, in_chip_out, cross_out, between,
):
    network = (w_in, b_in, w_out, b_out, inner, leave, lift, near)
    parity = parity_ref[0]
    below, above = take(parity, in_chip[...], cross[...])
    rows = lax.broadcasted_iota(jnp.int32, (256, 256), 0).astype(F32)
    for side, received in enumerate((below, above)):
        link[side] = mm(one_hot(rows, received[32:33]), far_ref[side]).astype(BF16)
    values = add_arrived(TIME_STEP, base_ref, below[0:16], above[0:16], link, second_ref)
    parts = split(values)
    hidden_parts = activate(parts, network, hidden_second, arrived_ref)
    rates = full_rates(parts, hidden_parts, network, arrived_ref)
    between[...] = 0.5 * (state_ref[...] + values) + HALF_STEP * rates
    put(parity, *leaving(edge_rows(between)), in_chip_out, cross_out)
    values = add_arrived(HALF_STEP, between, below[16:32], above[16:32], link, third_ref)
    parts = split(values)
    hidden_parts = activate(parts, network, hidden_third, arrived_ref)
    rates = edge_rates(parts, hidden_parts, network, arrived_ref)
    put(parity, *leaving(edge_rows(values) + TIME_STEP * rates), in_chip_out, cross_out, 16)


def rest_kernel(
    third_ref, hidden_ref, arrived_ref, w_in, b_in, w_out, b_out, inner, leave, lift, near, next_ref
):
    network = (w_in, b_in, w_out, b_out, inner, leave, lift, near)
    values = third_ref[...]
    next_ref[...] = values + TIME_STEP * full_rates(split(values), split(hidden_ref[...]), network, arrived_ref)


def sensitivities(edge, link):
    upward = pick(edge[16:32] - edge[48:64], link[1], mm_nt)
    return upward, pick(edge[0:16] + edge[32:48], link[0], mm_nt)


def through_closure(parts, hidden, w_out_t):
    return (1.0 - hidden * hidden) * mm3(w_out_t, parts)


def gather_back(parts, lift_t, near):
    high, low = split(mm(lift_t[...], parts[0]) + mm(lift_t[...], parts[1]))
    return split(jnp.concatenate([a[0:16] + a[16:32] for a in gather(high, low, near, mm_nt)], axis=0))


def back_rates(parts, delta_parts, network, gathered, rows=lambda values: values[...]):
    w_in_t, inner_t, leave_t, lift_t, near = network
    rates = mm3([rows(x) for x in pair(inner_t)], parts) + mm3([rows(x) for x in pair(w_in_t)], delta_parts)
    return rates + (mm(rows(leave_t), gathered[0]) + mm(rows(leave_t), gathered[1]))


def turn_kernel(
    parity_ref, base_ref, third_ref, in_chip, cross, link, target_ref,
    w_in, b_in, w_out, b_out, inner, leave, lift, near, w_in_t, w_out_t, inner_t, leave_t, lift_t,
    final_ref, loss_ref, fourth_ref, hidden_ref, adjoint_ref, delta_ref, gathered_ref, in_chip_out, cross_out,
    between, arrived_ref,
):
    network = (w_in, b_in, w_out, b_out, inner, leave, lift, near)
    parity = parity_ref[0]
    below, above = take(parity, in_chip[...], cross[...])
    values = add_arrived(TIME_STEP, base_ref, below[0:16], above[0:16], link, fourth_ref)
    parts = split(values)
    hidden_parts = activate(parts, network, hidden_ref, arrived_ref)
    rates = full_rates(parts, hidden_parts, network, arrived_ref)
    between[...] = 0.5 * (third_ref[...] + values) + HALF_STEP * rates
    final = add_arrived(HALF_STEP, between, below[16:32], above[16:32], link, final_ref)
    mismatch = final - target_ref[...]
    adjoint = (HALF_STEP / COUNT) * mismatch
    adjoint_ref[...] = adjoint
    squares = jnp.sum(mismatch * mismatch, axis=0, keepdims=True)
    loss_ref[...] = jnp.broadcast_to(squares[:, 0:128] + squares[:, 128:256], (8, 128))
    edge = edge_rows(adjoint)
    put(parity, *sensitivities(edge, link), in_chip_out, cross_out)
    parts = split(adjoint)
    delta = through_closure(parts, hidden_ref[...], pair(w_out_t))
    delta_ref[...] = delta
    gathered = gather_back(parts, lift_t, near)
    gathered_ref[0], gathered_ref[1] = gathered
    back = (w_in_t, inner_t, leave_t, lift_t, near)
    rates = back_rates(parts, split(delta), back, gathered, edge_rows)
    put(parity, *sensitivities(edge + TIME_STEP * rates, link), in_chip_out, cross_out, 16)


def bias_rows(first, second):
    rows = lax.broadcasted_iota(jnp.int32, (8, 128), 0)
    bias = jnp.where(rows == 0, first[:, 0:128], jnp.where(rows == 1, first[:, 128:256], 0.0))
    bias = jnp.where(rows == 2, second[:, 0:128], bias)
    if second.shape[1] == 256:
        bias = jnp.where(rows == 3, second[:, 128:256], bias)
    return bias


def row_sums(parts):
    ones = jnp.ones((8, 256), BF16)
    return mm_nt(ones, parts[0]) + mm_nt(ones, parts[1])


def gradients(parts, delta_parts, state, hidden):
    bias = bias_rows(row_sums(delta_parts), row_sums(parts))
    return mm3(delta_parts, split(state), mm_nt), mm3(parts, split(hidden), mm_nt), bias


def beside_kernel(
    adjoint_ref, delta_ref, gathered_ref, state_ref, hidden_ref, in_chip, cross, w_in, b_in,
    w_in_t, inner_t, leave_t, lift_t, near,
    next_ref, grad_in, grad_out, extra, in_chip_hidden, cross_hidden,
):
    adjoint = adjoint_ref[...]
    parts, delta_parts = split(adjoint), split(delta_ref[...])
    gathered = gathered_ref[0], gathered_ref[1]
    next_ref[...] = adjoint + TIME_STEP * back_rates(
        parts, delta_parts, (w_in_t, inner_t, leave_t, lift_t, near), gathered
    )
    grad_in[...], grad_out[...], extra[...] = gradients(parts, delta_parts, state_ref[...], hidden_ref[...])
    for source, ref in ((in_chip, in_chip_hidden), (cross, cross_hidden)):
        ref[...] = jnp.tanh(mm3(pair(w_in), split(source[...])) + wide(b_in))


def back_kernel(
    parity_ref, base_ref, adjoint_ref, in_chip, cross, link,
    third_ref, hidden_third, second_ref, hidden_second, state_ref, hidden_first,
    in_chip_state, cross_state, in_chip_hidden, cross_hidden,
    near, w_in_t, w_out_t, inner_t, leave_t, lift_t, eff, old_in, old_out, old_extra, loss_ref,
    keep_ref, send_ref, now_ref, between, sum_ref,
):
    network = (w_in_t, inner_t, leave_t, lift_t, near)
    parity = parity_ref[0]
    even = parity == 0
    below, above = take(parity, in_chip[...], cross[...])
    totals = [old_in[...], old_out[...], old_extra[...]]

    def arrive(source_ref, weight, low, high):
        now_ref[...] = source_ref[...]
        low, high = weight * low, weight * high
        add_edges(now_ref, low, high, -low, high)
        return now_ref[...]

    def collect(*args):
        for n, term in enumerate(gradients(*args)):
            totals[n] = totals[n] + term

    values = arrive(base_ref, 3.0 * TIME_STEP, below[0:16], above[0:16])
    parts = split(values)
    delta = split(through_closure(parts, hidden_third[...], pair(w_out_t)))
    rates = back_rates(parts, delta, network, gather_back(parts, lift_t, near))
    between[...] = 0.5 * (adjoint_ref[...] + values) + HALF_STEP * rates
    collect(parts, delta, third_ref[...], hidden_third[...])
    upward, downward = sensitivities(edge_rows(between), link)

    values = arrive(between, 3.0 * HALF_STEP, below[16:32], above[16:32])
    parts = split(values)
    delta = split(through_closure(parts, hidden_second[...], pair(w_out_t)))
    values = values + TIME_STEP * back_rates(parts, delta, network, gather_back(parts, lift_t, near))
    collect(parts, delta, second_ref[...], hidden_second[...])

    states = take(parity, in_chip_state[...], cross_state[...])
    hiddens = take(parity, in_chip_hidden[...], cross_hidden[...])
    weight = 3.0 * TIME_STEP
    blocks = []
    for side, received in enumerate((weight * downward, weight * upward)):
        high, low = split(received)
        hidden = hiddens[side]
        seen = mm(eff[side], jnp.concatenate([high, low, high], axis=0))
        delta = split((1.0 - hidden * hidden) * seen)
        totals[0] = totals[0] + mm3(delta, split(states[side]), mm_nt)
        blocks.append(mm3((high, low), split(hidden), mm_nt))
        none = jnp.zeros((48, 256), F32)
        spread = [none, received, none, received] if side == 0 else [received, none, -received, none]
        totals[2] = totals[2] + bias_rows(row_sums(delta), row_sums(split(jnp.concatenate(spread, axis=0))))

    parts = split(values)
    delta = split(through_closure(parts, hidden_first[...], pair(w_out_t)))
    collect(parts, delta, state_ref[...], hidden_first[...])
    sum_ref[...] = totals[1]
    add_edges(sum_ref, blocks[1], blocks[0], -blocks[1], blocks[0])
    first, second, bias = totals[0], sum_ref[...], totals[2]
    rows = lax.broadcasted_iota(jnp.int32, (8, 128), 0)
    bias = jnp.where(rows == 4, loss_ref[...], bias)
    for ref, values in ((keep_ref, jnp.where(even, first, second)), (send_ref, jnp.where(even, second, first))):
        for n in range(16):
            ref[n, 0:16] = values[16 * n : 16 * n + 16, 0:128]
            ref[n, 16:32] = values[16 * n : 16 * n + 16, 128:256]
            ref[n, 32:40] = bias


def chip_kernel(keep_ref, got_ref, out_ref):
    out_ref[...] = keep_ref[...] + got_ref[...]


def plane_kernel(parts_ref, out_ref):
    total = jnp.sum(parts_ref[...], axis=0)
    for n in range(8):
        out_ref[n] = total


def line_kernel(parts_ref, out_ref, extra_ref):
    total = jnp.sum(parts_ref[...], axis=0)
    extra_ref[...] = total[32:40]
    for n in range(16):
        out_ref[n] = total[0:32]


def last_kernel(parity_ref, own_ref, other_ref, extra_ref, in_ref, b_in_ref, out_ref, b_out_ref, loss_ref):
    even = parity_ref[0] == 0
    own, other = own_ref[...], other_ref[...]
    first = jnp.where(even, own, other)
    second = jnp.where(even, other, own)
    bias = extra_ref[0:4]
    squares = jnp.sum(first * first + second * second, axis=0)
    total = jnp.sum(squares, keepdims=True) + jnp.sum(bias * bias, keepdims=True)
    scale = lax.rsqrt(total / PARAMS + TINY)
    for ref, values in ((in_ref, first * scale), (out_ref, second * scale)):
        for n in range(16):
            ref[16 * n : 16 * n + 16, 0:128] = values[n, 0:16]
            ref[16 * n : 16 * n + 16, 128:256] = values[n, 16:32]
    bias = bias * scale
    for row, ref in ((0, b_in_ref), (2, b_out_ref)):
        ref[:, 0:128] = bias[row : row + 1]
        ref[:, 128:256] = bias[row + 1 : row + 2]
    loss_ref[...] = jnp.sum(extra_ref[4:5], keepdims=True) * (0.5 / COUNT)


IN_CHIP = [(n, n ^ 1) for n in range(DEVICES)]
CROSS = [(n, (n - 1) % DEVICES if n % 2 == 0 else (n + 1) % DEVICES) for n in range(DEVICES)]


def exchange(in_chip, cross):
    return lax.ppermute(in_chip, AXES, IN_CHIP), lax.ppermute(cross, AXES, CROSS)


def local(state, target, w_in, b_in, w_out, b_out, nbr, send):
    parity = lax.axis_index("core").reshape(1)
    inner, leave, lift = operators()
    fixed = np.concatenate([*halves(inner), leave, lift.T], axis=0).astype(ml_dtypes.bfloat16)
    b_in, b_out = b_in.reshape(1, 256), b_out.reshape(1, 256)
    tall, flat, thin = ((512, 256), BF16), ((64, 256), BF16), ((256, 64), BF16)
    arrival = ((2, 64, 256), BF16)
    arrived, hidden_first, *edge, w_in2, w_out2, state, nbr, inner2, leave1, lift1, lift_t = call(
        first_kernel,
        [arrival, SQUARE, ((40, 256), F32), ((40, 256), F32), PAIR, PAIR, SQUARE, ((6, 256), jnp.int32)]
        + [tall, flat, thin, flat],
        parity, state, w_in, nbr, jnp.asarray(fixed), b_in, w_out, b_out, send,
        name="first", micros=1.5,
        far=range(1, 9),
        limit=52.25,
        scratch=[
            pltpu.VMEM((256, 256), F32), pltpu.VMEM((1, 256), F32), pltpu.VMEM((256, 256), F32),
            pltpu.VMEM((1, 256), F32), pltpu.VMEM((2, 256), jnp.int32), pltpu.VMEM((4, 256, 256), BF16),
            pltpu.SemaphoreType.DMA((10,)),
        ],
    )
    got = exchange(*edge)
    base, w_in_t, w_out_t, inner_t, leave_t, near, far, eff, copy, b_in2, b_out2 = call(
        tables_kernel,
        [SQUARE, PAIR, PAIR, tall, thin, ((4, 256, 256), BF16), PAIR, ((2, 256, 48), BF16), SQUARE] + [((256, 128), F32)] * 2,
        w_in2, b_in, w_out2, b_out, inner2, leave1, lift1, nbr, state, arrived, hidden_first, got[0],
        name="tables", micros=1,
    )
    beside = exchange(copy, copy)
    network = (w_in2, b_in2, w_out2, b_out2, inner2, leave1, lift1, near)
    back = (w_in_t, inner_t, leave_t, lift_t)
    edge_shapes = [((32, 256), F32)] * 2
    second, third, hidden_second, hidden_third, arrived, link, *edge, _ = call(
        middle_kernel,
        [SQUARE] * 4 + [arrival, PAIR] + edge_shapes + [SQUARE],
        parity, base, state, *got, far, *network, name="middle", micros=2.4,
    )
    got = exchange(*edge)
    (base,) = call(rest_kernel, [SQUARE], third, hidden_third, arrived, *network, name="rest", micros=0.6)
    final, loss, fourth, hidden_fourth, adjoint, delta, gathered, *edge, _, _ = call(
        turn_kernel,
        [SQUARE, EXTRA] + [SQUARE] * 4 + [arrival] + edge_shapes + [SQUARE, arrival],
        parity, base, third, *got, link, target, *network, w_in_t, w_out_t, inner_t, leave_t, lift_t,
        name="turn", micros=3,
    )
    got = exchange(*edge)
    base, *grads, in_chip_hidden, cross_hidden = call(
        beside_kernel,
        [SQUARE, SQUARE, SQUARE, EXTRA, SQUARE, SQUARE],
        adjoint, delta, gathered, fourth, hidden_fourth, *beside, w_in2, b_in2, *back, near,
        name="beside", micros=1.3,
    )
    keep, give, *_ = call(
        back_kernel,
        [PACKED] * 2 + [SQUARE] * 3,
        parity, base, adjoint, *got, link, third, hidden_third, second, hidden_second, state, hidden_first,
        *beside, in_chip_hidden, cross_hidden, near, w_in_t, w_out_t, inner_t, leave_t, lift_t, eff, *grads, loss,
        name="back", micros=4.5,
    )
    swap = [(0, 1), (1, 0)]
    (parts,) = call(chip_kernel, [PACKED], keep, lax.ppermute(give, "core", swap), name="chip_sum", micros=0.3)
    parts = lax.all_to_all(parts, PLANE, 0, 0, tiled=True)
    (parts,) = call(plane_kernel, [((8, 40, 128), F32)], parts, name="plane_sum", micros=0.3)
    parts = lax.all_to_all(parts, "z", 0, 0, tiled=True)
    parts, extra = call(line_kernel, [((16, 32, 128), F32), EXTRA], parts, name="line_sum", micros=0.3)
    own = lax.all_to_all(parts, PLANE, 0, 0, tiled=True)
    other = lax.ppermute(own, "core", swap)
    row = ((1, 256), F32)
    step_in, step_b_in, step_out, step_b_out, loss = call(
        last_kernel, [SQUARE, row, SQUARE, row, ((1, 1), F32)], parity, own, other, extra, name="scale", micros=1
    )
    return final, loss.reshape(()), step_in, step_b_in.reshape(256), step_out, step_b_out.reshape(256)


def solution(mesh):
    split_mesh = Mesh(mesh.devices.reshape(SIZES), AXES)
    whole = P(None, AXES)
    return jax.shard_map(
        local,
        mesh=split_mesh,
        in_specs=(whole, whole, P(), P(), P(), P(), whole, whole),
        out_specs=(whole, P(), P(), P(), P(), P()),
        check_vma=False,
    )
```

```python
import jax
import jax.numpy as jnp
import ml_dtypes
import numpy as np
from jax import lax
from jax.experimental import pallas as pl
from jax.experimental.pallas import tpu as pltpu
from jax.sharding import Mesh, PartitionSpec as P

AXES = ("x", "y", "z", "core")
PLANE = ("x", "y")
SIZES = (4, 4, 8, 2)
DEVICES = 256
WIDTH = 256
COUNT = 16777216.0
PARAMS = 131584.0
TIME_STEP = 0.05
HALF_STEP = 0.025
TINY = 1e-20
F32 = jnp.float32
BF16 = jnp.bfloat16


def face_rows(face):
    layer = 0 if face % 2 == 0 else 3
    grid = np.arange(64).reshape(4, 4, 4)
    return np.take(grid, layer, axis=face // 2).reshape(16)


def operators():
    points = np.array([-1.0, -1.0 / np.sqrt(5.0), 1.0 / np.sqrt(5.0), 1.0])
    bary = np.array(
        [1.0 / np.prod([points[m] - points[n] for n in range(4) if n != m]) for m in range(4)]
    )
    deriv = np.zeros((4, 4))
    for m in range(4):
        for n in range(4):
            if m != n:
                deriv[m, n] = bary[n] / bary[m] / (points[m] - points[n])
        deriv[m, m] = -np.sum(deriv[m])
    eye = np.eye(4)
    tables = [
        np.kron(np.kron(deriv, eye), eye),
        np.kron(np.kron(eye, deriv), eye),
        np.kron(eye, np.kron(eye, deriv)),
    ]
    inner = np.zeros((256, 256))
    for a in range(3):
        inner[0:64, 64 * (a + 1) : 64 * (a + 2)] -= tables[a]
        inner[64 * (a + 1) : 64 * (a + 2), 0:64] -= tables[a]
    for face in range(6):
        sign = 2.0 * (face % 2) - 1.0
        for row in face_rows(face):
            speed = 64 * (face // 2 + 1) + row
            inner[row, row] -= 3.0
            inner[row, speed] += 3.0 * sign
            inner[speed, speed] -= 3.0
            inner[speed, row] += 3.0 * sign
    leave = np.zeros((64, 256))
    lift = np.zeros((256, 64))
    for face in range(2, 6):
        sign = 2.0 * (face % 2) - 1.0
        base = 16 * (face - 2)
        for n, row in enumerate(face_rows(face ^ 1)):
            leave[base + n, row] = 3.0
            leave[base + n, 64 * (face // 2 + 1) + row] = -3.0 * sign
        for n, row in enumerate(face_rows(face)):
            lift[row, base + n] = 1.0
            lift[64 * (face // 2 + 1) + row, base + n] = -sign
    return inner, leave, lift


def halves(values):
    high = values.astype(ml_dtypes.bfloat16)
    low = (values - high.astype(np.float64)).astype(ml_dtypes.bfloat16)
    return high, low


def split(values):
    high = values.astype(BF16)
    return high, (values - high.astype(F32)).astype(BF16)


def mm(left, right):
    return jnp.dot(left, right, preferred_element_type=F32)


def mm_nt(left, right):
    return lax.dot_general(left, right, (((1,), (1,)), ((), ())), preferred_element_type=F32)


def mm3(left, right, dot=mm):
    return dot(left[0], right[0]) + (dot(left[0], right[1]) + dot(left[1], right[0]))


def pair(ref):
    if len(ref.shape) == 2:
        return ref[0:256], ref[256:512]
    return ref[0], ref[1]


def call(body, outs, *args, name, micros, far=(), scratch=(), limit=24, reads=1000000):
    def space(n, value):
        if value.shape == (1,):
            return pltpu.SMEM
        return pltpu.HBM if n in far else pltpu.VMEM

    return list(pl.pallas_call(
        body,
        out_shape=[jax.ShapeDtypeStruct(s, t) for s, t in outs],
        in_specs=[pl.BlockSpec(memory_space=space(n, a)) for n, a in enumerate(args)],
        out_specs=[pl.BlockSpec(memory_space=pltpu.VMEM)] * len(outs),
        scratch_shapes=scratch,
        cost_estimate=pl.CostEstimate(flops=int(micros * 1.15e9), bytes_accessed=reads, transcendentals=0),
        compiler_params=pltpu.CompilerParams(vmem_limit_bytes=int(limit * 1048576)),
        name=name,
    )(*args))


SQUARE = ((256, 256), F32)
PAIR = ((2, 256, 256), BF16)
EXTRA = ((8, 128), F32)
PACKED = ((16, 40, 128), F32)


def edges(values):
    return values[0:16], values[48:64], values[64:80], values[112:128]


def edge_rows(values):
    return jnp.concatenate(edges(values), axis=0)


def leaving(edge):
    return 3.0 * (edge[16:32] + edge[48:64]), 3.0 * (edge[0:16] - edge[32:48])


def put(parity, upward, downward, in_chip_ref, cross_ref, rows=0):
    even = parity == 0
    in_chip_ref[rows : rows + 16] = jnp.where(even, upward, downward)
    cross_ref[rows : rows + 16] = jnp.where(even, downward, upward)


def take(parity, in_chip, cross):
    even = parity == 0
    return jnp.where(even, cross, in_chip), jnp.where(even, in_chip, cross)


def pick(values, table, dot=mm):
    both = dot(jnp.concatenate(split(values), axis=0), table)
    return both[0:16] + both[16:32]


def add_edges(values_ref, first, second, third, fourth):
    values_ref[0:16] += first
    values_ref[48:64] += second
    values_ref[64:80] += third
    values_ref[112:128] += fourth


def one_hot(rows, column):
    return (rows == column).astype(F32).astype(BF16)


def make_near(small_ref, near):
    rows = lax.broadcasted_iota(jnp.int32, (256, 256), 0).astype(F32)
    for face in range(2, 6):
        near[face - 2] = one_hot(rows, small_ref[face : face + 1] - 256.0 * (face ^ 1))


def first_kernel(
    parity_ref, state_far, w_in_far, fixed_far, w_out_far, small_ref,
    arrived_ref, hidden_ref, in_chip_ref, cross_ref, w_in, state_ref,
    w_in_ref, w_out_ref, fixed, near, sems,
):
    pairs = (
        (state_far, state_ref), (w_in_far, w_in_ref), (fixed_far.at[0:256], fixed), (w_out_far.at[0:16], w_out_ref.at[0:16]),
        (w_out_far.at[48:80], w_out_ref.at[16:48]), (w_out_far.at[112:128], w_out_ref.at[48:64]),
    )
    copies = [pltpu.make_async_copy(s, t, sems.at[n]) for n, (s, t) in enumerate(pairs)]
    for copy in copies:
        copy.start()
    make_near(small_ref, near)
    bias = wide(small_ref.at[8:9])
    copies[0].wait()
    values = state_ref[...]
    edge = edge_rows(values)
    parts = split(values)
    parity = parity_ref[0]
    put(parity, *leaving(edge), in_chip_ref, cross_ref)
    copies[1].wait()
    w_in[0], w_in[1] = split(w_in_ref[...])
    hidden = jnp.tanh(mm3(pair(w_in), parts) + bias)
    hidden_ref[...] = hidden
    for copy in copies[2:]:
        copy.wait()
    arrive_near(mm(fixed[128:192], parts[0]) + mm(fixed[128:192], parts[1]), near, arrived_ref)
    rates = mm3((fixed[0:64], fixed[64:128]), parts) + mm3(split(w_out_ref[...]), split(hidden))
    lift = fixed[192:256, 0:64]
    rates += mm(lift, arrived_ref[0]) + mm(lift, arrived_ref[1])
    put(parity, *leaving(edge + TIME_STEP * rates), in_chip_ref, cross_ref, 16)
    down_index = small_ref[6:7]
    up_index = small_ref[7:8] - 256.0
    even = parity == 0
    in_chip_ref[32:40] = jnp.broadcast_to(jnp.where(even, up_index, down_index), (8, 256))
    cross_ref[32:40] = jnp.broadcast_to(jnp.where(even, down_index, up_index), (8, 256))


def flip(values):
    return values.astype(F32).T.astype(BF16)


def forward_pairs(turned):
    return jnp.concatenate([turned[0:16] + turned[64:80], turned[48:64] - turned[112:128]], axis=0)


def backward_pairs(turned):
    return jnp.concatenate([turned[0:16] - turned[64:80], turned[48:64] + turned[112:128]], axis=0)


def deep(rows):
    high, low = split(rows.T)
    return jnp.concatenate([high, high, low], axis=1)


def tables_kernel(
    w_in, w_out_ref, inner, leave, lift_t, small_ref, state_ref, arrived_ref, hidden_ref, after_ref,
    next_ref, sum_ref, linear_ref, out_ref, w_out, in_t_ref, out_t_ref, inner_t, leave_t, lift,
    near, far_ref, column_in, column_out, in_deep, inner_deep, leave_deep, out_deep, inner_t_deep, lift_t_deep, eff_ref,
):
    b_in, b_out = small_ref.at[8:9], small_ref.at[9:10]
    column_in[...] = column(b_in)
    column_out[...] = column(b_out)
    second = w_out_ref[...]
    w_out[0], w_out[1] = split(second)
    lift[...] = flip(lift_t[...])
    leave_t[...] = flip(leave[...])
    values = state_ref[...]
    network = (w_in, column_in, w_out, column_out, inner, leave, lift, near)
    rates = full_rates(split(values), split(hidden_ref[...]), network, arrived_ref)
    base = values + TIME_STEP * rates
    next_ref[...] = base
    sum_ref[...], linear_ref[...], out_ref[...] = prepare(split(base), network)
    make_near(small_ref, near)
    rows = lax.broadcasted_iota(jnp.int32, (256, 256), 0).astype(F32)
    for face in range(2):
        far_ref[face] = one_hot(rows, small_ref[face : face + 1] - (1536.0 + 256.0 * face))
    for part in range(2):
        in_t_ref[part] = flip(w_in[part])
        out_t_ref[part] = flip(w_out[part])
        inner_t[256 * part : 256 * part + 256] = flip(inner[256 * part : 256 * part + 256])
    whole = lambda values: values[0].astype(F32) + values[1].astype(F32)
    in_deep[...] = deep(TIME_STEP * forward_pairs(whole(pair(in_t_ref))))
    inner_deep[...] = deep(TIME_STEP * forward_pairs(whole(pair(inner_t))))
    leave_deep[...] = deep(TIME_STEP * forward_pairs(leave_t[...].astype(F32)))
    weight = 3.0 * TIME_STEP
    out_deep[...] = deep(weight * backward_pairs(second))
    inner_t_deep[...] = deep(weight * backward_pairs(whole(pair(inner))))
    lift_t_deep[...] = deep(weight * backward_pairs(lift[...].astype(F32)))
    seen = backward_pairs(second)
    eff_ref[0] = deep(seen[16:32])
    eff_ref[1] = deep(seen[0:16])


def column(row):
    return jnp.broadcast_to(row[...], (128, 256)).T


def wide(bias):
    values = column(bias) if bias.shape[0] == 1 else bias[...]
    return jnp.concatenate([values, values], axis=1)


def gather(high, low, near, dot):
    for n in range(4):
        both = jnp.concatenate([high[16 * n : 16 * n + 16], low[16 * n : 16 * n + 16]], axis=0)
        yield dot(both, near[n])


def arrive_near(out, near, arrived_ref):
    high, low = split(out)
    for n, both in enumerate(gather(high, low, near, mm)):
        both = both.astype(BF16)
        arrived_ref[0, 16 * n : 16 * n + 16] = both[0:16]
        arrived_ref[1, 16 * n : 16 * n + 16] = both[16:32]


def prepare(parts, network):
    w_in, b_in, w_out, b_out, inner, leave, lift, near = network
    out = mm(leave[...], parts[0]) + mm(leave[...], parts[1])
    return mm3(pair(w_in), parts) + wide(b_in), mm3(pair(inner), parts) + wide(b_out), out


def full_rates(parts, hidden_parts, network, arrived_ref):
    w_in, b_in, w_out, b_out, inner, leave, lift, near = network
    rates = mm3(pair(inner), parts) + wide(b_out)
    rates += mm(lift[...], arrived_ref[0]) + mm(lift[...], arrived_ref[1])
    return rates + mm3(pair(w_out), hidden_parts)


def edge_rates(parts, hidden_parts, network, arrived_ref):
    w_in, b_in, w_out, b_out, inner, leave, lift, near = network
    rates = mm3([edge_rows(x) for x in pair(inner)], parts) + edge_rows(wide(b_out))
    rates += mm(edge_rows(lift), arrived_ref[0]) + mm(edge_rows(lift), arrived_ref[1])
    return rates + mm3([edge_rows(x) for x in pair(w_out)], hidden_parts)


def pick_parts(below, above, link):
    low = mm(jnp.concatenate(split(below), axis=0), link[0])
    high = mm(jnp.concatenate(split(above), axis=0), link[1])
    return low, high


def stack(low, high):
    top = jnp.concatenate([low[0:16], high[0:16]], axis=0).astype(BF16)
    rest = jnp.concatenate([low[16:32], high[16:32]], axis=0).astype(BF16)
    return jnp.concatenate([top, rest, top], axis=0)


def add_arrived(weight, base_ref, low, high, now_ref):
    low = weight * (low[0:16] + low[16:32])
    high = weight * (high[0:16] + high[16:32])
    now_ref[...] = base_ref[...]
    add_edges(now_ref, low, high, low, -high)
    return now_ref[...]


def prepared_rates(stacked, prepared, deeps, network, hidden_ref, arrived_ref):
    total, linear, out = (ref[...] + mm(d[...], stacked) for ref, d in zip(prepared, deeps))
    hidden = jnp.tanh(total)
    hidden_ref[...] = hidden
    lift, near, w_out = network[6], network[7], network[2]
    arrive_near(out, near, arrived_ref)
    linear += mm(lift[...], arrived_ref[0]) + mm(lift[...], arrived_ref[1])
    return linear + mm3(pair(w_out), split(hidden))


def middle_kernel(
    parity_ref, base_ref, state_ref, in_chip, cross, far_ref, sum_ref, linear_ref, out_ref, in_deep, inner_deep, leave_deep,
    w_in, b_in, w_out, b_out, inner, leave, lift, near,
    second_ref, third_ref, hidden_second, hidden_third, arrived_ref, link, in_chip_out, cross_out, between,
):
    network = (w_in, b_in, w_out, b_out, inner, leave, lift, near)
    parity = parity_ref[0]
    below, above = take(parity, in_chip[...], cross[...])
    rows = lax.broadcasted_iota(jnp.int32, (256, 256), 0).astype(F32)
    for side, received in enumerate((below, above)):
        link[side] = mm(one_hot(rows, received[32:33]), far_ref[side]).astype(BF16)
    low, high = pick_parts(below[0:16], above[0:16], link)
    rates = prepared_rates(
        stack(low, high), (sum_ref, linear_ref, out_ref), (in_deep, inner_deep, leave_deep),
        network, hidden_second, arrived_ref,
    )
    values = add_arrived(TIME_STEP, base_ref, low, high, second_ref)
    between[...] = 0.5 * (state_ref[...] + values) + HALF_STEP * rates
    put(parity, *leaving(edge_rows(between)), in_chip_out, cross_out)
    up_bias, down_bias = leaving(TIME_STEP * edge_rows(wide(b_out)))
    low, high = pick_parts(below[16:32] + up_bias, above[16:32] + down_bias, link)
    values = add_arrived(HALF_STEP, between, low, high, third_ref)
    parts = split(values)
    hidden = jnp.tanh(mm3(pair(w_in), parts) + wide(b_in))
    hidden_third[...] = hidden
    arrive_near(mm(leave[...], parts[0]) + mm(leave[...], parts[1]), near, arrived_ref)
    rates = edge_rates(parts, split(hidden), network, arrived_ref)
    put(parity, *leaving(edge_rows(values) + TIME_STEP * rates), in_chip_out, cross_out, 16)


def rest_kernel(
    third_ref, hidden_ref, arrived_ref, state_ref, w_in, b_in, w_out, b_out, inner, leave, lift, near,
    next_ref, sum_ref, linear_ref, out_ref, copy_ref,
):
    copy_ref[...] = state_ref[...]
    network = (w_in, b_in, w_out, b_out, inner, leave, lift, near)
    values = third_ref[...]
    base = values + TIME_STEP * full_rates(split(values), split(hidden_ref[...]), network, arrived_ref)
    next_ref[...] = base
    sum_ref[...], linear_ref[...], out_ref[...] = prepare(split(base), network)


def sensitivities(edge, link):
    upward = pick(edge[16:32] - edge[48:64], link[1], mm_nt)
    return upward, pick(edge[0:16] + edge[32:48], link[0], mm_nt)


def through_closure(parts, hidden, w_out_t):
    return (1.0 - hidden * hidden) * mm3(w_out_t, parts)


def gather_back(parts, lift_t, near):
    high, low = split(mm(lift_t[...], parts[0]) + mm(lift_t[...], parts[1]))
    return split(jnp.concatenate([a[0:16] + a[16:32] for a in gather(high, low, near, mm_nt)], axis=0))


def back_rates(parts, delta_parts, network, gathered, rows=lambda values: values[...]):
    w_in_t, inner_t, leave_t, lift_t, near = network
    rates = mm3([rows(x) for x in pair(inner_t)], parts) + mm3([rows(x) for x in pair(w_in_t)], delta_parts)
    return rates + (mm(rows(leave_t), gathered[0]) + mm(rows(leave_t), gathered[1]))


def turn_kernel(
    parity_ref, base_ref, third_ref, in_chip, cross, link, target_ref,
    sum_ref, linear_ref, out_ref, in_deep, inner_deep, leave_deep,
    w_in, b_in, w_out, b_out, inner, leave, lift, near, w_in_t, w_out_t, inner_t, leave_t, lift_t,
    final_ref, loss_ref, fourth_ref, hidden_ref, adjoint_ref, delta_ref, gathered_ref, in_chip_out, cross_out,
    between, arrived_ref,
):
    network = (w_in, b_in, w_out, b_out, inner, leave, lift, near)
    parity = parity_ref[0]
    below, above = take(parity, in_chip[...], cross[...])
    low, high = pick_parts(below[0:16], above[0:16], link)
    rates = prepared_rates(
        stack(low, high), (sum_ref, linear_ref, out_ref), (in_deep, inner_deep, leave_deep),
        network, hidden_ref, arrived_ref,
    )
    values = add_arrived(TIME_STEP, base_ref, low, high, fourth_ref)
    between[...] = 0.5 * (third_ref[...] + values) + HALF_STEP * rates
    low, high = pick_parts(below[16:32], above[16:32], link)
    final = add_arrived(HALF_STEP, between, low, high, final_ref)
    mismatch = final - target_ref[...]
    adjoint = (HALF_STEP / COUNT) * mismatch
    adjoint_ref[...] = adjoint
    squares = jnp.sum(mismatch * mismatch, axis=0, keepdims=True)
    loss_ref[...] = jnp.broadcast_to(squares[:, 0:128] + squares[:, 128:256], (8, 128))
    edge = edge_rows(adjoint)
    put(parity, *sensitivities(edge, link), in_chip_out, cross_out)
    parts = split(adjoint)
    delta = through_closure(parts, hidden_ref[...], pair(w_out_t))
    delta_ref[...] = delta
    gathered = gather_back(parts, lift_t, near)
    gathered_ref[0], gathered_ref[1] = gathered
    back = (w_in_t, inner_t, leave_t, lift_t, near)
    rates = back_rates(parts, split(delta), back, gathered, edge_rows)
    put(parity, *sensitivities(edge + TIME_STEP * rates, link), in_chip_out, cross_out, 16)


def bias_rows(first, second):
    rows = lax.broadcasted_iota(jnp.int32, (8, 128), 0)
    bias = jnp.where(rows == 0, first[:, 0:128], jnp.where(rows == 1, first[:, 128:256], 0.0))
    bias = jnp.where(rows == 2, second[:, 0:128], bias)
    if second.shape[1] == 256:
        bias = jnp.where(rows == 3, second[:, 128:256], bias)
    return bias


def row_sums(parts):
    ones = jnp.ones((8, 256), BF16)
    return mm_nt(ones, parts[0]) + mm_nt(ones, parts[1])


def gradients(parts, delta_parts, state, hidden):
    bias = bias_rows(row_sums(delta_parts), row_sums(parts))
    return mm3(delta_parts, split(state), mm_nt), mm3(parts, split(hidden), mm_nt), bias


def beside_kernel(
    adjoint_ref, delta_ref, gathered_ref, state_ref, hidden_ref, in_chip, cross, w_in, b_in,
    w_in_t, inner_t, leave_t, lift_t, near, w_out_t, hidden_third,
    next_ref, grad_in, grad_out, extra, in_chip_hidden, cross_hidden, back_ref, linear_ref, out_ref,
):
    adjoint = adjoint_ref[...]
    parts, delta_parts = split(adjoint), split(delta_ref[...])
    gathered = gathered_ref[0], gathered_ref[1]
    base = adjoint + TIME_STEP * back_rates(parts, delta_parts, (w_in_t, inner_t, leave_t, lift_t, near), gathered)
    next_ref[...] = base
    base_parts = split(base)
    back_ref[...] = mm3(pair(w_out_t), base_parts)
    linear_ref[...] = mm3(pair(inner_t), base_parts)
    out_ref[...] = mm(lift_t[...], base_parts[0]) + mm(lift_t[...], base_parts[1])
    first, second, bias = gradients(parts, delta_parts, state_ref[...], hidden_ref[...])
    grad_in[...] = first
    grad_out[...] = second + mm3(base_parts, split(hidden_third[...]), mm_nt)
    extra[...] = bias
    for source, ref in ((in_chip, in_chip_hidden), (cross, cross_hidden)):
        ref[...] = jnp.tanh(mm3(pair(w_in), split(source[...])) + wide(b_in))


def back_kernel(
    parity_ref, base_ref, adjoint_ref, in_chip, cross, link,
    third_ref, hidden_third, second_ref, hidden_second, state_ref, hidden_first,
    in_chip_state, cross_state, in_chip_hidden, cross_hidden,
    near, w_in_t, w_out_t, inner_t, leave_t, lift_t, eff, back_ref, linear_ref, out_ref, out_deep, inner_t_deep, lift_t_deep,
    old_in, old_out, old_extra, loss_ref,
    keep_ref, send_ref, now_ref, between, sum_ref,
):
    network = (w_in_t, inner_t, leave_t, lift_t, near)
    parity = parity_ref[0]
    even = parity == 0
    below, above = take(parity, in_chip[...], cross[...])
    totals = [old_in[...], old_out[...], old_extra[...]]

    def arrive(source_ref, weight, low, high):
        now_ref[...] = source_ref[...]
        low, high = weight * low, weight * high
        add_edges(now_ref, low, high, -low, high)
        return now_ref[...]

    def collect(*args):
        for n, term in enumerate(gradients(*args)):
            totals[n] = totals[n] + term

    received = below[0:16], above[0:16]
    high_parts, low_parts = zip(*(split(x) for x in received))
    top, rest = jnp.concatenate(high_parts, axis=0), jnp.concatenate(low_parts, axis=0)
    stacked = jnp.concatenate([top, rest, top], axis=0)
    hidden = hidden_third[...]
    delta_full = (1.0 - hidden * hidden) * (back_ref[...] + mm(out_deep[...], stacked))
    delta = split(delta_full)
    high, low = split(out_ref[...] + mm(lift_t_deep[...], stacked))
    gathered = split(jnp.concatenate([a[0:16] + a[16:32] for a in gather(high, low, near, mm_nt)], axis=0))
    rates = linear_ref[...] + mm(inner_t_deep[...], stacked) + mm3(pair(w_in_t), delta)
    rates += mm(leave_t[...], gathered[0]) + mm(leave_t[...], gathered[1])
    values = arrive(base_ref, 3.0 * TIME_STEP, *received)
    between[...] = 0.5 * (adjoint_ref[...] + values) + HALF_STEP * rates
    totals[0] = totals[0] + mm3(delta, split(third_ref[...]), mm_nt)
    totals[2] = totals[2] + bias_rows(row_sums(delta), row_sums(split(values)))
    weight = 3.0 * TIME_STEP
    hidden_parts = split(hidden)
    early = [weight * mm3((h, l), hidden_parts, mm_nt) for h, l in zip(high_parts, low_parts)]
    upward, downward = sensitivities(edge_rows(between), link)

    values = arrive(between, 3.0 * HALF_STEP, below[16:32], above[16:32])
    parts = split(values)
    delta = split(through_closure(parts, hidden_second[...], pair(w_out_t)))
    values = values + TIME_STEP * back_rates(parts, delta, network, gather_back(parts, lift_t, near))
    collect(parts, delta, second_ref[...], hidden_second[...])

    states = take(parity, in_chip_state[...], cross_state[...])
    hiddens = take(parity, in_chip_hidden[...], cross_hidden[...])
    blocks = []
    for side, received in enumerate((weight * downward, weight * upward)):
        high, low = split(received)
        hidden = hiddens[side]
        seen = mm(eff[side], jnp.concatenate([high, low, high], axis=0))
        delta = split((1.0 - hidden * hidden) * seen)
        totals[0] = totals[0] + mm3(delta, split(states[side]), mm_nt)
        blocks.append(mm3((high, low), split(hidden), mm_nt))
        none = jnp.zeros((48, 256), F32)
        spread = [none, received, none, received] if side == 0 else [received, none, -received, none]
        totals[2] = totals[2] + bias_rows(row_sums(delta), row_sums(split(jnp.concatenate(spread, axis=0))))

    parts = split(values)
    delta = split(through_closure(parts, hidden_first[...], pair(w_out_t)))
    collect(parts, delta, state_ref[...], hidden_first[...])
    sum_ref[...] = totals[1]
    low, high = blocks[1] + early[0], blocks[0] + early[1]
    add_edges(sum_ref, low, high, -low, high)
    first, second, bias = totals[0], sum_ref[...], totals[2]
    rows = lax.broadcasted_iota(jnp.int32, (8, 128), 0)
    bias = jnp.where(rows == 4, loss_ref[...], bias)
    for ref, values in ((keep_ref, jnp.where(even, first, second)), (send_ref, jnp.where(even, second, first))):
        for n in range(16):
            ref[n, 0:16] = values[16 * n : 16 * n + 16, 0:128]
            ref[n, 16:32] = values[16 * n : 16 * n + 16, 128:256]
            ref[n, 32:40] = bias


def chip_kernel(keep_ref, got_ref, out_ref):
    out_ref[...] = keep_ref[...] + got_ref[...]


def plane_kernel(parts_ref, out_ref):
    total = jnp.sum(parts_ref[...], axis=0)
    for n in range(8):
        out_ref[n] = total


def line_kernel(parts_ref, out_ref, extra_ref):
    total = jnp.sum(parts_ref[...], axis=0)
    extra_ref[...] = total[32:40]
    for n in range(16):
        out_ref[n] = total[0:32]


def last_kernel(parity_ref, own_ref, other_ref, extra_ref, in_ref, b_in_ref, out_ref, b_out_ref, loss_ref):
    even = parity_ref[0] == 0
    own, other = own_ref[...], other_ref[...]
    first = jnp.where(even, own, other)
    second = jnp.where(even, other, own)
    bias = extra_ref[0:4]
    squares = jnp.sum(first * first + second * second, axis=0)
    total = jnp.sum(squares, keepdims=True) + jnp.sum(bias * bias, keepdims=True)
    scale = lax.rsqrt(total / PARAMS + TINY)
    for ref, values in ((in_ref, first * scale), (out_ref, second * scale)):
        for n in range(16):
            ref[16 * n : 16 * n + 16, 0:128] = values[n, 0:16]
            ref[16 * n : 16 * n + 16, 128:256] = values[n, 16:32]
    bias = bias * scale
    for row, ref in ((0, b_in_ref), (2, b_out_ref)):
        ref[:, 0:128] = bias[row : row + 1]
        ref[:, 128:256] = bias[row + 1 : row + 2]
    loss_ref[...] = jnp.sum(extra_ref[4:5], keepdims=True) * (0.5 / COUNT)


IN_CHIP = [(n, n ^ 1) for n in range(DEVICES)]
CROSS = [(n, (n - 1) % DEVICES if n % 2 == 0 else (n + 1) % DEVICES) for n in range(DEVICES)]


def exchange(in_chip, cross):
    crossed = lax.ppermute(cross, AXES, CROSS)
    return lax.ppermute(in_chip, AXES, IN_CHIP), crossed


def local(state, target, w_in, b_in, w_out, b_out, nbr, send):
    parity = lax.axis_index("core").reshape(1)
    inner, leave, lift = operators()
    edge = np.concatenate([np.arange(0, 16), np.arange(48, 80), np.arange(112, 128)])
    fixed = np.zeros((768, 256))
    fixed[0:64], fixed[64:128] = (x[edge].astype(np.float64) for x in halves(inner))
    fixed[128:192], fixed[192:256, 0:64] = leave, lift[edge]
    to_bf16 = lambda values: jnp.asarray(values.astype(ml_dtypes.bfloat16))
    fixed, inner2, leave1, lift_t = (to_bf16(x) for x in (fixed, np.concatenate(halves(inner)), leave, lift.T))
    rows = ((0, nbr), (6, send), (8, b_in.reshape(1, 256)), (9, b_out.reshape(1, 256)))
    small = sum(jnp.pad(x.astype(F32), ((at, 16 - at - x.shape[0]), (0, 0))) for at, x in rows)
    tall, flat, thin = ((512, 256), BF16), ((64, 256), BF16), ((256, 64), BF16)
    arrival = ((2, 64, 256), BF16)
    arrived, hidden_first, *edge, w_in2, state = call(
        first_kernel,
        [arrival, SQUARE, ((40, 256), F32), ((40, 256), F32), PAIR, SQUARE],
        parity, state, w_in, fixed, w_out, small,
        name="first", micros=1.5,
        far=range(1, 5),
        limit=53,
        scratch=[
            pltpu.VMEM((256, 256), F32), pltpu.VMEM((64, 256), F32), pltpu.VMEM((256, 256), BF16),
            pltpu.VMEM((4, 256, 256), BF16), pltpu.SemaphoreType.DMA((6,)),
        ],
    )
    got = exchange(*edge)
    middle = [SQUARE, SQUARE, ((64, 256), F32)]
    depth, shallow = ((256, 96), BF16), ((64, 96), BF16)
    made = call(
        tables_kernel,
        [SQUARE, *middle, PAIR, PAIR, PAIR, tall, thin, thin, ((4, 256, 256), BF16), PAIR]
        + [((256, 128), F32)] * 2
        + [depth, depth, shallow] * 2
        + [((2, 256, 48), BF16)],
        w_in2, w_out, inner2, leave1, lift_t, small, state, arrived, hidden_first, edge[0],
        name="tables", micros=1.5,
    )
    base, prepared, deeps, eff = made[0], made[1:4], made[14:20], made[20]
    w_out2, w_in_t, w_out_t, inner_t, leave_t, lift1, near, far, b_in2, b_out2 = made[4:14]
    forward_deeps, backward_deeps = deeps[:3], deeps[3:]
    network = (w_in2, b_in2, w_out2, b_out2, inner2, leave1, lift1, near)
    back = (w_in_t, inner_t, leave_t, lift_t)
    edge_shapes = [((32, 256), F32)] * 2
    square = pltpu.VMEM((256, 256), F32)
    second, third, hidden_second, hidden_third, arrived, link, *edge = call(
        middle_kernel,
        [SQUARE] * 4 + [arrival, PAIR] + edge_shapes,
        parity, base, state, *got, far, *prepared, *forward_deeps, *network, name="middle", micros=2.1, scratch=[square],
    )
    got = exchange(*edge)
    base, *prepared, copy = call(
        rest_kernel, [SQUARE, *middle, SQUARE], third, hidden_third, arrived, state, *network, name="rest", micros=0.9
    )
    beside = exchange(copy, copy)
    final, loss, fourth, hidden_fourth, adjoint, delta, gathered, *edge = call(
        turn_kernel,
        [SQUARE, EXTRA] + [SQUARE] * 4 + [arrival] + edge_shapes,
        parity, base, third, *got, link, target, *prepared, *forward_deeps, *network,
        w_in_t, w_out_t, inner_t, leave_t, lift_t,
        name="turn", micros=2.5, scratch=[square, pltpu.VMEM((2, 64, 256), BF16)],
    )
    got = exchange(*edge)
    base, *grads, in_chip_hidden, cross_hidden, back_product, linear, out = call(
        beside_kernel,
        [SQUARE, SQUARE, SQUARE, EXTRA, SQUARE, SQUARE, *middle],
        adjoint, delta, gathered, fourth, hidden_fourth, *beside, w_in2, b_in2, *back, near, w_out_t, hidden_third,
        name="beside", micros=2,
    )
    keep, give = call(
        back_kernel,
        [PACKED] * 2,
        parity, base, adjoint, *got, link, third, hidden_third, second, hidden_second, state, hidden_first,
        *beside, in_chip_hidden, cross_hidden, near, w_in_t, w_out_t, inner_t, leave_t, lift_t, eff,
        back_product, linear, out, *backward_deeps, *grads, loss,
        name="back", micros=4, scratch=[square] * 3,
    )
    swap = [(0, 1), (1, 0)]
    (parts,) = call(chip_kernel, [PACKED], keep, lax.ppermute(give, "core", swap), name="chip_sum", micros=0.3)
    parts = lax.all_to_all(parts, PLANE, 0, 0, tiled=True)
    (parts,) = call(plane_kernel, [((8, 40, 128), F32)], parts, name="plane_sum", micros=0.3)
    parts = lax.all_to_all(parts, "z", 0, 0, tiled=True)
    parts, extra = call(line_kernel, [((16, 32, 128), F32), EXTRA], parts, name="line_sum", micros=0.3)
    own = lax.all_to_all(parts, PLANE, 0, 0, tiled=True)
    other = lax.ppermute(own, "core", swap)
    row = ((1, 256), F32)
    step_in, step_b_in, step_out, step_b_out, loss = call(
        last_kernel, [SQUARE, row, SQUARE, row, ((1, 1), F32)], parity, own, other, extra, name="scale", micros=1
    )
    return final, loss.reshape(()), step_in, step_b_in.reshape(256), step_out, step_b_out.reshape(256)


def solution(mesh):
    split_mesh = Mesh(mesh.devices.reshape(SIZES), AXES)
    whole = P(None, AXES)
    return jax.shard_map(
        local,
        mesh=split_mesh,
        in_specs=(whole, whole, P(), P(), P(), P(), whole, whole),
        out_specs=(whole, P(), P(), P(), P(), P()),
        check_vma=False,
    )
```

```python
import jax
import jax.numpy as jnp
import ml_dtypes
import numpy as np
from jax import lax
from jax.experimental import pallas as pl
from jax.experimental.pallas import tpu as pltpu
from jax.sharding import Mesh, PartitionSpec as P

AXES = ("x", "y", "z", "core")
PLANE = ("x", "y")
SIZES = (4, 4, 8, 2)
DEVICES = 256
WIDTH = 256
COUNT = 16777216.0
PARAMS = 131584.0
TIME_STEP = 0.05
HALF_STEP = 0.025
TINY = 1e-20
F32 = jnp.float32
BF16 = jnp.bfloat16


def face_rows(face):
    layer = 0 if face % 2 == 0 else 3
    grid = np.arange(64).reshape(4, 4, 4)
    return np.take(grid, layer, axis=face // 2).reshape(16)


def operators():
    points = np.array([-1.0, -1.0 / np.sqrt(5.0), 1.0 / np.sqrt(5.0), 1.0])
    bary = np.array(
        [1.0 / np.prod([points[m] - points[n] for n in range(4) if n != m]) for m in range(4)]
    )
    deriv = np.zeros((4, 4))
    for m in range(4):
        for n in range(4):
            if m != n:
                deriv[m, n] = bary[n] / bary[m] / (points[m] - points[n])
        deriv[m, m] = -np.sum(deriv[m])
    eye = np.eye(4)
    tables = [
        np.kron(np.kron(deriv, eye), eye),
        np.kron(np.kron(eye, deriv), eye),
        np.kron(eye, np.kron(eye, deriv)),
    ]
    inner = np.zeros((256, 256))
    for a in range(3):
        inner[0:64, 64 * (a + 1) : 64 * (a + 2)] -= tables[a]
        inner[64 * (a + 1) : 64 * (a + 2), 0:64] -= tables[a]
    for face in range(6):
        sign = 2.0 * (face % 2) - 1.0
        for row in face_rows(face):
            speed = 64 * (face // 2 + 1) + row
            inner[row, row] -= 3.0
            inner[row, speed] += 3.0 * sign
            inner[speed, speed] -= 3.0
            inner[speed, row] += 3.0 * sign
    leave = np.zeros((64, 256))
    lift = np.zeros((256, 64))
    for face in range(2, 6):
        sign = 2.0 * (face % 2) - 1.0
        base = 16 * (face - 2)
        for n, row in enumerate(face_rows(face ^ 1)):
            leave[base + n, row] = 3.0
            leave[base + n, 64 * (face // 2 + 1) + row] = -3.0 * sign
        for n, row in enumerate(face_rows(face)):
            lift[row, base + n] = 1.0
            lift[64 * (face // 2 + 1) + row, base + n] = -sign
    return inner, leave, lift


def halves(values):
    high = values.astype(ml_dtypes.bfloat16)
    low = (values - high.astype(np.float64)).astype(ml_dtypes.bfloat16)
    return high, low


def split(values):
    high = values.astype(BF16)
    return high, (values - high.astype(F32)).astype(BF16)


def mm(left, right):
    return jnp.dot(left, right, preferred_element_type=F32)


def mm_nt(left, right):
    return lax.dot_general(left, right, (((1,), (1,)), ((), ())), preferred_element_type=F32)


def mm3(left, right, dot=mm):
    return dot(left[0], right[0]) + (dot(left[0], right[1]) + dot(left[1], right[0]))


def pair(ref):
    if len(ref.shape) == 2:
        return ref[0:256], ref[256:512]
    return ref[0], ref[1]


def call(body, outs, *args, name, micros, far=(), scratch=(), limit=24, reads=1000000):
    def space(n, value):
        if value.shape == (1,):
            return pltpu.SMEM
        return pltpu.HBM if n in far else pltpu.VMEM

    return list(pl.pallas_call(
        body,
        out_shape=[jax.ShapeDtypeStruct(s, t) for s, t in outs],
        in_specs=[pl.BlockSpec(memory_space=space(n, a)) for n, a in enumerate(args)],
        out_specs=[pl.BlockSpec(memory_space=pltpu.VMEM)] * len(outs),
        scratch_shapes=scratch,
        cost_estimate=pl.CostEstimate(flops=int(micros * 1.15e9), bytes_accessed=reads, transcendentals=0),
        compiler_params=pltpu.CompilerParams(vmem_limit_bytes=int(limit * 1048576)),
        name=name,
    )(*args))


SQUARE = ((256, 256), F32)
PAIR = ((2, 256, 256), BF16)
EXTRA = ((8, 128), F32)
PACKED = ((16, 40, 128), F32)


def edges(values):
    return values[0:16], values[48:64], values[64:80], values[112:128]


def edge_rows(values):
    return jnp.concatenate(edges(values), axis=0)


def leaving(edge):
    return 3.0 * (edge[16:32] + edge[48:64]), 3.0 * (edge[0:16] - edge[32:48])


def put(parity, upward, downward, in_chip_ref, cross_ref, rows=0):
    even = parity == 0
    in_chip_ref[rows : rows + 16] = jnp.where(even, upward, downward)
    cross_ref[rows : rows + 16] = jnp.where(even, downward, upward)


def take(parity, in_chip, cross):
    even = parity == 0
    return jnp.where(even, cross, in_chip), jnp.where(even, in_chip, cross)


def pick(values, table, dot=mm):
    both = dot(jnp.concatenate(split(values), axis=0), table)
    return both[0:16] + both[16:32]


def add_edges(values_ref, first, second, third, fourth):
    values_ref[0:16] += first
    values_ref[48:64] += second
    values_ref[64:80] += third
    values_ref[112:128] += fourth


def one_hot(rows, column):
    return (rows == column).astype(F32).astype(BF16)


def make_near(index_ref, near):
    rows = lax.broadcasted_iota(jnp.int32, (256, 256), 0)
    for face in range(2, 6):
        near[face - 2] = one_hot(rows, index_ref[face : face + 1] - 256 * (face ^ 1))


def first_kernel(
    parity_ref, state_far, w_in_far, fixed_far, w_out_far, nbr_far, send_far, b_in_far,
    arrived_ref, hidden_ref, in_chip_ref, cross_ref, w_in, state_ref,
    w_in_ref, w_out_ref, fixed, near, nbr_ref, send_ref, b_in, sems,
):
    pairs = (
        (state_far, state_ref), (w_in_far, w_in_ref), (fixed_far.at[0:256], fixed), (w_out_far.at[0:16], w_out_ref.at[0:16]),
        (w_out_far.at[48:80], w_out_ref.at[16:48]), (w_out_far.at[112:128], w_out_ref.at[48:64]),
        (nbr_far, nbr_ref), (send_far, send_ref), (b_in_far, b_in),
    )
    copies = [pltpu.make_async_copy(s, t, sems.at[n]) for n, (s, t) in enumerate(pairs)]
    for copy in copies:
        copy.start()
    copies[0].wait()
    values = state_ref[...]
    edge = edge_rows(values)
    parts = split(values)
    parity = parity_ref[0]
    put(parity, *leaving(edge), in_chip_ref, cross_ref)
    copies[1].wait()
    w_in[0], w_in[1] = split(w_in_ref[...])
    copies[8].wait()
    bias = wide(b_in)
    hidden = jnp.tanh(mm3(pair(w_in), parts) + bias)
    hidden_ref[...] = hidden
    for copy in copies[2:8]:
        copy.wait()
    make_near(nbr_ref, near)
    arrive_near(mm(fixed[128:192], parts[0]) + mm(fixed[128:192], parts[1]), near, arrived_ref)
    rates = mm3((fixed[0:64], fixed[64:128]), parts) + mm3(split(w_out_ref[...]), split(hidden))
    lift = fixed[192:256, 0:64]
    rates += mm(lift, arrived_ref[0]) + mm(lift, arrived_ref[1])
    put(parity, *leaving(edge + TIME_STEP * rates), in_chip_ref, cross_ref, 16)
    down_index = send_ref[0:1].astype(F32)
    up_index = (send_ref[1:2] - 256).astype(F32)
    even = parity == 0
    in_chip_ref[32:40] = jnp.broadcast_to(jnp.where(even, up_index, down_index), (8, 256))
    cross_ref[32:40] = jnp.broadcast_to(jnp.where(even, down_index, up_index), (8, 256))


def flip(values):
    return values.astype(F32).T.astype(BF16)


def forward_pairs(turned):
    return jnp.concatenate([turned[0:16] + turned[64:80], turned[48:64] - turned[112:128]], axis=0)


def backward_pairs(turned):
    return jnp.concatenate([turned[0:16] - turned[64:80], turned[48:64] + turned[112:128]], axis=0)


def deep(rows):
    high, low = split(rows.T)
    return jnp.concatenate([high, high, low], axis=1)


def tables_kernel(
    w_in, w_out_ref, inner, leave, lift_t, nbr_ref, b_in, b_out, state_ref, arrived_ref, hidden_ref, after_ref,
    next_ref, sum_ref, linear_ref, out_ref, w_out, in_t_ref, out_t_ref, inner_t, leave_t, lift,
    near, far_ref, column_in, column_out, in_deep, inner_deep, leave_deep, out_deep, inner_t_deep, lift_t_deep, eff_ref,
):
    column_in[...] = column(b_in)
    column_out[...] = column(b_out)
    second = w_out_ref[...]
    w_out[0], w_out[1] = split(second)
    lift[...] = flip(lift_t[...])
    leave_t[...] = flip(leave[...])
    values = state_ref[...]
    network = (w_in, column_in, w_out, column_out, inner, leave, lift, near)
    rates = full_rates(split(values), split(hidden_ref[...]), network, arrived_ref)
    base = values + TIME_STEP * rates
    next_ref[...] = base
    sum_ref[...], linear_ref[...], out_ref[...] = prepare(split(base), network)
    make_near(nbr_ref, near)
    rows = lax.broadcasted_iota(jnp.int32, (256, 256), 0)
    for face in range(2):
        far_ref[face] = one_hot(rows, nbr_ref[face : face + 1] - (1536 + 256 * face))
    for part in range(2):
        in_t_ref[part] = flip(w_in[part])
        out_t_ref[part] = flip(w_out[part])
        inner_t[256 * part : 256 * part + 256] = flip(inner[256 * part : 256 * part + 256])
    whole = lambda values: values[0].astype(F32) + values[1].astype(F32)
    in_deep[...] = deep(TIME_STEP * forward_pairs(whole(pair(in_t_ref))))
    inner_deep[...] = deep(TIME_STEP * forward_pairs(whole(pair(inner_t))))
    leave_deep[...] = deep(TIME_STEP * forward_pairs(leave_t[...].astype(F32)))
    weight = 3.0 * TIME_STEP
    out_deep[...] = deep(weight * backward_pairs(second))
    inner_t_deep[...] = deep(weight * backward_pairs(whole(pair(inner))))
    lift_t_deep[...] = deep(weight * backward_pairs(lift[...].astype(F32)))
    seen = backward_pairs(second)
    eff_ref[0] = deep(seen[16:32])
    eff_ref[1] = deep(seen[0:16])


def column(row):
    return jnp.broadcast_to(row[...], (128, 256)).T


def wide(bias):
    values = column(bias) if bias.shape[0] == 1 else bias[...]
    return jnp.concatenate([values, values], axis=1)


def gather(high, low, near, dot):
    for n in range(4):
        both = jnp.concatenate([high[16 * n : 16 * n + 16], low[16 * n : 16 * n + 16]], axis=0)
        yield dot(both, near[n])


def arrive_near(out, near, arrived_ref):
    high, low = split(out)
    for n, both in enumerate(gather(high, low, near, mm)):
        both = both.astype(BF16)
        arrived_ref[0, 16 * n : 16 * n + 16] = both[0:16]
        arrived_ref[1, 16 * n : 16 * n + 16] = both[16:32]


def prepare(parts, network):
    w_in, b_in, w_out, b_out, inner, leave, lift, near = network
    out = mm(leave[...], parts[0]) + mm(leave[...], parts[1])
    return mm3(pair(w_in), parts) + wide(b_in), mm3(pair(inner), parts) + wide(b_out), out


def full_rates(parts, hidden_parts, network, arrived_ref):
    w_in, b_in, w_out, b_out, inner, leave, lift, near = network
    rates = mm3(pair(inner), parts) + wide(b_out)
    rates += mm(lift[...], arrived_ref[0]) + mm(lift[...], arrived_ref[1])
    return rates + mm3(pair(w_out), hidden_parts)


def edge_rates(parts, hidden_parts, network, arrived_ref):
    w_in, b_in, w_out, b_out, inner, leave, lift, near = network
    rates = mm3([edge_rows(x) for x in pair(inner)], parts) + edge_rows(wide(b_out))
    rates += mm(edge_rows(lift), arrived_ref[0]) + mm(edge_rows(lift), arrived_ref[1])
    return rates + mm3([edge_rows(x) for x in pair(w_out)], hidden_parts)


def pick_parts(below, above, link):
    low = mm(jnp.concatenate(split(below), axis=0), link[0])
    high = mm(jnp.concatenate(split(above), axis=0), link[1])
    return low, high


def stack(low, high):
    top = jnp.concatenate([low[0:16], high[0:16]], axis=0).astype(BF16)
    rest = jnp.concatenate([low[16:32], high[16:32]], axis=0).astype(BF16)
    return jnp.concatenate([top, rest, top], axis=0)


def add_arrived(weight, base_ref, low, high, now_ref):
    low = weight * (low[0:16] + low[16:32])
    high = weight * (high[0:16] + high[16:32])
    now_ref[...] = base_ref[...]
    add_edges(now_ref, low, high, low, -high)
    return now_ref[...]


def prepared_rates(stacked, prepared, deeps, network, hidden_ref, arrived_ref):
    total, linear, out = (ref[...] + mm(d[...], stacked) for ref, d in zip(prepared, deeps))
    hidden = jnp.tanh(total)
    hidden_ref[...] = hidden
    lift, near, w_out = network[6], network[7], network[2]
    arrive_near(out, near, arrived_ref)
    linear += mm(lift[...], arrived_ref[0]) + mm(lift[...], arrived_ref[1])
    return linear + mm3(pair(w_out), split(hidden))


def middle_kernel(
    parity_ref, base_ref, state_ref, cross, in_chip, far_ref, sum_ref, linear_ref, out_ref, in_deep, inner_deep, leave_deep,
    w_in, b_in, w_out, b_out, inner, leave, lift, near,
    second_ref, third_ref, hidden_second, hidden_third, arrived_ref, link, in_chip_out, cross_out, between,
):
    network = (w_in, b_in, w_out, b_out, inner, leave, lift, near)
    parity = parity_ref[0]
    below, above = take(parity, in_chip[...], cross[...])
    rows = lax.broadcasted_iota(jnp.int32, (256, 256), 0).astype(F32)
    for side, received in enumerate((below, above)):
        link[side] = mm(one_hot(rows, received[32:33]), far_ref[side]).astype(BF16)
    low, high = pick_parts(below[0:16], above[0:16], link)
    rates = prepared_rates(
        stack(low, high), (sum_ref, linear_ref, out_ref), (in_deep, inner_deep, leave_deep),
        network, hidden_second, arrived_ref,
    )
    values = add_arrived(TIME_STEP, base_ref, low, high, second_ref)
    between[...] = 0.5 * (state_ref[...] + values) + HALF_STEP * rates
    put(parity, *leaving(edge_rows(between)), in_chip_out, cross_out)
    up_bias, down_bias = leaving(TIME_STEP * edge_rows(wide(b_out)))
    low, high = pick_parts(below[16:32] + up_bias, above[16:32] + down_bias, link)
    values = add_arrived(HALF_STEP, between, low, high, third_ref)
    parts = split(values)
    hidden = jnp.tanh(mm3(pair(w_in), parts) + wide(b_in))
    hidden_third[...] = hidden
    arrive_near(mm(leave[...], parts[0]) + mm(leave[...], parts[1]), near, arrived_ref)
    rates = edge_rates(parts, split(hidden), network, arrived_ref)
    put(parity, *leaving(edge_rows(values) + TIME_STEP * rates), in_chip_out, cross_out, 16)


def rest_kernel(
    third_ref, hidden_ref, arrived_ref, state_ref, w_in, b_in, w_out, b_out, inner, leave, lift, near,
    next_ref, sum_ref, linear_ref, out_ref, copy_ref,
):
    copy_ref[...] = state_ref[...]
    network = (w_in, b_in, w_out, b_out, inner, leave, lift, near)
    values = third_ref[...]
    base = values + TIME_STEP * full_rates(split(values), split(hidden_ref[...]), network, arrived_ref)
    next_ref[...] = base
    sum_ref[...], linear_ref[...], out_ref[...] = prepare(split(base), network)


def sensitivities(edge, link):
    upward = pick(edge[16:32] - edge[48:64], link[1], mm_nt)
    return upward, pick(edge[0:16] + edge[32:48], link[0], mm_nt)


def through_closure(parts, hidden, w_out_t):
    return (1.0 - hidden * hidden) * mm3(w_out_t, parts)


def gather_back(parts, lift_t, near):
    high, low = split(mm(lift_t[...], parts[0]) + mm(lift_t[...], parts[1]))
    return split(jnp.concatenate([a[0:16] + a[16:32] for a in gather(high, low, near, mm_nt)], axis=0))


def back_rates(parts, delta_parts, network, gathered, rows=lambda values: values[...]):
    w_in_t, inner_t, leave_t, lift_t, near = network
    rates = mm3([rows(x) for x in pair(inner_t)], parts) + mm3([rows(x) for x in pair(w_in_t)], delta_parts)
    return rates + (mm(rows(leave_t), gathered[0]) + mm(rows(leave_t), gathered[1]))


def turn_kernel(
    parity_ref, base_ref, third_ref, cross, in_chip, link, target_ref,
    sum_ref, linear_ref, out_ref, in_deep, inner_deep, leave_deep,
    w_in, b_in, w_out, b_out, inner, leave, lift, near, w_in_t, w_out_t, inner_t, leave_t, lift_t,
    final_ref, loss_ref, fourth_ref, hidden_ref, adjoint_ref, delta_ref, gathered_ref, in_chip_out, cross_out,
    between, arrived_ref,
):
    network = (w_in, b_in, w_out, b_out, inner, leave, lift, near)
    parity = parity_ref[0]
    below, above = take(parity, in_chip[...], cross[...])
    low, high = pick_parts(below[0:16], above[0:16], link)
    rates = prepared_rates(
        stack(low, high), (sum_ref, linear_ref, out_ref), (in_deep, inner_deep, leave_deep),
        network, hidden_ref, arrived_ref,
    )
    values = add_arrived(TIME_STEP, base_ref, low, high, fourth_ref)
    between[...] = 0.5 * (third_ref[...] + values) + HALF_STEP * rates
    low, high = pick_parts(below[16:32], above[16:32], link)
    final = add_arrived(HALF_STEP, between, low, high, final_ref)
    mismatch = final - target_ref[...]
    adjoint = (HALF_STEP / COUNT) * mismatch
    adjoint_ref[...] = adjoint
    squares = jnp.sum(mismatch * mismatch, axis=0, keepdims=True)
    loss_ref[...] = jnp.broadcast_to(squares[:, 0:128] + squares[:, 128:256], (8, 128))
    edge = edge_rows(adjoint)
    put(parity, *sensitivities(edge, link), in_chip_out, cross_out)
    parts = split(adjoint)
    delta = through_closure(parts, hidden_ref[...], pair(w_out_t))
    delta_ref[...] = delta
    gathered = gather_back(parts, lift_t, near)
    gathered_ref[0], gathered_ref[1] = gathered
    back = (w_in_t, inner_t, leave_t, lift_t, near)
    rates = back_rates(parts, split(delta), back, gathered, edge_rows)
    put(parity, *sensitivities(edge + TIME_STEP * rates, link), in_chip_out, cross_out, 16)


def bias_rows(first, second):
    rows = lax.broadcasted_iota(jnp.int32, (8, 128), 0)
    bias = jnp.where(rows == 0, first[:, 0:128], jnp.where(rows == 1, first[:, 128:256], 0.0))
    bias = jnp.where(rows == 2, second[:, 0:128], bias)
    if second.shape[1] == 256:
        bias = jnp.where(rows == 3, second[:, 128:256], bias)
    return bias


def row_sums(parts):
    ones = jnp.ones((8, 256), BF16)
    return mm_nt(ones, parts[0]) + mm_nt(ones, parts[1])


def gradients(parts, delta_parts, state, hidden):
    bias = bias_rows(row_sums(delta_parts), row_sums(parts))
    return mm3(delta_parts, split(state), mm_nt), mm3(parts, split(hidden), mm_nt), bias


def beside_kernel(
    adjoint_ref, delta_ref, gathered_ref, state_ref, hidden_ref,
    w_in_t, inner_t, leave_t, lift_t, near, w_out_t, hidden_third,
    next_ref, grad_in, grad_out, extra, back_ref, linear_ref, out_ref,
):
    adjoint = adjoint_ref[...]
    parts, delta_parts = split(adjoint), split(delta_ref[...])
    gathered = gathered_ref[0], gathered_ref[1]
    base = adjoint + TIME_STEP * back_rates(parts, delta_parts, (w_in_t, inner_t, leave_t, lift_t, near), gathered)
    next_ref[...] = base
    base_parts = split(base)
    back_ref[...] = mm3(pair(w_out_t), base_parts)
    linear_ref[...] = mm3(pair(inner_t), base_parts)
    out_ref[...] = mm(lift_t[...], base_parts[0]) + mm(lift_t[...], base_parts[1])
    first, second, bias = gradients(parts, delta_parts, state_ref[...], hidden_ref[...])
    grad_in[...] = first
    grad_out[...] = second + mm3(base_parts, split(hidden_third[...]), mm_nt)
    extra[...] = bias


def hidden_kernel(cross, in_chip, w_in, b_in, cross_hidden, in_chip_hidden):
    for source, ref in ((cross, cross_hidden), (in_chip, in_chip_hidden)):
        ref[...] = jnp.tanh(mm3(pair(w_in), split(source[...])) + wide(b_in))


def back_kernel(
    parity_ref, base_ref, adjoint_ref, cross, in_chip, link,
    third_ref, hidden_third, second_ref, hidden_second, state_ref, hidden_first,
    cross_state, in_chip_state, cross_hidden, in_chip_hidden,
    near, w_in_t, w_out_t, inner_t, leave_t, lift_t, eff, back_ref, linear_ref, out_ref, out_deep, inner_t_deep, lift_t_deep,
    old_in, old_out, old_extra, loss_ref,
    keep_ref, send_ref, now_ref, between, sum_ref,
):
    network = (w_in_t, inner_t, leave_t, lift_t, near)
    parity = parity_ref[0]
    even = parity == 0
    below, above = take(parity, in_chip[...], cross[...])
    totals = [old_in[...], old_out[...], old_extra[...]]

    def arrive(source_ref, weight, low, high):
        now_ref[...] = source_ref[...]
        low, high = weight * low, weight * high
        add_edges(now_ref, low, high, -low, high)
        return now_ref[...]

    def collect(*args):
        for n, term in enumerate(gradients(*args)):
            totals[n] = totals[n] + term

    received = below[0:16], above[0:16]
    high_parts, low_parts = zip(*(split(x) for x in received))
    top, rest = jnp.concatenate(high_parts, axis=0), jnp.concatenate(low_parts, axis=0)
    stacked = jnp.concatenate([top, rest, top], axis=0)
    hidden = hidden_third[...]
    delta_full = (1.0 - hidden * hidden) * (back_ref[...] + mm(out_deep[...], stacked))
    delta = split(delta_full)
    high, low = split(out_ref[...] + mm(lift_t_deep[...], stacked))
    gathered = split(jnp.concatenate([a[0:16] + a[16:32] for a in gather(high, low, near, mm_nt)], axis=0))
    rates = linear_ref[...] + mm(inner_t_deep[...], stacked) + mm3(pair(w_in_t), delta)
    rates += mm(leave_t[...], gathered[0]) + mm(leave_t[...], gathered[1])
    values = arrive(base_ref, 3.0 * TIME_STEP, *received)
    between[...] = 0.5 * (adjoint_ref[...] + values) + HALF_STEP * rates
    totals[0] = totals[0] + mm3(delta, split(third_ref[...]), mm_nt)
    totals[2] = totals[2] + bias_rows(row_sums(delta), row_sums(split(values)))
    weight = 3.0 * TIME_STEP
    hidden_parts = split(hidden)
    early = [weight * mm3((h, l), hidden_parts, mm_nt) for h, l in zip(high_parts, low_parts)]
    upward, downward = sensitivities(edge_rows(between), link)

    values = arrive(between, 3.0 * HALF_STEP, below[16:32], above[16:32])
    parts = split(values)
    delta = split(through_closure(parts, hidden_second[...], pair(w_out_t)))
    values = values + TIME_STEP * back_rates(parts, delta, network, gather_back(parts, lift_t, near))
    collect(parts, delta, second_ref[...], hidden_second[...])

    states = take(parity, in_chip_state[...], cross_state[...])
    hiddens = take(parity, in_chip_hidden[...], cross_hidden[...])
    blocks = []
    for side, received in enumerate((weight * downward, weight * upward)):
        high, low = split(received)
        hidden = hiddens[side]
        seen = mm(eff[side], jnp.concatenate([high, low, high], axis=0))
        delta = split((1.0 - hidden * hidden) * seen)
        totals[0] = totals[0] + mm3(delta, split(states[side]), mm_nt)
        blocks.append(mm3((high, low), split(hidden), mm_nt))
        none = jnp.zeros((48, 256), F32)
        spread = [none, received, none, received] if side == 0 else [received, none, -received, none]
        totals[2] = totals[2] + bias_rows(row_sums(delta), row_sums(split(jnp.concatenate(spread, axis=0))))

    parts = split(values)
    delta = split(through_closure(parts, hidden_first[...], pair(w_out_t)))
    collect(parts, delta, state_ref[...], hidden_first[...])
    sum_ref[...] = totals[1]
    low, high = blocks[1] + early[0], blocks[0] + early[1]
    add_edges(sum_ref, low, high, -low, high)
    first, second, bias = totals[0], sum_ref[...], totals[2]
    rows = lax.broadcasted_iota(jnp.int32, (8, 128), 0)
    bias = jnp.where(rows == 4, loss_ref[...], bias)
    for ref, values in ((keep_ref, jnp.where(even, first, second)), (send_ref, jnp.where(even, second, first))):
        for n in range(16):
            ref[n, 0:16] = values[16 * n : 16 * n + 16, 0:128]
            ref[n, 16:32] = values[16 * n : 16 * n + 16, 128:256]
            ref[n, 32:40] = bias


def chip_kernel(keep_ref, got_ref, out_ref):
    out_ref[...] = keep_ref[...] + got_ref[...]


def plane_kernel(parts_ref, out_ref):
    total = jnp.sum(parts_ref[...], axis=0)
    for n in range(8):
        out_ref[n] = total


def line_kernel(parts_ref, out_ref, extra_ref):
    total = jnp.sum(parts_ref[...], axis=0)
    extra_ref[...] = total[32:40]
    for n in range(16):
        out_ref[n] = total[0:32]


def last_kernel(parity_ref, own_ref, other_ref, extra_ref, in_ref, b_in_ref, out_ref, b_out_ref, loss_ref):
    even = parity_ref[0] == 0
    own, other = own_ref[...], other_ref[...]
    first = jnp.where(even, own, other)
    second = jnp.where(even, other, own)
    bias = extra_ref[0:4]
    squares = jnp.sum(first * first + second * second, axis=0)
    total = jnp.sum(squares, keepdims=True) + jnp.sum(bias * bias, keepdims=True)
    scale = lax.rsqrt(total / PARAMS + TINY)
    for ref, values in ((in_ref, first * scale), (out_ref, second * scale)):
        for n in range(16):
            ref[16 * n : 16 * n + 16, 0:128] = values[n, 0:16]
            ref[16 * n : 16 * n + 16, 128:256] = values[n, 16:32]
    bias = bias * scale
    for row, ref in ((0, b_in_ref), (2, b_out_ref)):
        ref[:, 0:128] = bias[row : row + 1]
        ref[:, 128:256] = bias[row + 1 : row + 2]
    loss_ref[...] = jnp.sum(extra_ref[4:5], keepdims=True) * (0.5 / COUNT)


IN_CHIP = [(n, n ^ 1) for n in range(DEVICES)]
CROSS = [(n, (n - 1) % DEVICES if n % 2 == 0 else (n + 1) % DEVICES) for n in range(DEVICES)]


def exchange(in_chip, cross):
    return lax.ppermute(cross, AXES, CROSS), lax.ppermute(in_chip, AXES, IN_CHIP)


def local(state, target, w_in, b_in, w_out, b_out, nbr, send):
    parity = lax.axis_index("core").reshape(1)
    inner, leave, lift = operators()
    edge = np.concatenate([np.arange(0, 16), np.arange(48, 80), np.arange(112, 128)])
    fixed = np.zeros((768, 256))
    fixed[0:64], fixed[64:128] = (x[edge].astype(np.float64) for x in halves(inner))
    fixed[128:192], fixed[192:256, 0:64] = leave, lift[edge]
    to_bf16 = lambda values: jnp.asarray(values.astype(ml_dtypes.bfloat16))
    fixed, inner2, leave1, lift_t = (to_bf16(x) for x in (fixed, np.concatenate(halves(inner)), leave, lift.T))
    b_in, b_out = b_in.reshape(1, 256), b_out.reshape(1, 256)
    tall, flat, thin = ((512, 256), BF16), ((64, 256), BF16), ((256, 64), BF16)
    arrival = ((2, 64, 256), BF16)
    arrived, hidden_first, *edge, w_in2, state = call(
        first_kernel,
        [arrival, SQUARE, ((40, 256), F32), ((40, 256), F32), PAIR, SQUARE],
        parity, state, w_in, fixed, w_out, nbr, send, b_in,
        name="first", micros=1.5,
        far=range(1, 8),
        limit=53,
        scratch=[
            pltpu.VMEM((256, 256), F32), pltpu.VMEM((64, 256), F32), pltpu.VMEM((256, 256), BF16),
            pltpu.VMEM((4, 256, 256), BF16), pltpu.VMEM((6, 256), jnp.int32), pltpu.VMEM((2, 256), jnp.int32),
            pltpu.VMEM((1, 256), F32), pltpu.SemaphoreType.DMA((9,)),
        ],
    )
    got = exchange(*edge)
    middle = [SQUARE, SQUARE, ((64, 256), F32)]
    depth, shallow = ((256, 96), BF16), ((64, 96), BF16)
    made = call(
        tables_kernel,
        [SQUARE, *middle, PAIR, PAIR, PAIR, tall, thin, thin, ((4, 256, 256), BF16), PAIR]
        + [((256, 128), F32)] * 2
        + [depth, depth, shallow] * 2
        + [((2, 256, 48), BF16)],
        w_in2, w_out, inner2, leave1, lift_t, nbr, b_in, b_out, state, arrived, hidden_first, edge[0],
        name="tables", micros=1.5,
    )
    base, prepared, deeps, eff = made[0], made[1:4], made[14:20], made[20]
    w_out2, w_in_t, w_out_t, inner_t, leave_t, lift1, near, far, b_in2, b_out2 = made[4:14]
    forward_deeps, backward_deeps = deeps[:3], deeps[3:]
    network = (w_in2, b_in2, w_out2, b_out2, inner2, leave1, lift1, near)
    back = (w_in_t, inner_t, leave_t, lift_t)
    edge_shapes = [((32, 256), F32)] * 2
    square = pltpu.VMEM((256, 256), F32)
    second, third, hidden_second, hidden_third, arrived, link, *edge = call(
        middle_kernel,
        [SQUARE] * 4 + [arrival, PAIR] + edge_shapes,
        parity, base, state, *got, far, *prepared, *forward_deeps, *network, name="middle", micros=2.1, scratch=[square],
    )
    got = exchange(*edge)
    base, *prepared, copy = call(
        rest_kernel, [SQUARE, *middle, SQUARE], third, hidden_third, arrived, state, *network, name="rest", micros=0.9
    )
    beside = exchange(copy, copy)
    final, loss, fourth, hidden_fourth, adjoint, delta, gathered, *edge = call(
        turn_kernel,
        [SQUARE, EXTRA] + [SQUARE] * 4 + [arrival] + edge_shapes,
        parity, base, third, *got, link, target, *prepared, *forward_deeps, *network,
        w_in_t, w_out_t, inner_t, leave_t, lift_t,
        name="turn", micros=2.5, scratch=[square, pltpu.VMEM((2, 64, 256), BF16)],
    )
    got = exchange(*edge)
    base, *grads, back_product, linear, out = call(
        beside_kernel,
        [SQUARE, SQUARE, SQUARE, EXTRA, *middle],
        adjoint, delta, gathered, fourth, hidden_fourth, *back, near, w_out_t, hidden_third,
        name="beside", micros=1.4,
    )
    beside_hidden = call(hidden_kernel, [SQUARE] * 2, *beside, w_in2, b_in2, name="hidden", micros=0.6)
    keep, give = call(
        back_kernel,
        [PACKED] * 2,
        parity, base, adjoint, *got, link, third, hidden_third, second, hidden_second, state, hidden_first,
        *beside, *beside_hidden, near, w_in_t, w_out_t, inner_t, leave_t, lift_t, eff,
        back_product, linear, out, *backward_deeps, *grads, loss,
        name="back", micros=4, scratch=[square] * 3,
    )
    swap = [(0, 1), (1, 0)]
    (parts,) = call(chip_kernel, [PACKED], keep, lax.ppermute(give, "core", swap), name="chip_sum", micros=0.3)
    parts = lax.all_to_all(parts, PLANE, 0, 0, tiled=True)
    (parts,) = call(plane_kernel, [((8, 40, 128), F32)], parts, name="plane_sum", micros=0.3)
    parts = lax.all_to_all(parts, "z", 0, 0, tiled=True)
    parts, extra = call(line_kernel, [((16, 32, 128), F32), EXTRA], parts, name="line_sum", micros=0.3)
    own = lax.all_to_all(parts, PLANE, 0, 0, tiled=True)
    other = lax.ppermute(own, "core", swap)
    row = ((1, 256), F32)
    step_in, step_b_in, step_out, step_b_out, loss = call(
        last_kernel, [SQUARE, row, SQUARE, row, ((1, 1), F32)], parity, own, other, extra, name="scale", micros=1
    )
    return final, loss.reshape(()), step_in, step_b_in.reshape(256), step_out, step_b_out.reshape(256)


def solution(mesh):
    split_mesh = Mesh(mesh.devices.reshape(SIZES), AXES)
    whole = P(None, AXES)
    return jax.shard_map(
        local,
        mesh=split_mesh,
        in_specs=(whole, whole, P(), P(), P(), P(), whole, whole),
        out_specs=(whole, P(), P(), P(), P(), P()),
        check_vma=False,
    )
```

```python
import jax
import jax.numpy as jnp
import ml_dtypes
import numpy as np
from jax import lax
from jax.experimental import pallas as pl
from jax.experimental.pallas import tpu as pltpu
from jax.sharding import Mesh, PartitionSpec as P

AXES = ("x", "y", "z", "core")
PLANE = ("x", "y")
SIZES = (4, 4, 8, 2)
DEVICES = 256
WIDTH = 256
COUNT = 16777216.0
PARAMS = 131584.0
TIME_STEP = 0.05
HALF_STEP = 0.025
TINY = 1e-20
F32 = jnp.float32
BF16 = jnp.bfloat16


def face_rows(face):
    layer = 0 if face % 2 == 0 else 3
    grid = np.arange(64).reshape(4, 4, 4)
    return np.take(grid, layer, axis=face // 2).reshape(16)


def operators():
    points = np.array([-1.0, -1.0 / np.sqrt(5.0), 1.0 / np.sqrt(5.0), 1.0])
    bary = np.array(
        [1.0 / np.prod([points[m] - points[n] for n in range(4) if n != m]) for m in range(4)]
    )
    deriv = np.zeros((4, 4))
    for m in range(4):
        for n in range(4):
            if m != n:
                deriv[m, n] = bary[n] / bary[m] / (points[m] - points[n])
        deriv[m, m] = -np.sum(deriv[m])
    eye = np.eye(4)
    tables = [
        np.kron(np.kron(deriv, eye), eye),
        np.kron(np.kron(eye, deriv), eye),
        np.kron(eye, np.kron(eye, deriv)),
    ]
    inner = np.zeros((256, 256))
    for a in range(3):
        inner[0:64, 64 * (a + 1) : 64 * (a + 2)] -= tables[a]
        inner[64 * (a + 1) : 64 * (a + 2), 0:64] -= tables[a]
    for face in range(6):
        sign = 2.0 * (face % 2) - 1.0
        for row in face_rows(face):
            speed = 64 * (face // 2 + 1) + row
            inner[row, row] -= 3.0
            inner[row, speed] += 3.0 * sign
            inner[speed, speed] -= 3.0
            inner[speed, row] += 3.0 * sign
    leave = np.zeros((64, 256))
    lift = np.zeros((256, 64))
    for face in range(2, 6):
        sign = 2.0 * (face % 2) - 1.0
        base = 16 * (face - 2)
        for n, row in enumerate(face_rows(face ^ 1)):
            leave[base + n, row] = 3.0
            leave[base + n, 64 * (face // 2 + 1) + row] = -3.0 * sign
        for n, row in enumerate(face_rows(face)):
            lift[row, base + n] = 1.0
            lift[64 * (face // 2 + 1) + row, base + n] = -sign
    return inner, leave, lift


def halves(values):
    high = values.astype(ml_dtypes.bfloat16)
    low = (values - high.astype(np.float64)).astype(ml_dtypes.bfloat16)
    return high, low


def split(values):
    high = values.astype(BF16)
    return high, (values - high.astype(F32)).astype(BF16)


def mm(left, right):
    return jnp.dot(left, right, preferred_element_type=F32)


def mm_nt(left, right):
    return lax.dot_general(left, right, (((1,), (1,)), ((), ())), preferred_element_type=F32)


def mm3(left, right, dot=mm):
    return dot(left[0], right[0]) + (dot(left[0], right[1]) + dot(left[1], right[0]))


def pair(ref):
    if len(ref.shape) == 2:
        return ref[0:256], ref[256:512]
    return ref[0], ref[1]


def call(body, outs, *args, name, micros, far=(), scratch=(), limit=24, reads=1000000):
    def space(n, value):
        if value.shape == (1,):
            return pltpu.SMEM
        return pltpu.HBM if n in far else pltpu.VMEM

    return list(pl.pallas_call(
        body,
        out_shape=[jax.ShapeDtypeStruct(s, t) for s, t in outs],
        in_specs=[pl.BlockSpec(memory_space=space(n, a)) for n, a in enumerate(args)],
        out_specs=[pl.BlockSpec(memory_space=pltpu.VMEM)] * len(outs),
        scratch_shapes=scratch,
        cost_estimate=pl.CostEstimate(flops=int(micros * 1.15e9), bytes_accessed=reads, transcendentals=0),
        compiler_params=pltpu.CompilerParams(vmem_limit_bytes=int(limit * 1048576)),
        name=name,
    )(*args))


SQUARE = ((256, 256), F32)
PAIR = ((2, 256, 256), BF16)
EXTRA = ((8, 128), F32)
PACKED = ((16, 40, 128), F32)


def edges(values):
    return values[0:16], values[48:64], values[64:80], values[112:128]


def edge_rows(values):
    return jnp.concatenate(edges(values), axis=0)


def leaving(edge):
    return 3.0 * (edge[16:32] + edge[48:64]), 3.0 * (edge[0:16] - edge[32:48])


def put(parity, upward, downward, in_chip_ref, cross_ref, rows=0):
    even = parity == 0
    in_chip_ref[rows : rows + 16] = jnp.where(even, upward, downward)
    cross_ref[rows : rows + 16] = jnp.where(even, downward, upward)


def take(parity, in_chip, cross):
    even = parity == 0
    return jnp.where(even, cross, in_chip), jnp.where(even, in_chip, cross)


def pick(values, table, dot=mm):
    both = dot(jnp.concatenate(split(values), axis=0), table)
    return both[0:16] + both[16:32]


def add_edges(values_ref, first, second, third, fourth):
    values_ref[0:16] += first
    values_ref[48:64] += second
    values_ref[64:80] += third
    values_ref[112:128] += fourth


def one_hot(rows, column):
    return (rows == column).astype(F32).astype(BF16)


def make_near(index_ref, near):
    rows = lax.broadcasted_iota(jnp.int32, (256, 256), 0)
    for face in range(2, 6):
        near[face - 2] = one_hot(rows, index_ref[face : face + 1] - 256 * (face ^ 1))


def first_kernel(
    parity_ref, state_far, w_in_far, fixed_far, w_out_far, nbr_far, send_far, b_in_far,
    arrived_ref, hidden_ref, in_chip_ref, cross_ref, w_in, state_ref,
    w_in_ref, w_out_ref, fixed, near, nbr_ref, send_ref, b_in, sems,
):
    pairs = (
        (state_far, state_ref), (w_in_far, w_in_ref), (fixed_far.at[0:256], fixed), (w_out_far.at[0:16], w_out_ref.at[0:16]),
        (w_out_far.at[48:80], w_out_ref.at[16:48]), (w_out_far.at[112:128], w_out_ref.at[48:64]),
        (nbr_far, nbr_ref), (send_far, send_ref), (b_in_far, b_in),
    )
    copies = [pltpu.make_async_copy(s, t, sems.at[n]) for n, (s, t) in enumerate(pairs)]
    for copy in copies:
        copy.start()
    copies[0].wait()
    values = state_ref[...]
    edge = edge_rows(values)
    parts = split(values)
    parity = parity_ref[0]
    put(parity, *leaving(edge), in_chip_ref, cross_ref)
    copies[1].wait()
    w_in[0], w_in[1] = split(w_in_ref[...])
    copies[8].wait()
    bias = wide(b_in)
    hidden = jnp.tanh(mm3(pair(w_in), parts) + bias)
    hidden_ref[...] = hidden
    for copy in copies[2:8]:
        copy.wait()
    make_near(nbr_ref, near)
    arrive_near(mm(fixed[128:192], parts[0]) + mm(fixed[128:192], parts[1]), near, arrived_ref)
    rates = mm3((fixed[0:64], fixed[64:128]), parts) + mm3(split(w_out_ref[...]), split(hidden))
    lift = fixed[192:256, 0:64]
    rates += mm(lift, arrived_ref[0]) + mm(lift, arrived_ref[1])
    put(parity, *leaving(edge + TIME_STEP * rates), in_chip_ref, cross_ref, 16)
    down_index = send_ref[0:1].astype(F32)
    up_index = (send_ref[1:2] - 256).astype(F32)
    even = parity == 0
    in_chip_ref[32:40] = jnp.broadcast_to(jnp.where(even, up_index, down_index), (8, 256))
    cross_ref[32:40] = jnp.broadcast_to(jnp.where(even, down_index, up_index), (8, 256))


def flip(values):
    return values.astype(F32).T.astype(BF16)


def forward_pairs(turned):
    return jnp.concatenate([turned[0:16] + turned[64:80], turned[48:64] - turned[112:128]], axis=0)


def backward_pairs(turned):
    return jnp.concatenate([turned[0:16] - turned[64:80], turned[48:64] + turned[112:128]], axis=0)


def deep(rows):
    high, low = split(rows.T)
    return jnp.concatenate([high, high, low], axis=1)


def tables_kernel(
    w_in, w_out_ref, inner, leave, lift_t, nbr_ref, b_in, b_out, state_ref, arrived_ref, hidden_ref, after_ref,
    next_ref, sum_ref, linear_ref, out_ref, w_out, in_t_ref, out_t_ref, inner_t, leave_t, lift,
    near, far_ref, column_in, column_out, in_deep, inner_deep, leave_deep, out_deep, inner_t_deep, lift_t_deep, eff_ref,
):
    column_in[...] = column(b_in)
    column_out[...] = column(b_out)
    second = w_out_ref[...]
    w_out[0], w_out[1] = split(second)
    lift[...] = flip(lift_t[...])
    leave_t[...] = flip(leave[...])
    values = state_ref[...]
    network = (w_in, column_in, w_out, column_out, inner, leave, lift, near)
    rates = full_rates(split(values), split(hidden_ref[...]), network, arrived_ref)
    base = values + TIME_STEP * rates
    next_ref[...] = base
    sum_ref[...], linear_ref[...], out_ref[...] = prepare(split(base), network)
    make_near(nbr_ref, near)
    rows = lax.broadcasted_iota(jnp.int32, (256, 256), 0)
    for face in range(2):
        far_ref[face] = one_hot(rows, nbr_ref[face : face + 1] - (1536 + 256 * face))
    for part in range(2):
        in_t_ref[part] = flip(w_in[part])
        out_t_ref[part] = flip(w_out[part])
        inner_t[256 * part : 256 * part + 256] = flip(inner[256 * part : 256 * part + 256])
    whole = lambda values: values[0].astype(F32) + values[1].astype(F32)
    in_deep[...] = deep(TIME_STEP * forward_pairs(whole(pair(in_t_ref))))
    inner_deep[...] = deep(TIME_STEP * forward_pairs(whole(pair(inner_t))))
    leave_deep[...] = deep(TIME_STEP * forward_pairs(leave_t[...].astype(F32)))
    weight = 3.0 * TIME_STEP
    out_deep[...] = deep(weight * backward_pairs(second))
    inner_t_deep[...] = deep(weight * backward_pairs(whole(pair(inner))))
    lift_t_deep[...] = deep(weight * backward_pairs(lift[...].astype(F32)))
    seen = backward_pairs(second)
    eff_ref[0] = deep(seen[16:32])
    eff_ref[1] = deep(seen[0:16])


def column(row):
    return jnp.broadcast_to(row[...], (128, 256)).T


def wide(bias):
    values = column(bias) if bias.shape[0] == 1 else bias[...]
    return jnp.concatenate([values, values], axis=1)


def gather(high, low, near, dot):
    for n in range(4):
        both = jnp.concatenate([high[16 * n : 16 * n + 16], low[16 * n : 16 * n + 16]], axis=0)
        yield dot(both, near[n])


def arrive_near(out, near, arrived_ref):
    high, low = split(out)
    for n, both in enumerate(gather(high, low, near, mm)):
        both = both.astype(BF16)
        arrived_ref[0, 16 * n : 16 * n + 16] = both[0:16]
        arrived_ref[1, 16 * n : 16 * n + 16] = both[16:32]


def prepare(parts, network):
    w_in, b_in, w_out, b_out, inner, leave, lift, near = network
    out = mm(leave[...], parts[0]) + mm(leave[...], parts[1])
    return mm3(pair(w_in), parts) + wide(b_in), mm3(pair(inner), parts) + wide(b_out), out


def full_rates(parts, hidden_parts, network, arrived_ref):
    w_in, b_in, w_out, b_out, inner, leave, lift, near = network
    rates = mm3(pair(inner), parts) + wide(b_out)
    rates += mm(lift[...], arrived_ref[0]) + mm(lift[...], arrived_ref[1])
    return rates + mm3(pair(w_out), hidden_parts)


def edge_rates(parts, hidden_parts, network, arrived_ref):
    w_in, b_in, w_out, b_out, inner, leave, lift, near = network
    rates = mm3([edge_rows(x) for x in pair(inner)], parts) + edge_rows(wide(b_out))
    rates += mm(edge_rows(lift), arrived_ref[0]) + mm(edge_rows(lift), arrived_ref[1])
    return rates + mm3([edge_rows(x) for x in pair(w_out)], hidden_parts)


def pick_parts(below, above, link):
    low = mm(jnp.concatenate(split(below), axis=0), link[0])
    high = mm(jnp.concatenate(split(above), axis=0), link[1])
    return low, high


def stack(low, high):
    top = jnp.concatenate([low[0:16], high[0:16]], axis=0).astype(BF16)
    rest = jnp.concatenate([low[16:32], high[16:32]], axis=0).astype(BF16)
    return jnp.concatenate([top, rest, top], axis=0)


def add_arrived(weight, base_ref, low, high, now_ref):
    low = weight * (low[0:16] + low[16:32])
    high = weight * (high[0:16] + high[16:32])
    now_ref[...] = base_ref[...]
    add_edges(now_ref, low, high, low, -high)
    return now_ref[...]


def prepared_rates(stacked, prepared, deeps, network, hidden_ref, arrived_ref):
    total, linear, out = (ref[...] + mm(d[...], stacked) for ref, d in zip(prepared, deeps))
    hidden = jnp.tanh(total)
    hidden_ref[...] = hidden
    lift, near, w_out = network[6], network[7], network[2]
    arrive_near(out, near, arrived_ref)
    linear += mm(lift[...], arrived_ref[0]) + mm(lift[...], arrived_ref[1])
    return linear + mm3(pair(w_out), split(hidden))


def middle_kernel(
    parity_ref, base_ref, state_ref, cross, in_chip, far_ref, sum_ref, linear_ref, out_ref, in_deep, inner_deep, leave_deep,
    w_in, b_in, w_out, b_out, inner, leave, lift, near,
    second_ref, third_ref, hidden_second, hidden_third, arrived_ref, link, in_chip_out, cross_out, between,
):
    network = (w_in, b_in, w_out, b_out, inner, leave, lift, near)
    parity = parity_ref[0]
    below, above = take(parity, in_chip[...], cross[...])
    rows = lax.broadcasted_iota(jnp.int32, (256, 256), 0).astype(F32)
    for side, received in enumerate((below, above)):
        link[side] = mm(one_hot(rows, received[32:33]), far_ref[side]).astype(BF16)
    low, high = pick_parts(below[0:16], above[0:16], link)
    rates = prepared_rates(
        stack(low, high), (sum_ref, linear_ref, out_ref), (in_deep, inner_deep, leave_deep),
        network, hidden_second, arrived_ref,
    )
    values = add_arrived(TIME_STEP, base_ref, low, high, second_ref)
    between[...] = 0.5 * (state_ref[...] + values) + HALF_STEP * rates
    put(parity, *leaving(edge_rows(between)), in_chip_out, cross_out)
    up_bias, down_bias = leaving(TIME_STEP * edge_rows(wide(b_out)))
    low, high = pick_parts(below[16:32] + up_bias, above[16:32] + down_bias, link)
    values = add_arrived(HALF_STEP, between, low, high, third_ref)
    parts = split(values)
    hidden = jnp.tanh(mm3(pair(w_in), parts) + wide(b_in))
    hidden_third[...] = hidden
    arrive_near(mm(leave[...], parts[0]) + mm(leave[...], parts[1]), near, arrived_ref)
    rates = edge_rates(parts, split(hidden), network, arrived_ref)
    put(parity, *leaving(edge_rows(values) + TIME_STEP * rates), in_chip_out, cross_out, 16)


def rest_kernel(
    third_ref, hidden_ref, arrived_ref, state_ref, w_in, b_in, w_out, b_out, inner, leave, lift, near,
    next_ref, sum_ref, linear_ref, out_ref, copy_ref,
):
    copy_ref[...] = state_ref[...]
    network = (w_in, b_in, w_out, b_out, inner, leave, lift, near)
    values = third_ref[...]
    base = values + TIME_STEP * full_rates(split(values), split(hidden_ref[...]), network, arrived_ref)
    next_ref[...] = base
    sum_ref[...], linear_ref[...], out_ref[...] = prepare(split(base), network)


def sensitivities(edge, link):
    upward = pick(edge[16:32] - edge[48:64], link[1], mm_nt)
    return upward, pick(edge[0:16] + edge[32:48], link[0], mm_nt)


def through_closure(parts, hidden, w_out_t):
    return (1.0 - hidden * hidden) * mm3(w_out_t, parts)


def gather_back(parts, lift_t, near):
    high, low = split(mm(lift_t[...], parts[0]) + mm(lift_t[...], parts[1]))
    return split(jnp.concatenate([a[0:16] + a[16:32] for a in gather(high, low, near, mm_nt)], axis=0))


def back_rates(parts, delta_parts, network, gathered, rows=lambda values: values[...]):
    w_in_t, inner_t, leave_t, lift_t, near = network
    rates = mm3([rows(x) for x in pair(inner_t)], parts) + mm3([rows(x) for x in pair(w_in_t)], delta_parts)
    return rates + (mm(rows(leave_t), gathered[0]) + mm(rows(leave_t), gathered[1]))


def turn_kernel(
    parity_ref, base_ref, third_ref, cross, in_chip, link, target_ref,
    sum_ref, linear_ref, out_ref, in_deep, inner_deep, leave_deep,
    w_in, b_in, w_out, b_out, inner, leave, lift, near, w_in_t, w_out_t, inner_t, leave_t, lift_t,
    final_ref, loss_ref, fourth_ref, hidden_ref, adjoint_ref, delta_ref, gathered_ref, in_chip_out, cross_out,
    between, arrived_ref,
):
    network = (w_in, b_in, w_out, b_out, inner, leave, lift, near)
    parity = parity_ref[0]
    below, above = take(parity, in_chip[...], cross[...])
    low, high = pick_parts(below[0:16], above[0:16], link)
    rates = prepared_rates(
        stack(low, high), (sum_ref, linear_ref, out_ref), (in_deep, inner_deep, leave_deep),
        network, hidden_ref, arrived_ref,
    )
    values = add_arrived(TIME_STEP, base_ref, low, high, fourth_ref)
    between[...] = 0.5 * (third_ref[...] + values) + HALF_STEP * rates
    low, high = pick_parts(below[16:32], above[16:32], link)
    final = add_arrived(HALF_STEP, between, low, high, final_ref)
    mismatch = final - target_ref[...]
    adjoint = (HALF_STEP / COUNT) * mismatch
    adjoint_ref[...] = adjoint
    squares = jnp.sum(mismatch * mismatch, axis=0, keepdims=True)
    loss_ref[...] = jnp.broadcast_to(squares[:, 0:128] + squares[:, 128:256], (8, 128))
    edge = edge_rows(adjoint)
    put(parity, *sensitivities(edge, link), in_chip_out, cross_out)
    parts = split(adjoint)
    delta = through_closure(parts, hidden_ref[...], pair(w_out_t))
    delta_ref[...] = delta
    gathered = gather_back(parts, lift_t, near)
    gathered_ref[0], gathered_ref[1] = gathered
    back = (w_in_t, inner_t, leave_t, lift_t, near)
    rates = back_rates(parts, split(delta), back, gathered, edge_rows)
    put(parity, *sensitivities(edge + TIME_STEP * rates, link), in_chip_out, cross_out, 16)


def bias_rows(first, second):
    rows = lax.broadcasted_iota(jnp.int32, (8, 128), 0)
    bias = jnp.where(rows == 0, first[:, 0:128], jnp.where(rows == 1, first[:, 128:256], 0.0))
    bias = jnp.where(rows == 2, second[:, 0:128], bias)
    if second.shape[1] == 256:
        bias = jnp.where(rows == 3, second[:, 128:256], bias)
    return bias


def row_sums(parts):
    ones = jnp.ones((8, 256), BF16)
    return mm_nt(ones, parts[0]) + mm_nt(ones, parts[1])


def gradients(parts, delta_parts, state, hidden):
    bias = bias_rows(row_sums(delta_parts), row_sums(parts))
    return mm3(delta_parts, split(state), mm_nt), mm3(parts, split(hidden), mm_nt), bias


def beside_kernel(
    adjoint_ref, delta_ref, gathered_ref, state_ref, hidden_ref,
    w_in_t, inner_t, leave_t, lift_t, near, w_out_t, hidden_third,
    next_ref, grad_in, grad_out, extra, back_ref, linear_ref, out_ref,
):
    adjoint = adjoint_ref[...]
    parts, delta_parts = split(adjoint), split(delta_ref[...])
    gathered = gathered_ref[0], gathered_ref[1]
    base = adjoint + TIME_STEP * back_rates(parts, delta_parts, (w_in_t, inner_t, leave_t, lift_t, near), gathered)
    next_ref[...] = base
    base_parts = split(base)
    back_ref[...] = mm3(pair(w_out_t), base_parts)
    linear_ref[...] = mm3(pair(inner_t), base_parts)
    out_ref[...] = mm(lift_t[...], base_parts[0]) + mm(lift_t[...], base_parts[1])
    first, second, bias = gradients(parts, delta_parts, state_ref[...], hidden_ref[...])
    grad_in[...] = first
    grad_out[...] = second + mm3(base_parts, split(hidden_third[...]), mm_nt)
    extra[...] = bias


def final_kernel(final_ref, out_ref):
    out_ref[...] = final_ref[...]


def hidden_kernel(cross, in_chip, w_in, b_in, cross_hidden, in_chip_hidden):
    for source, ref in ((cross, cross_hidden), (in_chip, in_chip_hidden)):
        ref[...] = jnp.tanh(mm3(pair(w_in), split(source[...])) + wide(b_in))


def back_kernel(
    parity_ref, base_ref, adjoint_ref, cross, in_chip, link,
    third_ref, hidden_third, second_ref, hidden_second, state_ref, hidden_first,
    cross_state, in_chip_state, cross_hidden, in_chip_hidden,
    near, w_in_t, w_out_t, inner_t, leave_t, lift_t, eff, back_ref, linear_ref, out_ref, out_deep, inner_t_deep, lift_t_deep,
    old_in, old_out, old_extra, loss_ref,
    keep_ref, send_ref, now_ref, between, sum_ref,
):
    network = (w_in_t, inner_t, leave_t, lift_t, near)
    parity = parity_ref[0]
    even = parity == 0
    below, above = take(parity, in_chip[...], cross[...])
    totals = [old_in[...], old_out[...], old_extra[...]]

    def arrive(source_ref, weight, low, high):
        now_ref[...] = source_ref[...]
        low, high = weight * low, weight * high
        add_edges(now_ref, low, high, -low, high)
        return now_ref[...]

    def collect(*args):
        for n, term in enumerate(gradients(*args)):
            totals[n] = totals[n] + term

    received = below[0:16], above[0:16]
    high_parts, low_parts = zip(*(split(x) for x in received))
    top, rest = jnp.concatenate(high_parts, axis=0), jnp.concatenate(low_parts, axis=0)
    stacked = jnp.concatenate([top, rest, top], axis=0)
    hidden = hidden_third[...]
    delta_full = (1.0 - hidden * hidden) * (back_ref[...] + mm(out_deep[...], stacked))
    delta = split(delta_full)
    high, low = split(out_ref[...] + mm(lift_t_deep[...], stacked))
    gathered = split(jnp.concatenate([a[0:16] + a[16:32] for a in gather(high, low, near, mm_nt)], axis=0))
    rates = linear_ref[...] + mm(inner_t_deep[...], stacked) + mm3(pair(w_in_t), delta)
    rates += mm(leave_t[...], gathered[0]) + mm(leave_t[...], gathered[1])
    values = arrive(base_ref, 3.0 * TIME_STEP, *received)
    between[...] = 0.5 * (adjoint_ref[...] + values) + HALF_STEP * rates
    totals[0] = totals[0] + mm3(delta, split(third_ref[...]), mm_nt)
    totals[2] = totals[2] + bias_rows(row_sums(delta), row_sums(split(values)))
    weight = 3.0 * TIME_STEP
    hidden_parts = split(hidden)
    early = [weight * mm3((h, l), hidden_parts, mm_nt) for h, l in zip(high_parts, low_parts)]
    upward, downward = sensitivities(edge_rows(between), link)

    values = arrive(between, 3.0 * HALF_STEP, below[16:32], above[16:32])
    parts = split(values)
    delta = split(through_closure(parts, hidden_second[...], pair(w_out_t)))
    values = values + TIME_STEP * back_rates(parts, delta, network, gather_back(parts, lift_t, near))
    collect(parts, delta, second_ref[...], hidden_second[...])

    states = take(parity, in_chip_state[...], cross_state[...])
    hiddens = take(parity, in_chip_hidden[...], cross_hidden[...])
    blocks = []
    for side, received in enumerate((weight * downward, weight * upward)):
        high, low = split(received)
        hidden = hiddens[side]
        seen = mm(eff[side], jnp.concatenate([high, low, high], axis=0))
        delta = split((1.0 - hidden * hidden) * seen)
        totals[0] = totals[0] + mm3(delta, split(states[side]), mm_nt)
        blocks.append(mm3((high, low), split(hidden), mm_nt))
        none = jnp.zeros((48, 256), F32)
        spread = [none, received, none, received] if side == 0 else [received, none, -received, none]
        totals[2] = totals[2] + bias_rows(row_sums(delta), row_sums(split(jnp.concatenate(spread, axis=0))))

    parts = split(values)
    delta = split(through_closure(parts, hidden_first[...], pair(w_out_t)))
    collect(parts, delta, state_ref[...], hidden_first[...])
    sum_ref[...] = totals[1]
    low, high = blocks[1] + early[0], blocks[0] + early[1]
    add_edges(sum_ref, low, high, -low, high)
    first, second, bias = totals[0], sum_ref[...], totals[2]
    rows = lax.broadcasted_iota(jnp.int32, (8, 128), 0)
    bias = jnp.where(rows == 4, loss_ref[...], bias)
    for ref, values in ((keep_ref, jnp.where(even, first, second)), (send_ref, jnp.where(even, second, first))):
        for n in range(16):
            ref[n, 0:16] = values[16 * n : 16 * n + 16, 0:128]
            ref[n, 16:32] = values[16 * n : 16 * n + 16, 128:256]
            ref[n, 32:40] = bias


def chip_kernel(keep_ref, got_ref, out_ref):
    out_ref[...] = keep_ref[...] + got_ref[...]


def plane_kernel(parts_ref, out_ref):
    total = jnp.sum(parts_ref[...], axis=0)
    for n in range(8):
        out_ref[n] = total


def line_kernel(parts_ref, out_ref, extra_ref):
    total = jnp.sum(parts_ref[...], axis=0)
    extra_ref[...] = total[32:40]
    for n in range(16):
        out_ref[n] = total[0:32]


def last_kernel(parity_ref, own_ref, other_ref, extra_ref, in_ref, b_in_ref, out_ref, b_out_ref, loss_ref):
    even = parity_ref[0] == 0
    own, other = own_ref[...], other_ref[...]
    first = jnp.where(even, own, other)
    second = jnp.where(even, other, own)
    bias = extra_ref[0:4]
    squares = jnp.sum(first * first + second * second, axis=0)
    total = jnp.sum(squares, keepdims=True) + jnp.sum(bias * bias, keepdims=True)
    scale = lax.rsqrt(total / PARAMS + TINY)
    for ref, values in ((in_ref, first * scale), (out_ref, second * scale)):
        for n in range(16):
            ref[16 * n : 16 * n + 16, 0:128] = values[n, 0:16]
            ref[16 * n : 16 * n + 16, 128:256] = values[n, 16:32]
    bias = bias * scale
    for row, ref in ((0, b_in_ref), (2, b_out_ref)):
        ref[:, 0:128] = bias[row : row + 1]
        ref[:, 128:256] = bias[row + 1 : row + 2]
    loss_ref[...] = jnp.sum(extra_ref[4:5], keepdims=True) * (0.5 / COUNT)


IN_CHIP = [(n, n ^ 1) for n in range(DEVICES)]
CROSS = [(n, (n - 1) % DEVICES if n % 2 == 0 else (n + 1) % DEVICES) for n in range(DEVICES)]


def exchange(in_chip, cross):
    return lax.ppermute(cross, AXES, CROSS), lax.ppermute(in_chip, AXES, IN_CHIP)


def local(state, target, w_in, b_in, w_out, b_out, nbr, send):
    parity = lax.axis_index("core").reshape(1)
    inner, leave, lift = operators()
    edge = np.concatenate([np.arange(0, 16), np.arange(48, 80), np.arange(112, 128)])
    fixed = np.zeros((768, 256))
    fixed[0:64], fixed[64:128] = (x[edge].astype(np.float64) for x in halves(inner))
    fixed[128:192], fixed[192:256, 0:64] = leave, lift[edge]
    to_bf16 = lambda values: jnp.asarray(values.astype(ml_dtypes.bfloat16))
    fixed, inner2, leave1, lift_t = (to_bf16(x) for x in (fixed, np.concatenate(halves(inner)), leave, lift.T))
    b_in, b_out = b_in.reshape(1, 256), b_out.reshape(1, 256)
    tall, flat, thin = ((512, 256), BF16), ((64, 256), BF16), ((256, 64), BF16)
    arrival = ((2, 64, 256), BF16)
    arrived, hidden_first, *edge, w_in2, state = call(
        first_kernel,
        [arrival, SQUARE, ((40, 256), F32), ((40, 256), F32), PAIR, SQUARE],
        parity, state, w_in, fixed, w_out, nbr, send, b_in,
        name="first", micros=1.5,
        far=range(1, 8),
        limit=53,
        scratch=[
            pltpu.VMEM((256, 256), F32), pltpu.VMEM((64, 256), F32), pltpu.VMEM((256, 256), BF16),
            pltpu.VMEM((4, 256, 256), BF16), pltpu.VMEM((6, 256), jnp.int32), pltpu.VMEM((2, 256), jnp.int32),
            pltpu.VMEM((1, 256), F32), pltpu.SemaphoreType.DMA((9,)),
        ],
    )
    got = exchange(*edge)
    middle = [SQUARE, SQUARE, ((64, 256), F32)]
    depth, shallow = ((256, 96), BF16), ((64, 96), BF16)
    made = call(
        tables_kernel,
        [SQUARE, *middle, PAIR, PAIR, PAIR, tall, thin, thin, ((4, 256, 256), BF16), PAIR]
        + [((256, 128), F32)] * 2
        + [depth, depth, shallow] * 2
        + [((2, 256, 48), BF16)],
        w_in2, w_out, inner2, leave1, lift_t, nbr, b_in, b_out, state, arrived, hidden_first, edge[0],
        name="tables", micros=1.5,
    )
    base, prepared, deeps, eff = made[0], made[1:4], made[14:20], made[20]
    w_out2, w_in_t, w_out_t, inner_t, leave_t, lift1, near, far, b_in2, b_out2 = made[4:14]
    forward_deeps, backward_deeps = deeps[:3], deeps[3:]
    network = (w_in2, b_in2, w_out2, b_out2, inner2, leave1, lift1, near)
    back = (w_in_t, inner_t, leave_t, lift_t)
    edge_shapes = [((32, 256), F32)] * 2
    square = pltpu.VMEM((256, 256), F32)
    second, third, hidden_second, hidden_third, arrived, link, *edge = call(
        middle_kernel,
        [SQUARE] * 4 + [arrival, PAIR] + edge_shapes,
        parity, base, state, *got, far, *prepared, *forward_deeps, *network, name="middle", micros=2.1, scratch=[square],
    )
    got = exchange(*edge)
    base, *prepared, copy = call(
        rest_kernel, [SQUARE, *middle, SQUARE], third, hidden_third, arrived, state, *network, name="rest", micros=0.9
    )
    beside = exchange(copy, copy)
    final, loss, fourth, hidden_fourth, adjoint, delta, gathered, *edge = call(
        turn_kernel,
        [SQUARE, EXTRA] + [SQUARE] * 4 + [arrival] + edge_shapes,
        parity, base, third, *got, link, target, *prepared, *forward_deeps, *network,
        w_in_t, w_out_t, inner_t, leave_t, lift_t,
        name="turn", micros=2.5, scratch=[square, pltpu.VMEM((2, 64, 256), BF16)],
    )
    got = exchange(*edge)
    base, *grads, back_product, linear, out = call(
        beside_kernel,
        [SQUARE, SQUARE, SQUARE, EXTRA, *middle],
        adjoint, delta, gathered, fourth, hidden_fourth, *back, near, w_out_t, hidden_third,
        name="beside", micros=1.4,
    )
    beside_hidden = call(hidden_kernel, [SQUARE] * 2, *beside, w_in2, b_in2, name="hidden", micros=0.6)
    (final,) = call(final_kernel, [SQUARE], final, name="final", micros=0.4)
    keep, give = call(
        back_kernel,
        [PACKED] * 2,
        parity, base, adjoint, *got, link, third, hidden_third, second, hidden_second, state, hidden_first,
        *beside, *beside_hidden, near, w_in_t, w_out_t, inner_t, leave_t, lift_t, eff,
        back_product, linear, out, *backward_deeps, *grads, loss,
        name="back", micros=4, scratch=[square] * 3,
    )
    swap = [(0, 1), (1, 0)]
    (parts,) = call(chip_kernel, [PACKED], keep, lax.ppermute(give, "core", swap), name="chip_sum", micros=0.3)
    parts = lax.all_to_all(parts, PLANE, 0, 0, tiled=True)
    (parts,) = call(plane_kernel, [((8, 40, 128), F32)], parts, name="plane_sum", micros=0.3)
    parts = lax.all_to_all(parts, "z", 0, 0, tiled=True)
    parts, extra = call(line_kernel, [((16, 32, 128), F32), EXTRA], parts, name="line_sum", micros=0.3)
    own = lax.all_to_all(parts, PLANE, 0, 0, tiled=True)
    other = lax.ppermute(own, "core", swap)
    row = ((1, 256), F32)
    step_in, step_b_in, step_out, step_b_out, loss = call(
        last_kernel, [SQUARE, row, SQUARE, row, ((1, 1), F32)], parity, own, other, extra, name="scale", micros=1
    )
    return final, loss.reshape(()), step_in, step_b_in.reshape(256), step_out, step_b_out.reshape(256)


def solution(mesh):
    split_mesh = Mesh(mesh.devices.reshape(SIZES), AXES)
    whole = P(None, AXES)
    return jax.shard_map(
        local,
        mesh=split_mesh,
        in_specs=(whole, whole, P(), P(), P(), P(), whole, whole),
        out_specs=(whole, P(), P(), P(), P(), P()),
        check_vma=False,
    )
```

```python
import jax
import jax.numpy as jnp
import ml_dtypes
import numpy as np
from jax import lax
from jax.experimental import pallas as pl
from jax.experimental.pallas import tpu as pltpu
from jax.sharding import Mesh, PartitionSpec as P

AXES = ("x", "y", "z", "core")
PLANE = ("x", "y")
SIZES = (4, 4, 8, 2)
DEVICES = 256
WIDTH = 256
COUNT = 16777216.0
PARAMS = 131584.0
TIME_STEP = 0.05
HALF_STEP = 0.025
TINY = 1e-20
F32 = jnp.float32
BF16 = jnp.bfloat16


def face_rows(face):
    layer = 0 if face % 2 == 0 else 3
    grid = np.arange(64).reshape(4, 4, 4)
    return np.take(grid, layer, axis=face // 2).reshape(16)


def operators():
    points = np.array([-1.0, -1.0 / np.sqrt(5.0), 1.0 / np.sqrt(5.0), 1.0])
    bary = np.array(
        [1.0 / np.prod([points[m] - points[n] for n in range(4) if n != m]) for m in range(4)]
    )
    deriv = np.zeros((4, 4))
    for m in range(4):
        for n in range(4):
            if m != n:
                deriv[m, n] = bary[n] / bary[m] / (points[m] - points[n])
        deriv[m, m] = -np.sum(deriv[m])
    eye = np.eye(4)
    tables = [
        np.kron(np.kron(deriv, eye), eye),
        np.kron(np.kron(eye, deriv), eye),
        np.kron(eye, np.kron(eye, deriv)),
    ]
    inner = np.zeros((256, 256))
    for a in range(3):
        inner[0:64, 64 * (a + 1) : 64 * (a + 2)] -= tables[a]
        inner[64 * (a + 1) : 64 * (a + 2), 0:64] -= tables[a]
    for face in range(6):
        sign = 2.0 * (face % 2) - 1.0
        for row in face_rows(face):
            speed = 64 * (face // 2 + 1) + row
            inner[row, row] -= 3.0
            inner[row, speed] += 3.0 * sign
            inner[speed, speed] -= 3.0
            inner[speed, row] += 3.0 * sign
    leave = np.zeros((64, 256))
    lift = np.zeros((256, 64))
    for face in range(2, 6):
        sign = 2.0 * (face % 2) - 1.0
        base = 16 * (face - 2)
        for n, row in enumerate(face_rows(face ^ 1)):
            leave[base + n, row] = 3.0
            leave[base + n, 64 * (face // 2 + 1) + row] = -3.0 * sign
        for n, row in enumerate(face_rows(face)):
            lift[row, base + n] = 1.0
            lift[64 * (face // 2 + 1) + row, base + n] = -sign
    return inner, leave, lift


def halves(values):
    high = values.astype(ml_dtypes.bfloat16)
    low = (values - high.astype(np.float64)).astype(ml_dtypes.bfloat16)
    return high, low


def split(values):
    high = values.astype(BF16)
    return high, (values - high.astype(F32)).astype(BF16)


def mm(left, right):
    return jnp.dot(left, right, preferred_element_type=F32)


def mm_nt(left, right):
    return lax.dot_general(left, right, (((1,), (1,)), ((), ())), preferred_element_type=F32)


def mm3(left, right, dot=mm):
    return dot(left[0], right[0]) + (dot(left[0], right[1]) + dot(left[1], right[0]))


def pair(ref):
    if len(ref.shape) == 2:
        return ref[0:256], ref[256:512]
    return ref[0], ref[1]


def call(body, outs, *args, name, micros, far=(), scratch=(), limit=24, reads=1000000):
    def space(n, value):
        if value.shape == (1,):
            return pltpu.SMEM
        return pltpu.HBM if n in far else pltpu.VMEM

    return list(pl.pallas_call(
        body,
        out_shape=[jax.ShapeDtypeStruct(s, t) for s, t in outs],
        in_specs=[pl.BlockSpec(memory_space=space(n, a)) for n, a in enumerate(args)],
        out_specs=[pl.BlockSpec(memory_space=pltpu.VMEM)] * len(outs),
        scratch_shapes=scratch,
        cost_estimate=pl.CostEstimate(flops=int(micros * 1.15e9), bytes_accessed=reads, transcendentals=0),
        compiler_params=pltpu.CompilerParams(vmem_limit_bytes=int(limit * 1048576)),
        name=name,
    )(*args))


SQUARE = ((256, 256), F32)
PAIR = ((2, 256, 256), BF16)
EXTRA = ((8, 128), F32)
PACKED = ((16, 40, 128), F32)


def edges(values):
    return values[0:16], values[48:64], values[64:80], values[112:128]


def edge_rows(values):
    return jnp.concatenate(edges(values), axis=0)


def leaving(edge):
    return 3.0 * (edge[16:32] + edge[48:64]), 3.0 * (edge[0:16] - edge[32:48])


def put(parity, upward, downward, in_chip_ref, cross_ref, rows=0):
    even = parity == 0
    in_chip_ref[rows : rows + 16] = jnp.where(even, upward, downward)
    cross_ref[rows : rows + 16] = jnp.where(even, downward, upward)


def take(parity, in_chip, cross):
    even = parity == 0
    return jnp.where(even, cross, in_chip), jnp.where(even, in_chip, cross)


def pick(values, table, dot=mm):
    both = dot(jnp.concatenate(split(values), axis=0), table)
    return both[0:16] + both[16:32]


def add_edges(values_ref, first, second, third, fourth):
    values_ref[0:16] += first
    values_ref[48:64] += second
    values_ref[64:80] += third
    values_ref[112:128] += fourth


def one_hot(rows, column):
    return (rows == column).astype(F32).astype(BF16)


def make_near(index_ref, near):
    rows = lax.broadcasted_iota(jnp.int32, (256, 256), 0)
    for face in range(2, 6):
        near[face - 2] = one_hot(rows, index_ref[face : face + 1] - 256 * (face ^ 1))


def load_kernel(
    state_far, w_in_far, fixed_far, w_out_far, total_ref, linear_ref, out_ref, w_out, lift, w_in, state_ref,
    w_in_ref, w_out_ref, fixed, sems,
):
    pairs = (
        (state_far, state_ref), (w_in_far, w_in_ref), (fixed_far.at[0:256], fixed), (w_out_far.at[0:16], w_out_ref.at[0:16]),
        (w_out_far.at[48:80], w_out_ref.at[16:48]), (w_out_far.at[112:128], w_out_ref.at[48:64]),
    )
    copies = [pltpu.make_async_copy(s, t, sems.at[n]) for n, (s, t) in enumerate(pairs)]
    for copy in copies:
        copy.start()
    copies[0].wait()
    parts = split(state_ref[...])
    copies[1].wait()
    w_in[0], w_in[1] = split(w_in_ref[...])
    total_ref[...] = mm3(pair(w_in), parts)
    for copy in copies[2:]:
        copy.wait()
    out_ref[...] = mm(fixed[128:192], parts[0]) + mm(fixed[128:192], parts[1])
    linear_ref[...] = mm3((fixed[0:64], fixed[64:128]), parts)
    w_out[0], w_out[1] = split(w_out_ref[...])
    lift[...] = fixed[192:256, 0:64]


def first_kernel(
    parity_ref, state_ref, total_ref, linear_ref, out_ref, w_out, lift, nbr_ref, send_ref, b_in,
    arrived_ref, hidden_ref, in_chip_ref, cross_ref, near,
):
    edge = edge_rows(state_ref)
    parity = parity_ref[0]
    put(parity, *leaving(edge), in_chip_ref, cross_ref)
    hidden = jnp.tanh(total_ref[...] + wide(b_in))
    hidden_ref[...] = hidden
    make_near(nbr_ref, near)
    arrive_near(out_ref[...], near, arrived_ref)
    rates = linear_ref[...] + mm3(pair(w_out), split(hidden))
    rates += mm(lift[...], arrived_ref[0]) + mm(lift[...], arrived_ref[1])
    put(parity, *leaving(edge + TIME_STEP * rates), in_chip_ref, cross_ref, 16)
    down_index = send_ref[0:1].astype(F32)
    up_index = (send_ref[1:2] - 256).astype(F32)
    even = parity == 0
    in_chip_ref[32:40] = jnp.broadcast_to(jnp.where(even, up_index, down_index), (8, 256))
    cross_ref[32:40] = jnp.broadcast_to(jnp.where(even, down_index, up_index), (8, 256))


def flip(values):
    return values.astype(F32).T.astype(BF16)


def forward_pairs(turned):
    return jnp.concatenate([turned[0:16] + turned[64:80], turned[48:64] - turned[112:128]], axis=0)


def backward_pairs(turned):
    return jnp.concatenate([turned[0:16] - turned[64:80], turned[48:64] + turned[112:128]], axis=0)


def deep(rows):
    high, low = split(rows.T)
    return jnp.concatenate([high, high, low], axis=1)


def tables_kernel(
    w_in, w_out_ref, inner, leave, lift_t, nbr_ref, b_in, b_out, state_ref, arrived_ref, hidden_ref, after_ref,
    next_ref, sum_ref, linear_ref, out_ref, w_out, in_t_ref, out_t_ref, inner_t, leave_t, lift,
    near, far_ref, column_in, column_out, in_deep, inner_deep, leave_deep, out_deep, inner_t_deep, lift_t_deep, eff_ref,
):
    column_in[...] = column(b_in)
    column_out[...] = column(b_out)
    second = w_out_ref[...]
    w_out[0], w_out[1] = split(second)
    lift[...] = flip(lift_t[...])
    leave_t[...] = flip(leave[...])
    values = state_ref[...]
    network = (w_in, column_in, w_out, column_out, inner, leave, lift, near)
    rates = full_rates(split(values), split(hidden_ref[...]), network, arrived_ref)
    base = values + TIME_STEP * rates
    next_ref[...] = base
    sum_ref[...], linear_ref[...], out_ref[...] = prepare(split(base), network)
    make_near(nbr_ref, near)
    rows = lax.broadcasted_iota(jnp.int32, (256, 256), 0)
    for face in range(2):
        far_ref[face] = one_hot(rows, nbr_ref[face : face + 1] - (1536 + 256 * face))
    for part in range(2):
        in_t_ref[part] = flip(w_in[part])
        out_t_ref[part] = flip(w_out[part])
        inner_t[256 * part : 256 * part + 256] = flip(inner[256 * part : 256 * part + 256])
    whole = lambda values: values[0].astype(F32) + values[1].astype(F32)
    in_deep[...] = deep(TIME_STEP * forward_pairs(whole(pair(in_t_ref))))
    inner_deep[...] = deep(TIME_STEP * forward_pairs(whole(pair(inner_t))))
    leave_deep[...] = deep(TIME_STEP * forward_pairs(leave_t[...].astype(F32)))
    weight = 3.0 * TIME_STEP
    out_deep[...] = deep(weight * backward_pairs(second))
    inner_t_deep[...] = deep(weight * backward_pairs(whole(pair(inner))))
    lift_t_deep[...] = deep(weight * backward_pairs(lift[...].astype(F32)))
    seen = backward_pairs(second)
    eff_ref[0] = deep(seen[16:32])
    eff_ref[1] = deep(seen[0:16])


def column(row):
    return jnp.broadcast_to(row[...], (128, 256)).T


def wide(bias):
    values = column(bias) if bias.shape[0] == 1 else bias[...]
    return jnp.concatenate([values, values], axis=1)


def gather(high, low, near, dot):
    for n in range(4):
        both = jnp.concatenate([high[16 * n : 16 * n + 16], low[16 * n : 16 * n + 16]], axis=0)
        yield dot(both, near[n])


def arrive_near(out, near, arrived_ref):
    high, low = split(out)
    for n, both in enumerate(gather(high, low, near, mm)):
        both = both.astype(BF16)
        arrived_ref[0, 16 * n : 16 * n + 16] = both[0:16]
        arrived_ref[1, 16 * n : 16 * n + 16] = both[16:32]


def prepare(parts, network):
    w_in, b_in, w_out, b_out, inner, leave, lift, near = network
    out = mm(leave[...], parts[0]) + mm(leave[...], parts[1])
    return mm3(pair(w_in), parts) + wide(b_in), mm3(pair(inner), parts) + wide(b_out), out


def full_rates(parts, hidden_parts, network, arrived_ref):
    w_in, b_in, w_out, b_out, inner, leave, lift, near = network
    rates = mm3(pair(inner), parts) + wide(b_out)
    rates += mm(lift[...], arrived_ref[0]) + mm(lift[...], arrived_ref[1])
    return rates + mm3(pair(w_out), hidden_parts)


def edge_rates(parts, hidden_parts, network, arrived_ref):
    w_in, b_in, w_out, b_out, inner, leave, lift, near = network
    rates = mm3([edge_rows(x) for x in pair(inner)], parts) + edge_rows(wide(b_out))
    rates += mm(edge_rows(lift), arrived_ref[0]) + mm(edge_rows(lift), arrived_ref[1])
    return rates + mm3([edge_rows(x) for x in pair(w_out)], hidden_parts)


def pick_parts(below, above, link):
    low = mm(jnp.concatenate(split(below), axis=0), link[0])
    high = mm(jnp.concatenate(split(above), axis=0), link[1])
    return low, high


def stack(low, high):
    top = jnp.concatenate([low[0:16], high[0:16]], axis=0).astype(BF16)
    rest = jnp.concatenate([low[16:32], high[16:32]], axis=0).astype(BF16)
    return jnp.concatenate([top, rest, top], axis=0)


def add_arrived(weight, base_ref, low, high, now_ref):
    low = weight * (low[0:16] + low[16:32])
    high = weight * (high[0:16] + high[16:32])
    now_ref[...] = base_ref[...]
    add_edges(now_ref, low, high, low, -high)
    return now_ref[...]


def prepared_rates(stacked, prepared, deeps, network, hidden_ref, arrived_ref):
    total, linear, out = (ref[...] + mm(d[...], stacked) for ref, d in zip(prepared, deeps))
    hidden = jnp.tanh(total)
    hidden_ref[...] = hidden
    lift, near, w_out = network[6], network[7], network[2]
    arrive_near(out, near, arrived_ref)
    linear += mm(lift[...], arrived_ref[0]) + mm(lift[...], arrived_ref[1])
    return linear + mm3(pair(w_out), split(hidden))


def middle_kernel(
    parity_ref, base_ref, state_ref, cross, in_chip, far_ref, sum_ref, linear_ref, out_ref, in_deep, inner_deep, leave_deep,
    w_in, b_in, w_out, b_out, inner, leave, lift, near,
    second_ref, third_ref, hidden_second, hidden_third, arrived_ref, link, in_chip_out, cross_out, between,
):
    network = (w_in, b_in, w_out, b_out, inner, leave, lift, near)
    parity = parity_ref[0]
    below, above = take(parity, in_chip[...], cross[...])
    rows = lax.broadcasted_iota(jnp.int32, (256, 256), 0).astype(F32)
    for side, received in enumerate((below, above)):
        link[side] = mm(one_hot(rows, received[32:33]), far_ref[side]).astype(BF16)
    low, high = pick_parts(below[0:16], above[0:16], link)
    rates = prepared_rates(
        stack(low, high), (sum_ref, linear_ref, out_ref), (in_deep, inner_deep, leave_deep),
        network, hidden_second, arrived_ref,
    )
    values = add_arrived(TIME_STEP, base_ref, low, high, second_ref)
    between[...] = 0.5 * (state_ref[...] + values) + HALF_STEP * rates
    put(parity, *leaving(edge_rows(between)), in_chip_out, cross_out)
    up_bias, down_bias = leaving(TIME_STEP * edge_rows(wide(b_out)))
    low, high = pick_parts(below[16:32] + up_bias, above[16:32] + down_bias, link)
    values = add_arrived(HALF_STEP, between, low, high, third_ref)
    parts = split(values)
    hidden = jnp.tanh(mm3(pair(w_in), parts) + wide(b_in))
    hidden_third[...] = hidden
    arrive_near(mm(leave[...], parts[0]) + mm(leave[...], parts[1]), near, arrived_ref)
    rates = edge_rates(parts, split(hidden), network, arrived_ref)
    put(parity, *leaving(edge_rows(values) + TIME_STEP * rates), in_chip_out, cross_out, 16)


def rest_kernel(
    third_ref, hidden_ref, arrived_ref, state_ref, w_in, b_in, w_out, b_out, inner, leave, lift, near,
    next_ref, sum_ref, linear_ref, out_ref, copy_ref,
):
    copy_ref[...] = state_ref[...]
    network = (w_in, b_in, w_out, b_out, inner, leave, lift, near)
    values = third_ref[...]
    base = values + TIME_STEP * full_rates(split(values), split(hidden_ref[...]), network, arrived_ref)
    next_ref[...] = base
    sum_ref[...], linear_ref[...], out_ref[...] = prepare(split(base), network)


def sensitivities(edge, link):
    upward = pick(edge[16:32] - edge[48:64], link[1], mm_nt)
    return upward, pick(edge[0:16] + edge[32:48], link[0], mm_nt)


def through_closure(parts, hidden, w_out_t):
    return (1.0 - hidden * hidden) * mm3(w_out_t, parts)


def gather_back(parts, lift_t, near):
    high, low = split(mm(lift_t[...], parts[0]) + mm(lift_t[...], parts[1]))
    return split(jnp.concatenate([a[0:16] + a[16:32] for a in gather(high, low, near, mm_nt)], axis=0))


def back_rates(parts, delta_parts, network, gathered, rows=lambda values: values[...]):
    w_in_t, inner_t, leave_t, lift_t, near = network
    rates = mm3([rows(x) for x in pair(inner_t)], parts) + mm3([rows(x) for x in pair(w_in_t)], delta_parts)
    return rates + (mm(rows(leave_t), gathered[0]) + mm(rows(leave_t), gathered[1]))


def turn_kernel(
    parity_ref, base_ref, third_ref, cross, in_chip, link, target_ref,
    sum_ref, linear_ref, out_ref, in_deep, inner_deep, leave_deep,
    w_in, b_in, w_out, b_out, inner, leave, lift, near, w_in_t, w_out_t, inner_t, leave_t, lift_t,
    final_ref, loss_ref, fourth_ref, hidden_ref, adjoint_ref, delta_ref, gathered_ref, in_chip_out, cross_out,
    between, arrived_ref,
):
    network = (w_in, b_in, w_out, b_out, inner, leave, lift, near)
    parity = parity_ref[0]
    below, above = take(parity, in_chip[...], cross[...])
    low, high = pick_parts(below[0:16], above[0:16], link)
    rates = prepared_rates(
        stack(low, high), (sum_ref, linear_ref, out_ref), (in_deep, inner_deep, leave_deep),
        network, hidden_ref, arrived_ref,
    )
    values = add_arrived(TIME_STEP, base_ref, low, high, fourth_ref)
    between[...] = 0.5 * (third_ref[...] + values) + HALF_STEP * rates
    low, high = pick_parts(below[16:32], above[16:32], link)
    final = add_arrived(HALF_STEP, between, low, high, final_ref)
    mismatch = final - target_ref[...]
    adjoint = (HALF_STEP / COUNT) * mismatch
    adjoint_ref[...] = adjoint
    squares = jnp.sum(mismatch * mismatch, axis=0, keepdims=True)
    loss_ref[...] = jnp.broadcast_to(squares[:, 0:128] + squares[:, 128:256], (8, 128))
    edge = edge_rows(adjoint)
    put(parity, *sensitivities(edge, link), in_chip_out, cross_out)
    parts = split(adjoint)
    delta = through_closure(parts, hidden_ref[...], pair(w_out_t))
    delta_ref[...] = delta
    gathered = gather_back(parts, lift_t, near)
    gathered_ref[0], gathered_ref[1] = gathered
    back = (w_in_t, inner_t, leave_t, lift_t, near)
    rates = back_rates(parts, split(delta), back, gathered, edge_rows)
    put(parity, *sensitivities(edge + TIME_STEP * rates, link), in_chip_out, cross_out, 16)


def bias_rows(first, second):
    rows = lax.broadcasted_iota(jnp.int32, (8, 128), 0)
    bias = jnp.where(rows == 0, first[:, 0:128], jnp.where(rows == 1, first[:, 128:256], 0.0))
    bias = jnp.where(rows == 2, second[:, 0:128], bias)
    if second.shape[1] == 256:
        bias = jnp.where(rows == 3, second[:, 128:256], bias)
    return bias


def row_sums(parts):
    ones = jnp.ones((8, 256), BF16)
    return mm_nt(ones, parts[0]) + mm_nt(ones, parts[1])


def gradients(parts, delta_parts, state, hidden):
    bias = bias_rows(row_sums(delta_parts), row_sums(parts))
    return mm3(delta_parts, split(state), mm_nt), mm3(parts, split(hidden), mm_nt), bias


def beside_kernel(
    adjoint_ref, delta_ref, gathered_ref, state_ref, hidden_ref,
    w_in_t, inner_t, leave_t, lift_t, near, w_out_t, hidden_third,
    next_ref, grad_in, grad_out, extra, back_ref, linear_ref, out_ref,
):
    adjoint = adjoint_ref[...]
    parts, delta_parts = split(adjoint), split(delta_ref[...])
    gathered = gathered_ref[0], gathered_ref[1]
    base = adjoint + TIME_STEP * back_rates(parts, delta_parts, (w_in_t, inner_t, leave_t, lift_t, near), gathered)
    next_ref[...] = base
    base_parts = split(base)
    back_ref[...] = mm3(pair(w_out_t), base_parts)
    linear_ref[...] = mm3(pair(inner_t), base_parts)
    out_ref[...] = mm(lift_t[...], base_parts[0]) + mm(lift_t[...], base_parts[1])
    first, second, bias = gradients(parts, delta_parts, state_ref[...], hidden_ref[...])
    grad_in[...] = first
    grad_out[...] = second + mm3(base_parts, split(hidden_third[...]), mm_nt)
    extra[...] = bias


def final_kernel(final_ref, out_ref):
    out_ref[...] = final_ref[...]


def hidden_kernel(cross, in_chip, w_in, b_in, cross_hidden, in_chip_hidden):
    for source, ref in ((cross, cross_hidden), (in_chip, in_chip_hidden)):
        ref[...] = jnp.tanh(mm3(pair(w_in), split(source[...])) + wide(b_in))


def back_kernel(
    parity_ref, base_ref, adjoint_ref, cross, in_chip, link,
    third_ref, hidden_third, second_ref, hidden_second, state_ref, hidden_first,
    cross_state, in_chip_state, cross_hidden, in_chip_hidden,
    near, w_in_t, w_out_t, inner_t, leave_t, lift_t, eff, back_ref, linear_ref, out_ref, out_deep, inner_t_deep, lift_t_deep,
    old_in, old_out, old_extra, loss_ref,
    keep_ref, send_ref, now_ref, between, sum_ref,
):
    network = (w_in_t, inner_t, leave_t, lift_t, near)
    parity = parity_ref[0]
    even = parity == 0
    below, above = take(parity, in_chip[...], cross[...])
    totals = [old_in[...], old_out[...], old_extra[...]]

    def arrive(source_ref, weight, low, high):
        now_ref[...] = source_ref[...]
        low, high = weight * low, weight * high
        add_edges(now_ref, low, high, -low, high)
        return now_ref[...]

    def collect(*args):
        for n, term in enumerate(gradients(*args)):
            totals[n] = totals[n] + term

    received = below[0:16], above[0:16]
    high_parts, low_parts = zip(*(split(x) for x in received))
    top, rest = jnp.concatenate(high_parts, axis=0), jnp.concatenate(low_parts, axis=0)
    stacked = jnp.concatenate([top, rest, top], axis=0)
    hidden = hidden_third[...]
    delta_full = (1.0 - hidden * hidden) * (back_ref[...] + mm(out_deep[...], stacked))
    delta = split(delta_full)
    high, low = split(out_ref[...] + mm(lift_t_deep[...], stacked))
    gathered = split(jnp.concatenate([a[0:16] + a[16:32] for a in gather(high, low, near, mm_nt)], axis=0))
    rates = linear_ref[...] + mm(inner_t_deep[...], stacked) + mm3(pair(w_in_t), delta)
    rates += mm(leave_t[...], gathered[0]) + mm(leave_t[...], gathered[1])
    values = arrive(base_ref, 3.0 * TIME_STEP, *received)
    between[...] = 0.5 * (adjoint_ref[...] + values) + HALF_STEP * rates
    totals[0] = totals[0] + mm3(delta, split(third_ref[...]), mm_nt)
    totals[2] = totals[2] + bias_rows(row_sums(delta), row_sums(split(values)))
    weight = 3.0 * TIME_STEP
    hidden_parts = split(hidden)
    early = [weight * mm3((h, l), hidden_parts, mm_nt) for h, l in zip(high_parts, low_parts)]
    upward, downward = sensitivities(edge_rows(between), link)

    values = arrive(between, 3.0 * HALF_STEP, below[16:32], above[16:32])
    parts = split(values)
    delta = split(through_closure(parts, hidden_second[...], pair(w_out_t)))
    values = values + TIME_STEP * back_rates(parts, delta, network, gather_back(parts, lift_t, near))
    collect(parts, delta, second_ref[...], hidden_second[...])

    states = take(parity, in_chip_state[...], cross_state[...])
    hiddens = take(parity, in_chip_hidden[...], cross_hidden[...])
    blocks = []
    for side, received in enumerate((weight * downward, weight * upward)):
        high, low = split(received)
        hidden = hiddens[side]
        seen = mm(eff[side], jnp.concatenate([high, low, high], axis=0))
        delta = split((1.0 - hidden * hidden) * seen)
        totals[0] = totals[0] + mm3(delta, split(states[side]), mm_nt)
        blocks.append(mm3((high, low), split(hidden), mm_nt))
        none = jnp.zeros((48, 256), F32)
        spread = [none, received, none, received] if side == 0 else [received, none, -received, none]
        totals[2] = totals[2] + bias_rows(row_sums(delta), row_sums(split(jnp.concatenate(spread, axis=0))))

    parts = split(values)
    delta = split(through_closure(parts, hidden_first[...], pair(w_out_t)))
    collect(parts, delta, state_ref[...], hidden_first[...])
    sum_ref[...] = totals[1]
    low, high = blocks[1] + early[0], blocks[0] + early[1]
    add_edges(sum_ref, low, high, -low, high)
    first, second, bias = totals[0], sum_ref[...], totals[2]
    rows = lax.broadcasted_iota(jnp.int32, (8, 128), 0)
    bias = jnp.where(rows == 4, loss_ref[...], bias)
    for ref, values in ((keep_ref, jnp.where(even, first, second)), (send_ref, jnp.where(even, second, first))):
        for n in range(16):
            ref[n, 0:16] = values[16 * n : 16 * n + 16, 0:128]
            ref[n, 16:32] = values[16 * n : 16 * n + 16, 128:256]
            ref[n, 32:40] = bias


def chip_kernel(keep_ref, got_ref, out_ref):
    out_ref[...] = keep_ref[...] + got_ref[...]


def plane_kernel(parts_ref, out_ref):
    total = jnp.sum(parts_ref[...], axis=0)
    for n in range(8):
        out_ref[n] = total


def line_kernel(parts_ref, out_ref, extra_ref):
    total = jnp.sum(parts_ref[...], axis=0)
    extra_ref[...] = total[32:40]
    for n in range(16):
        out_ref[n] = total[0:32]


def last_kernel(parity_ref, own_ref, other_ref, extra_ref, in_ref, b_in_ref, out_ref, b_out_ref, loss_ref):
    even = parity_ref[0] == 0
    own, other = own_ref[...], other_ref[...]
    first = jnp.where(even, own, other)
    second = jnp.where(even, other, own)
    bias = extra_ref[0:4]
    squares = jnp.sum(first * first + second * second, axis=0)
    total = jnp.sum(squares, keepdims=True) + jnp.sum(bias * bias, keepdims=True)
    scale = lax.rsqrt(total / PARAMS + TINY)
    for ref, values in ((in_ref, first * scale), (out_ref, second * scale)):
        for n in range(16):
            ref[16 * n : 16 * n + 16, 0:128] = values[n, 0:16]
            ref[16 * n : 16 * n + 16, 128:256] = values[n, 16:32]
    bias = bias * scale
    for row, ref in ((0, b_in_ref), (2, b_out_ref)):
        ref[:, 0:128] = bias[row : row + 1]
        ref[:, 128:256] = bias[row + 1 : row + 2]
    loss_ref[...] = jnp.sum(extra_ref[4:5], keepdims=True) * (0.5 / COUNT)


IN_CHIP = [(n, n ^ 1) for n in range(DEVICES)]
CROSS = [(n, (n - 1) % DEVICES if n % 2 == 0 else (n + 1) % DEVICES) for n in range(DEVICES)]


def exchange(in_chip, cross):
    return lax.ppermute(cross, AXES, CROSS), lax.ppermute(in_chip, AXES, IN_CHIP)


def local(state, target, w_in, b_in, w_out, b_out, nbr, send):
    parity = lax.axis_index("core").reshape(1)
    inner, leave, lift = operators()
    edge = np.concatenate([np.arange(0, 16), np.arange(48, 80), np.arange(112, 128)])
    fixed = np.zeros((768, 256))
    fixed[0:64], fixed[64:128] = (x[edge].astype(np.float64) for x in halves(inner))
    fixed[128:192], fixed[192:256, 0:64] = leave, lift[edge]
    to_bf16 = lambda values: jnp.asarray(values.astype(ml_dtypes.bfloat16))
    fixed, inner2, leave1, lift_t = (to_bf16(x) for x in (fixed, np.concatenate(halves(inner)), leave, lift.T))
    b_in, b_out = b_in.reshape(1, 256), b_out.reshape(1, 256)
    tall, flat, thin = ((512, 256), BF16), ((64, 256), BF16), ((256, 64), BF16)
    arrival = ((2, 64, 256), BF16)
    strip = ((64, 256), F32)
    *loaded, w_in2, state = call(
        load_kernel,
        [SQUARE, strip, strip, ((2, 64, 256), BF16), ((64, 64), BF16), PAIR, SQUARE],
        state, w_in, fixed, w_out,
        name="load", micros=1.3,
        far=range(4),
        limit=52.9,
        scratch=[
            pltpu.VMEM((256, 256), F32), pltpu.VMEM((64, 256), F32), pltpu.VMEM((256, 256), BF16),
            pltpu.SemaphoreType.DMA((6,)),
        ],
    )
    arrived, hidden_first, *edge = call(
        first_kernel,
        [arrival, SQUARE, ((40, 256), F32), ((40, 256), F32)],
        parity, state, *loaded, nbr, send, b_in,
        name="first", micros=0.8, scratch=[pltpu.VMEM((4, 256, 256), BF16)],
    )
    got = exchange(*edge)
    middle = [SQUARE, SQUARE, ((64, 256), F32)]
    depth, shallow = ((256, 96), BF16), ((64, 96), BF16)
    made = call(
        tables_kernel,
        [SQUARE, *middle, PAIR, PAIR, PAIR, tall, thin, thin, ((4, 256, 256), BF16), PAIR]
        + [((256, 128), F32)] * 2
        + [depth, depth, shallow] * 2
        + [((2, 256, 48), BF16)],
        w_in2, w_out, inner2, leave1, lift_t, nbr, b_in, b_out, state, arrived, hidden_first, edge[0],
        name="tables", micros=1.5,
    )
    base, prepared, deeps, eff = made[0], made[1:4], made[14:20], made[20]
    w_out2, w_in_t, w_out_t, inner_t, leave_t, lift1, near, far, b_in2, b_out2 = made[4:14]
    forward_deeps, backward_deeps = deeps[:3], deeps[3:]
    network = (w_in2, b_in2, w_out2, b_out2, inner2, leave1, lift1, near)
    back = (w_in_t, inner_t, leave_t, lift_t)
    edge_shapes = [((32, 256), F32)] * 2
    square = pltpu.VMEM((256, 256), F32)
    second, third, hidden_second, hidden_third, arrived, link, *edge = call(
        middle_kernel,
        [SQUARE] * 4 + [arrival, PAIR] + edge_shapes,
        parity, base, state, *got, far, *prepared, *forward_deeps, *network, name="middle", micros=2.1, scratch=[square],
    )
    got = exchange(*edge)
    base, *prepared, copy = call(
        rest_kernel, [SQUARE, *middle, SQUARE], third, hidden_third, arrived, state, *network, name="rest", micros=0.9
    )
    beside = exchange(copy, copy)
    final, loss, fourth, hidden_fourth, adjoint, delta, gathered, *edge = call(
        turn_kernel,
        [SQUARE, EXTRA] + [SQUARE] * 4 + [arrival] + edge_shapes,
        parity, base, third, *got, link, target, *prepared, *forward_deeps, *network,
        w_in_t, w_out_t, inner_t, leave_t, lift_t,
        name="turn", micros=2.5, scratch=[square, pltpu.VMEM((2, 64, 256), BF16)],
    )
    got = exchange(*edge)
    base, *grads, back_product, linear, out = call(
        beside_kernel,
        [SQUARE, SQUARE, SQUARE, EXTRA, *middle],
        adjoint, delta, gathered, fourth, hidden_fourth, *back, near, w_out_t, hidden_third,
        name="beside", micros=1.4,
    )
    beside_hidden = call(hidden_kernel, [SQUARE] * 2, *beside, w_in2, b_in2, name="hidden", micros=0.6)
    (final,) = call(final_kernel, [SQUARE], final, name="final", micros=0.4)
    keep, give = call(
        back_kernel,
        [PACKED] * 2,
        parity, base, adjoint, *got, link, third, hidden_third, second, hidden_second, state, hidden_first,
        *beside, *beside_hidden, near, w_in_t, w_out_t, inner_t, leave_t, lift_t, eff,
        back_product, linear, out, *backward_deeps, *grads, loss,
        name="back", micros=4, scratch=[square] * 3,
    )
    swap = [(0, 1), (1, 0)]
    (parts,) = call(chip_kernel, [PACKED], keep, lax.ppermute(give, "core", swap), name="chip_sum", micros=0.3)
    parts = lax.all_to_all(parts, PLANE, 0, 0, tiled=True)
    (parts,) = call(plane_kernel, [((8, 40, 128), F32)], parts, name="plane_sum", micros=0.3)
    parts = lax.all_to_all(parts, "z", 0, 0, tiled=True)
    parts, extra = call(line_kernel, [((16, 32, 128), F32), EXTRA], parts, name="line_sum", micros=0.3)
    own = lax.all_to_all(parts, PLANE, 0, 0, tiled=True)
    other = lax.ppermute(own, "core", swap)
    row = ((1, 256), F32)
    step_in, step_b_in, step_out, step_b_out, loss = call(
        last_kernel, [SQUARE, row, SQUARE, row, ((1, 1), F32)], parity, own, other, extra, name="scale", micros=1
    )
    return final, loss.reshape(()), step_in, step_b_in.reshape(256), step_out, step_b_out.reshape(256)


def solution(mesh):
    split_mesh = Mesh(mesh.devices.reshape(SIZES), AXES)
    whole = P(None, AXES)
    return jax.shard_map(
        local,
        mesh=split_mesh,
        in_specs=(whole, whole, P(), P(), P(), P(), whole, whole),
        out_specs=(whole, P(), P(), P(), P(), P()),
        check_vma=False,
    )
```
